32 devices in a mesh: groups: 2 (over y), dom: 4 (over z), sub: 2 (over x), rhs: 2 (over core).
Axes of the slice: x: 2, y: 2, z: 4, core: 2. Of those that a mesh axis runs over, the one named last changes fastest.
Arguments:
- traces: bfloat16 [2, 2, 30, 32, 4096], P(None, None, None, 'rhs', ('groups', 'dom', 'sub')), parts along dimension 4, may hold values from -6 to 6
- solver: bfloat16 [2, 2, 210, 120], P('groups'), parts along dimension 0, may hold values from -0.375 to 0.375
- mass: bfloat16 [1, 35, 35], replicated, as said below
- dom_lists: int32 [2, 256], P(None, ('dom', 'sub')), may hold values from 0 to 255
- sub_lists: int32 [2, 256], P(None, ('dom', 'sub')), may hold values from 0 to 255
- elem_face: int32 [4, 1024], P(None, ('dom', 'sub')), may hold values from 0 to 383, as said below
- volume: float32 [1024], P(('dom', 'sub')), may hold values from 0.3 to 3
- elem_owner: int32 [1024, 1], P(('dom', 'sub')), may hold values from 0 to 7; in each aligned block of 128 rows (0 to 127, 128 to 255, ...) at most 48 rows name the same one
- elem_slot: int32 [1024], P(('dom', 'sub')), may hold values from 0 to 127
Outputs:
- sensitivity: float32 [6, 32, 2048], P(None, 'rhs', ('groups', 'dom', 'sub')), parts along dimension 2
The draws below stay inside these ranges and needn't reach their ends.
There are 2 independent parts, one for each index of `groups`. The reference program is written for one: setup_inputs(seed, part) draws one part's arguments, and reference() takes and returns one part's arrays. A program takes and returns all parts, laid end to end along the dimension named above; an argument that names none is the same for every part. Nothing has to cross between parts.
Inputs may be any that keep to these rules, and one draw needn't show every extreme that they name: `elem_face`: entries below 256 name an owned face; 256 + b * 32 + r names entry r of block b of the extended table (b = 0 lower slab neighbour, 1 upper, 2 + t the partition of sub index t). Partitions of the first slab never name block 0, those of the last never block 1. `elem_owner`: among the elements of one partition at most 48 name the same owner. `mass`: symmetric in its last two dimensions.
All inputs are finite; a program needn't handle non-finite values.
Results may differ from the reference program's by a relative error of at most 0.0041.
Values may be sent and summed in bfloat16 or wider, within the bound.
No kernel may reach another device: no remote copies, remote signals or barrier semaphores. Data moves between devices by JAX's collectives and lax.ppermute only.
A program may use at most 64 MiB of HBM per device.

```python
import math
import jax
import jax.numpy as jnp
import numpy as np
from jax import lax

CLASSES = 1
CELLS_DEV = 128
RHS = 32
BASIS = 35
BND = 32
VOX_DEV = 128
SLABS = 4
PEERS = 2
OWNERS = 8
ELEM_DEV = 128
FACE_DEV = 256
FIELD = 210
TRACE = 30
ELEMS = 1024
FACES = 2048
BNDS = 256
VOX = 1024
CAP = 48
N_DOM = 4
N_SUB = 2


def draw_elem_face(key, part):
    key = jax.random.fold_in(key, 11)
    key_kind, key_own, key_block, key_row = jax.random.split(key, 4)
    dims_shape = (4, ELEMS)
    device = lax.broadcasted_iota(jnp.int32, dims_shape, 1) // ELEM_DEV
    slab_index = device // PEERS
    choose_kind = jax.random.randint(key_kind, dims_shape, 0, 5)
    own_face = jax.random.randint(key_own, dims_shape, 0, FACE_DEV)
    block_index = jax.random.randint(key_block, dims_shape, 0, 2 + PEERS)
    block_index = jnp.where((block_index == 0) & (slab_index == 0), 2, block_index)
    block_index = jnp.where((block_index == 1) & (slab_index == SLABS - 1), 2, block_index)
    row_index = jax.random.randint(key_row, dims_shape, 0, BND)
    remote = FACE_DEV + block_index * BND + row_index
    return jnp.where(choose_kind < 3, own_face, remote).astype(jnp.int32)


def draw_mass(key, part):
    key = jax.random.fold_in(key, 5)
    key_off, key_diag = jax.random.split(key, 2)
    off_diag = 0.12 * jax.random.normal(key_off, (CLASSES, BASIS, BASIS), jnp.float32)
    symmetric = 0.5 * (off_diag + jnp.swapaxes(off_diag, 1, 2))
    diagonal = jax.random.uniform(key_diag, (CLASSES, BASIS), jnp.float32, 0.6, 1.8)
    rows_iota = lax.broadcasted_iota(jnp.int32, (BASIS, BASIS), 0)
    cols_iota = lax.broadcasted_iota(jnp.int32, (BASIS, BASIS), 1)
    identity = (rows_iota == cols_iota).astype(jnp.float32)
    return (symmetric + identity[None] * diagonal[:, :, None]).astype(jnp.bfloat16)


def plant(values, rng, smallest, top_value):
    shape = values.shape
    index_at = [jax.random.randint(jax.random.fold_in(rng, axis), (), 0, shape[axis]) for axis in range(len(shape))]
    values = values.at[tuple(index_at)].set(smallest)
    longest = shape.index(max(shape))
    index_at[longest] = (index_at[longest] + 1) % shape[longest]
    return values.at[tuple(index_at)].set(top_value)


def level_of(own_key, shape, cuts, low, largest):
    factor_of = 1.0
    for axis_at, shards_of in cuts:
        heights = jax.random.uniform(jax.random.fold_in(jax.random.fold_in(own_key, 6), axis_at), (shards_of,), jnp.float32, low / len(cuts), largest / len(cuts))
        factor_of = factor_of * jnp.repeat(jnp.exp(heights), shape[axis_at] // shards_of).reshape((-1,) + (1,) * (len(shape) - 1 - axis_at))
    return factor_of


def deal_out(stream_key, own, number, rows, count, top, reach, skew):
    sequence = jax.random.permutation(stream_key, count)
    crowded, usual = load_shares(count, rows * top, reach, skew, True), load_shares(count, rows * top, reach, skew, False)
    places = jnp.arange(count)

    def named(lengths, offset_by):
        used = int((lengths > 0).sum())
        fixed = max(1, used // 4)
        passed = fixed + (places - fixed + offset_by * (used - fixed)) % max(1, count - fixed)
        return jnp.zeros((count,), jnp.int32).at[sequence[jnp.where(places < fixed, places, passed)]].set(jnp.asarray(lengths, jnp.int32))

    lengths = jnp.where(number % 4 == 0, named(crowded, number // 4), named(usual, number - number // 4 - 1))
    mixed = jax.random.permutation(jax.random.fold_in(own, 3), count)
    source_of, sink = mixed[0:count // 2 * 2:2], mixed[1:count // 2 * 2:2]
    slack = jnp.minimum(lengths[source_of] - 1, reach - lengths[sink]) // 2
    slack = jnp.where((source_of == sequence[0]) | (sink == sequence[0]) | (lengths[sink] == 0), 0, jnp.maximum(slack, 0))
    passed = jax.random.randint(jax.random.fold_in(own, 4), (count // 2,), 0, 1 << 20) % (slack + 1)
    lengths = lengths.at[source_of].add(-passed).at[sink].add(passed)
    members = jnp.searchsorted(jnp.cumsum(lengths), jnp.arange(rows * top), side="right").astype(jnp.int32)
    grid = members.reshape(top, rows).T
    grid = grid[jax.random.permutation(jax.random.fold_in(own, 1), rows)]
    offset_by = jax.random.randint(jax.random.fold_in(own, 2), (rows, 1), 0, top)
    return jnp.take_along_axis(grid, (jnp.arange(top)[None, :] + offset_by) % top, axis=1)


def load_shares(amount, total, bound, skew, full):
    portions = [(1 << 20) // math.isqrt(rank ** skew) + 1 for rank in range(1, amount + 1)]
    largest = bound if full else min(bound, max(-(-total // amount), total * portions[0] // sum(portions)))
    least = 1 if total - largest >= amount - 1 else 0
    holding, rest = [largest] + [least] * (amount - 1), total - largest - least * (amount - 1)
    while rest > 0:
        free = [i for i in range(1, amount) if holding[i] < largest] or [i for i in range(1, amount) if holding[i] < bound]
        pool, remaining = sum([portions[i] for i in free]), rest
        for i in free:
            more = min(bound - holding[i], max(1, remaining * portions[i] // pool), rest)
            holding[i] = holding[i] + more
            rest = rest - more
    return np.array(holding)


def centred(key, dims, spread, limit, cuts=(), kind=jnp.bfloat16):
    values = spread * jax.random.normal(key, dims, jnp.float32)
    if cuts:
        values = values * level_of(key, dims, cuts, -0.22, 0.18)
    return jnp.clip(values, -limit, limit).astype(kind)


def setup_inputs(seed: int = 0, part: int = 0) -> dict:
    key_list = jax.random.split(jax.random.key(seed), 10)
    own_keys = jax.random.split(jax.random.fold_in(key_list[9], part), 10)
    traces = centred(own_keys[0], (2, 2, TRACE, RHS, FACES), 1.0, 6.0, ((3, 2), (4, 8)))
    solver = centred(own_keys[1], (CLASSES, 2, FIELD, 4 * TRACE), (8 * TRACE) ** -0.5, 0.375)
    mass = draw_mass(jax.random.fold_in(key_list[9], 71), part)
    dom_lists = plant(jax.random.randint(key_list[3], (2, BNDS), 0, FACE_DEV), jax.random.fold_in(key_list[3], 1), 0, FACE_DEV - 1).astype(jnp.int32)
    sub_lists = plant(jax.random.randint(key_list[4], (PEERS, BNDS), 0, FACE_DEV), jax.random.fold_in(key_list[4], 1), 0, FACE_DEV - 1).astype(jnp.int32)
    elem_face = draw_elem_face(jax.random.fold_in(key_list[9], 71), part)
    volume = jnp.clip(jnp.exp(math.log(3.0) - 2.3025851 * jax.random.uniform(key_list[6], (ELEMS,), jnp.float32) ** level_of(key_list[6], (ELEMS,), ((0, 8),), -0.2, 0.2)), 0.3, 3.0)
    elem_owner_keys = jax.random.split(jax.random.fold_in(key_list[7], 1), ELEMS // ELEM_DEV)
    elem_owner_turns = jax.random.permutation(jax.random.fold_in(key_list[7], 3), ELEMS // ELEM_DEV)
    elem_owner = jax.vmap(lambda own, number: deal_out(jax.random.fold_in(key_list[7], 2), own, number, ELEM_DEV, OWNERS, 1, CAP, 2))(elem_owner_keys, elem_owner_turns).reshape((ELEMS, 1))
    elem_slot = plant(jax.random.randint(key_list[8], (ELEMS,), 0, VOX_DEV), jax.random.fold_in(key_list[8], 1), 0, VOX_DEV - 1).astype(jnp.int32)
    return dict(traces=traces, solver=solver, mass=mass, dom_lists=dom_lists, sub_lists=sub_lists, elem_face=elem_face, volume=volume, elem_owner=elem_owner, elem_slot=elem_slot)


def element_terms(extended, solver, mass, face_refs, volumes):
    pieces = []
    for class_index in range(CLASSES):
        start_cell = class_index * CELLS_DEV
        face_index = face_refs[:, start_cell:start_cell + CELLS_DEV]
        traces_block = jnp.take(extended, face_index, axis=4).astype(jnp.float32)
        matrix = solver[class_index].astype(jnp.float32).reshape(2, FIELD, 4, TRACE)
        stacked = jnp.stack([jnp.stack([matrix[0], -matrix[1]]), jnp.stack([matrix[1], matrix[0]])])
        fields = jnp.einsum('pqofn,aqncfe->poace', stacked, traces_block, precision=lax.Precision.HIGHEST).astype(jnp.bfloat16)
        electric = fields[:, :3 * BASIS].reshape(2, 3, BASIS, 2, fields.shape[3], CELLS_DEV)
        weighted = jnp.einsum('xb,pibce->pixce', mass[class_index].astype(jnp.float32), electric[:, :, :, 0].astype(jnp.float32), precision=lax.Precision.HIGHEST)
        sign_flip = jnp.array([1.0, -1.0], jnp.float32).reshape(2, 1, 1, 1, 1)
        tensor = jnp.einsum('pixce,pjxce->ijce', electric[:, :, :, 1].astype(jnp.float32), weighted * sign_flip, precision=lax.Precision.HIGHEST)
        symmetric = jnp.stack([tensor[0, 0], tensor[1, 1], tensor[2, 2], 0.5 * (tensor[0, 1] + tensor[1, 0]), 0.5 * (tensor[0, 2] + tensor[2, 0]), 0.5 * (tensor[1, 2] + tensor[2, 1])])
        norm_factor = 1.0 / math.sqrt(70.0 * ELEM_DEV / VOX_DEV)
        pieces.append(symmetric * (volumes[start_cell:start_cell + CELLS_DEV] * norm_factor))
    return jnp.concatenate(pieces, axis=2)

def reference(traces, solver, mass, dom_lists, sub_lists, elem_face, volume, elem_owner, elem_slot):
    owners_count = N_DOM * N_SUB
    by_device = traces.reshape(2, 2, TRACE, RHS, owners_count, FACE_DEV)
    slab_lists = dom_lists.reshape(2, owners_count, BND)
    peer_lists = sub_lists.reshape(N_SUB, owners_count, BND)
    face_table = elem_face.reshape(4, owners_count, ELEM_DEV)
    volume_table = volume.reshape(owners_count, ELEM_DEV)

    def owned(other):
        return lax.dynamic_index_in_dim(by_device, other, axis=4, keepdims=False)

    def device_terms(device):
        slab_index = device // N_SUB
        within = device % N_SUB
        below = jnp.maximum(device - N_SUB, 0).astype(jnp.int32)
        above = jnp.minimum(device + N_SUB, owners_count - 1).astype(jnp.int32)
        lower_block = jnp.take(owned(below), lax.dynamic_index_in_dim(slab_lists[1], below, 0, False), axis=4)
        lower_block = jnp.where(slab_index > 0, lower_block, jnp.zeros_like(lower_block))
        upper_block = jnp.take(owned(above), lax.dynamic_index_in_dim(slab_lists[0], above, 0, False), axis=4)
        upper_block = jnp.where(slab_index < N_DOM - 1, upper_block, jnp.zeros_like(upper_block))
        blocks = [owned(device), lower_block, upper_block]
        row_lists = lax.dynamic_index_in_dim(peer_lists, within, 0, False)
        for peer_index in range(N_SUB):
            source = (slab_index * N_SUB + peer_index).astype(jnp.int32)
            wanted = lax.dynamic_index_in_dim(row_lists, source, 0, False)
            blocks.append(jnp.take(owned(source), wanted, axis=4))
        extended = jnp.concatenate(blocks, axis=4)
        face_refs = lax.dynamic_index_in_dim(face_table, device, 1, False)
        volumes = lax.dynamic_index_in_dim(volume_table, device, 0, False)
        return element_terms(extended, solver, mass, face_refs, volumes)
    all_terms = lax.map(device_terms, jnp.arange(owners_count, dtype=jnp.int32))
    flat_terms = all_terms.transpose(0, 3, 1, 2).reshape(ELEMS, 6 * RHS)
    voxel_ids = (elem_owner[:, 0] * VOX_DEV + elem_slot).astype(jnp.int32)
    summed = jax.ops.segment_sum(flat_terms, voxel_ids, num_segments=VOX)
    return summed.T.reshape(6, RHS, VOX)
```

```python
import math

import jax
import jax.numpy as jnp
from jax import lax
from jax.experimental import pallas as pl
from jax.experimental.pallas import tpu as pltpu
from jax.sharding import PartitionSpec as P

BASIS = 35
HALF = 3 * BASIS
GROUP = 40
NODES = 30
BLOCK = 256
VMEM_LIMIT = 48 * 1024 * 1024

NT = (((1,), (1,)), ((), ()))
NN = (((1,), (0,)), ((), ()))
TN = (((0,), (0,)), ((), ()))


def dot(a, b, dims=NN):
    return lax.dot_general(a, b, dims, preferred_element_type=jnp.float32)


def iota(shape, axis):
    return lax.broadcasted_iota(jnp.int32, shape, axis)


def one_hot(condition):
    return jnp.where(condition, 1.0, 0.0).astype(jnp.bfloat16)


def pair_index(index, k, size):
    if size & (size - 1) == 0:
        return index ^ k, index ^ k
    return lax.rem(index + k, size), lax.rem(index + size - k, size)


def pack_kernel(n_sub, rows, dom_ref, sub_ref, traces_ref, *out_refs):
    faces = traces_ref.shape[1]
    parity = lax.rem(lax.axis_index("dom"), 2)
    within = lax.axis_index("sub")
    lists = [dom_ref[pl.ds(1 - parity, 1), :], dom_ref[pl.ds(parity, 1), :]]
    for k in range(1, n_sub):
        lists.append(sub_ref[pl.ds(pair_index(within, k, n_sub)[0], 1), :])
    face = iota((faces, rows), 0)
    picks = [jnp.where(face == row, 1.0, 0.0).T for row in lists]
    picks = jnp.concatenate(picks, axis=0).astype(jnp.bfloat16)
    packed = dot(picks, traces_ref[...], NT).astype(jnp.bfloat16)
    for k, out_ref in enumerate(out_refs):
        out_ref[...] = packed[k * rows : (k + 1) * rows]


def element_kernel(
    n_sub,
    capacity,
    columns,
    sub_ref,
    traces_ref,
    solver_ref,
    mass_ref,
    elem_ref,
    volume_ref,
    owner_ref,
    slot_ref,
    *refs,
):
    halo_refs = refs[: n_sub + 1]
    out_ref, gathered_ref, sums_ref = refs[n_sub + 1 :]
    faces = traces_ref.shape[1]
    elems = elem_ref.shape[1]
    rows = sub_ref.shape[1]
    slots = out_ref.shape[0]
    parity = lax.rem(lax.axis_index("dom"), 2)
    within = lax.axis_index("sub")
    face_rows = [elem_ref[f : f + 1, :] for f in range(4)]

    def picks(size, start):
        return jnp.concatenate(
            [jnp.where(iota((size, elems), 0) + start == row, 1.0, 0.0) for row in face_rows],
            axis=1,
        )

    own_list = sub_ref[pl.ds(within, 1), :]
    own_list = one_hot(iota((faces, rows), 0) == own_list)
    own_block = picks(rows, faces + (2 + within) * rows).astype(jnp.bfloat16)
    own = (picks(faces, 0) + dot(own_list, own_block)).astype(jnp.bfloat16)
    blocks = [1 - parity, parity]
    for k in range(1, n_sub):
        blocks.append(2 + pair_index(within, k, n_sub)[1])
    halo = [picks(rows, faces + block * rows).astype(jnp.bfloat16) for block in blocks]
    table = jnp.concatenate([own] + halo, axis=0)

    per_block = BLOCK // columns
    row = iota((BLOCK, BLOCK), 0)
    col = iota((BLOCK, BLOCK), 1)
    reorder = one_hot(
        lax.rem(row, per_block) * columns + lax.div(row, per_block) == col
    )
    half = 2 * NODES * columns
    starts = []
    for a in range(2):
        first = a * half - (a * half) % 128
        starts += [first + b * BLOCK for b in range(4)]
    halo_rows = jnp.concatenate([ref[...] for ref in halo_refs], axis=0)
    for b, start in enumerate(starts):
        mine = dot(reorder, traces_ref[start : start + BLOCK, :])
        others = dot(reorder, halo_rows[:, start : start + BLOCK], NT)
        both = jnp.concatenate([mine, others], axis=1).astype(jnp.bfloat16)
        got = dot(both, table).astype(jnp.bfloat16)
        gathered_ref[b] = got.reshape(columns, per_block, 4 * elems)

    place = iota((3 * GROUP, HALF), 0)
    source = iota((3 * GROUP, HALF), 1)
    spread = one_hot(
        (lax.div(place, GROUP) == lax.div(source, BASIS))
        & (lax.rem(place, GROUP) == lax.rem(source, BASIS))
    )
    real = dot(spread, solver_ref[0, :HALF, :]).astype(jnp.bfloat16)
    imag = dot(spread, solver_ref[1, :HALF, :]).astype(jnp.bfloat16)
    matrices = []
    for a in range(2):
        shift = ((a * half) % 128) // columns
        source = iota((4 * NODES, BLOCK), 0)
        place = iota((4 * NODES, BLOCK), 1)
        target = lax.div(source, NODES) * 64 + lax.rem(source, NODES) + shift
        for_real = one_hot(target == place)
        for_imag = one_hot(target + NODES == place)
        top = dot(real, for_real) - dot(imag, for_imag)
        bottom = dot(imag, for_real) + dot(real, for_imag)
        matrices.append(jnp.concatenate([top, bottom], axis=0).astype(jnp.bfloat16))

    size = 6 * GROUP
    spread = one_hot(lax.rem(iota((size, BASIS), 0), GROUP) == iota((size, BASIS), 1))
    tiles = dot(dot(spread, mass_ref[0]).astype(jnp.bfloat16), spread, NT)
    row = iota((size, size), 0)
    col = iota((size, size), 1)
    tiles = jnp.where(lax.div(row, GROUP) == lax.div(col, GROUP), tiles, 0.0)
    masses = jnp.where(row < 3 * GROUP, tiles, -tiles).astype(jnp.bfloat16)

    pairs = [(0, 0), (1, 1), (2, 2), (0, 1), (0, 2), (1, 2)]

    def step(index, carry):
        fields = []
        for a in range(2):
            parts = []
            for c in range(2):
                taken = [gathered_ref[a * 4 + b, 2 * index + c] for b in range(4)]
                parts.append(
                    jnp.concatenate(
                        [
                            taken[b][:, f * elems : (f + 1) * elems]
                            for f in range(4)
                            for b in range(4)
                        ],
                        axis=0,
                    )
                )
            values = dot(matrices[a], jnp.concatenate(parts, axis=1))
            fields.append(values.astype(jnp.bfloat16))
        weighted = dot(masses, fields[0])
        shape = (2, 3, GROUP // 8, 8, 2 * elems)
        adjoint = fields[1].astype(jnp.float32).reshape(shape)
        weighted = weighted.reshape(shape)
        for m, (i, j) in enumerate(pairs):
            products = adjoint[:, i] * weighted[:, j]
            if i != j:
                products = products + adjoint[:, j] * weighted[:, i]
            total = jnp.sum(products, axis=(0, 1))
            for c in range(2):
                start = pl.multiple_of((m * columns + 2 * index + c) * 8, 8)
                sums_ref[pl.ds(start, 8), :] = total[:, c * elems : (c + 1) * elems]
        return carry

    lax.fori_loop(0, columns // 2, step, 0)

    width = 6 * columns
    total = sums_ref[pl.ds(0, width, stride=8), :]
    for k in range(1, 8):
        total = total + sums_ref[pl.ds(k, width, stride=8), :]
    norm = 1.0 / math.sqrt(70.0)
    factor = jnp.where(iota((width, 1), 0) < 3 * columns, norm, 0.5 * norm)
    terms = total * (factor * volume_ref[...])

    owner = owner_ref[...]
    owners = iota((max(8, slots // capacity), elems), 0) == owner
    earlier = one_hot(iota((elems, elems), 0) < iota((elems, elems), 1))
    counts = dot(one_hot(owners), earlier)
    rank = jnp.sum(jnp.where(owners, counts, 0.0), axis=0, keepdims=True)
    target = owner * capacity + rank.astype(jnp.int32)
    sends = one_hot(iota((slots, elems), 0) == target)
    slot = jnp.broadcast_to(slot_ref[...].astype(jnp.float32), (128 - width, elems))
    payload = jnp.concatenate([terms, slot], axis=0).astype(jnp.bfloat16)
    out_ref[...] = dot(sends, payload, NT).astype(jnp.bfloat16)


def voxel_kernel(width, got_ref, out_ref):
    got = got_ref[...]
    slot = got[:, width : width + 1].astype(jnp.int32)
    voxels = out_ref.shape[1]
    members = one_hot(slot == iota((got.shape[0], voxels), 1))
    out_ref[...] = dot(got, members, TN)[:width]


def per_device(
    traces, solver, mass, dom_lists, sub_lists, elem_face, volume, elem_owner, elem_slot
):
    n_dom, n_sub = lax.axis_size("dom"), lax.axis_size("sub")
    owners = n_dom * n_sub
    columns, faces = traces.shape[3:]
    rows = dom_lists.shape[1]
    elems = elem_face.shape[1]
    capacity = max(2, 3 * elems // owners)
    width = 6 * columns
    table = traces.reshape(-1, faces)
    values = table.shape[0]
    params = pltpu.CompilerParams(vmem_limit_bytes=VMEM_LIMIT)

    packed = pl.pallas_call(
        lambda *refs: pack_kernel(n_sub, rows, *refs),
        out_shape=[jax.ShapeDtypeStruct((rows, values), jnp.bfloat16)] * (n_sub + 1),
        compiler_params=params,
        name="pack",
    )(dom_lists, sub_lists, table)

    even = [(i, i + 1) for i in range(0, n_dom - 1, 2)]
    odd = [(i, i + 1) for i in range(1, n_dom - 1, 2)]
    halos = [
        lax.ppermute(part, "dom", pairs + [(j, i) for i, j in pairs])
        for part, pairs in zip(packed, (even, odd))
    ]
    for k in range(1, n_sub):
        pairs = [(i, pair_index(i, k, n_sub)[0]) for i in range(n_sub)]
        halos.append(lax.ppermute(packed[1 + k], "sub", [(i, int(j)) for i, j in pairs]))

    sent = pl.pallas_call(
        lambda *refs: element_kernel(n_sub, capacity, columns, *refs),
        out_shape=jax.ShapeDtypeStruct((owners * capacity, 128), jnp.bfloat16),
        scratch_shapes=[
            pltpu.VMEM((8, columns, BLOCK // columns, 4 * elems), jnp.bfloat16),
            pltpu.VMEM((8 * width, elems), jnp.float32),
        ],
        compiler_params=params,
        name="elements",
    )(
        sub_lists,
        table,
        solver[0],
        mass,
        elem_face,
        volume.reshape(1, elems),
        elem_owner.reshape(1, elems),
        elem_slot.reshape(1, elems),
        *halos,
    )
    got = lax.all_to_all(sent, ("dom", "sub"), split_axis=0, concat_axis=0, tiled=True)
    summed = pl.pallas_call(
        lambda *refs: voxel_kernel(width, *refs),
        out_shape=jax.ShapeDtypeStruct((width, elems), jnp.float32),
        compiler_params=params,
        name="voxels",
    )(got)
    return summed.reshape(6, columns, elems)


def solution(mesh):
    return jax.shard_map(
        per_device,
        mesh=mesh,
        in_specs=(
            P(None, None, None, "rhs", ("groups", "dom", "sub")),
            P("groups", None, None, None),
            P(),
            P(None, ("dom", "sub")),
            P(None, ("dom", "sub")),
            P(None, ("dom", "sub")),
            P(("dom", "sub")),
            P(("dom", "sub"), None),
            P(("dom", "sub")),
        ),
        out_specs=P(None, "rhs", ("groups", "dom", "sub")),
        check_vma=False,
    )
```

```python
import math

import jax
import jax.numpy as jnp
from jax import lax
from jax.experimental import pallas as pl
from jax.experimental.pallas import tpu as pltpu
from jax.sharding import PartitionSpec as P

BASIS = 35
HALF = 3 * BASIS
GROUP = 40
NODES = 30
BLOCK = 256
N_INPUTS = 9
CHUNKS = 5
UNROLL = 1
VMEM_LIMIT = 24 * 1024 * 1024

NT = (((1,), (1,)), ((), ()))
NN = (((1,), (0,)), ((), ()))
TN = (((0,), (0,)), ((), ()))


def dot(a, b, dims=NN):
    return lax.dot_general(a, b, dims, preferred_element_type=jnp.float32)


def iota(shape, axis):
    return lax.broadcasted_iota(jnp.int32, shape, axis)


def one_hot(condition):
    return jnp.where(condition, 1.0, 0.0).astype(jnp.bfloat16)


def pair_index(index, k, size):
    if size & (size - 1) == 0:
        return index ^ k, index ^ k
    return lax.rem(index + k, size), lax.rem(index + size - k, size)


def pack_kernel(n_sub, rows, *refs):
    hbm_refs, refs = refs[:N_INPUTS], refs[N_INPUTS:]
    vmem_refs, refs = refs[:N_INPUTS], refs[N_INPUTS:]
    out_refs, (sems, chunk_sems) = refs[: n_sub + 1], refs[n_sub + 1 :]
    copies = [
        pltpu.make_async_copy(hbm_refs[i], vmem_refs[i], sems.at[i]) for i in range(1, N_INPUTS)
    ]
    for copy in copies[:2]:
        copy.start()
    table_ref, dom_ref, sub_ref = vmem_refs[:3]
    values, faces = table_ref.shape
    step = values // CHUNKS
    chunks = []
    for k in range(CHUNKS):
        part = pl.ds(k * step, step)
        chunks.append(
            pltpu.make_async_copy(hbm_refs[0].at[part, :], table_ref.at[part, :], chunk_sems.at[k])
        )
        chunks[k].start()
    for copy in copies[2:]:
        copy.start()
    for copy in copies[:2]:
        copy.wait()
    parity = lax.rem(lax.axis_index("dom"), 2)
    within = lax.axis_index("sub")
    lists = [dom_ref[pl.ds(1 - parity, 1), :], dom_ref[pl.ds(parity, 1), :]]
    for k in range(1, n_sub):
        lists.append(sub_ref[pl.ds(pair_index(within, k, n_sub)[0], 1), :])
    face = iota((faces, rows), 0)
    picks = [jnp.where(face == row, 1.0, 0.0).T for row in lists]
    picks = jnp.concatenate(picks, axis=0).astype(jnp.bfloat16)
    for k in range(CHUNKS):
        chunks[k].wait()
        part = slice(k * step, (k + 1) * step)
        packed = dot(picks, table_ref[part, :], NT).astype(jnp.bfloat16)
        for i, out_ref in enumerate(out_refs):
            out_ref[:, part] = packed[i * rows : (i + 1) * rows]
    for copy in copies[2:]:
        copy.wait()


def reorder_matrix(columns):
    per_block = BLOCK // columns
    row = iota((BLOCK, BLOCK), 0)
    col = iota((BLOCK, BLOCK), 1)
    return one_hot(lax.rem(row, per_block) * columns + lax.div(row, per_block) == col)


def block_starts(columns):
    half = 2 * NODES * columns
    return [a * half - (a * half) % 128 + b * BLOCK for a in range(2) for b in range(4)]


def prepare_kernel(
    n_sub,
    capacity,
    columns,
    sub_ref,
    table_ref,
    solver_ref,
    mass_ref,
    elem_ref,
    owner_ref,
    own_ref,
    halo_ref,
    matrix_ref,
    masses_ref,
    sends_ref,
):
    faces = table_ref.shape[1]
    elems = elem_ref.shape[1]
    rows = sub_ref.shape[1]
    slots = sends_ref.shape[0]
    parity = lax.rem(lax.axis_index("dom"), 2)
    within = lax.axis_index("sub")
    face_rows = [elem_ref[f : f + 1, :] for f in range(4)]

    def picks(size, start):
        return jnp.concatenate(
            [jnp.where(iota((size, elems), 0) + start == row, 1.0, 0.0) for row in face_rows],
            axis=1,
        )

    own_list = sub_ref[pl.ds(within, 1), :]
    own_list = one_hot(iota((faces, rows), 0) == own_list)
    own_block = picks(rows, faces + (2 + within) * rows).astype(jnp.bfloat16)
    own = (picks(faces, 0) + dot(own_list, own_block)).astype(jnp.bfloat16)
    blocks = [1 - parity, parity]
    for k in range(1, n_sub):
        blocks.append(2 + pair_index(within, k, n_sub)[1])
    for i, block in enumerate(blocks):
        halo_ref[i * rows : (i + 1) * rows, :] = picks(rows, faces + block * rows).astype(
            jnp.bfloat16
        )

    reorder = reorder_matrix(columns)
    for b, start in enumerate(block_starts(columns)):
        mine = dot(reorder, table_ref[start : start + BLOCK, :]).astype(jnp.bfloat16)
        own_ref[b] = dot(mine, own).astype(jnp.bfloat16)

    place = iota((3 * GROUP, HALF), 0)
    source = iota((3 * GROUP, HALF), 1)
    spread = one_hot(
        (lax.div(place, GROUP) == lax.div(source, BASIS))
        & (lax.rem(place, GROUP) == lax.rem(source, BASIS))
    )
    solver = solver_ref[:HALF].astype(jnp.float32)
    real = dot(spread, solver[:, 0, :].astype(jnp.bfloat16)).astype(jnp.bfloat16)
    imag = dot(spread, solver[:, 1, :].astype(jnp.bfloat16)).astype(jnp.bfloat16)
    half = 2 * NODES * columns
    for a in range(2):
        shift = ((a * half) % 128) // columns
        source = iota((4 * NODES, BLOCK), 0)
        place = iota((4 * NODES, BLOCK), 1)
        target = lax.div(source, NODES) * 64 + lax.rem(source, NODES) + shift
        for_real = one_hot(target == place)
        for_imag = one_hot(target + NODES == place)
        top = dot(real, for_real) - dot(imag, for_imag)
        bottom = dot(imag, for_real) + dot(real, for_imag)
        matrix_ref[a] = jnp.concatenate([top, bottom], axis=0).astype(jnp.bfloat16)

    size = 6 * GROUP
    spread = one_hot(lax.rem(iota((size, BASIS), 0), GROUP) == iota((size, BASIS), 1))
    tiles = dot(dot(spread, mass_ref[...]).astype(jnp.bfloat16), spread, NT)
    row = iota((size, size), 0)
    col = iota((size, size), 1)
    tiles = jnp.where(lax.div(row, GROUP) == lax.div(col, GROUP), tiles, 0.0)
    masses_ref[...] = jnp.where(row < 3 * GROUP, tiles, -tiles).astype(jnp.bfloat16)

    owner = owner_ref[...]
    owners = iota((max(8, slots // capacity), elems), 0) == owner
    earlier = one_hot(iota((elems, elems), 0) < iota((elems, elems), 1))
    counts = dot(one_hot(owners), earlier)
    rank = jnp.sum(jnp.where(owners, counts, 0.0), axis=0, keepdims=True)
    target = owner * capacity + rank.astype(jnp.int32)
    sends_ref[...] = one_hot(iota((slots, elems), 0) == target)


def element_kernel(
    columns,
    volume_ref,
    slot_ref,
    own_ref,
    halo_ref,
    matrix_ref,
    masses_ref,
    sends_ref,
    *refs,
):
    halo_refs = refs[:-3]
    out_ref, gathered_ref, sums_ref = refs[-3:]
    elems = volume_ref.shape[1]
    per_block = BLOCK // columns
    reorder = reorder_matrix(columns)
    halo_rows = jnp.concatenate([ref[...] for ref in halo_refs], axis=0)
    for b, start in enumerate(block_starts(columns)):
        others = dot(reorder, halo_rows[:, start : start + BLOCK], NT).astype(jnp.bfloat16)
        got = own_ref[b] + dot(others, halo_ref[...]).astype(jnp.bfloat16)
        gathered_ref[b] = got.reshape(columns, per_block, 4 * elems)

    masses = masses_ref[...]
    pairs = [(0, 0), (1, 1), (2, 2), (0, 1), (0, 2), (1, 2)]

    def step(index, carry):
        fields = []
        for a in range(2):
            parts = []
            for c in range(2):
                taken = [gathered_ref[a * 4 + b, 2 * index + c] for b in range(4)]
                parts.append(
                    jnp.concatenate(
                        [
                            taken[b][:, f * elems : (f + 1) * elems]
                            for f in range(4)
                            for b in range(4)
                        ],
                        axis=0,
                    )
                )
            values = dot(matrix_ref[a], jnp.concatenate(parts, axis=1))
            fields.append(values.astype(jnp.bfloat16))
        weighted = dot(masses, fields[0])
        shape = (2, 3, GROUP // 8, 8, 2 * elems)
        adjoint = fields[1].astype(jnp.float32).reshape(shape)
        weighted = weighted.reshape(shape)
        for m, (i, j) in enumerate(pairs):
            products = adjoint[:, i] * weighted[:, j]
            if i != j:
                products = products + adjoint[:, j] * weighted[:, i]
            total = jnp.sum(products, axis=(0, 1))
            for c in range(2):
                start = pl.multiple_of((m * columns + 2 * index + c) * 8, 8)
                sums_ref[pl.ds(start, 8), :] = total[:, c * elems : (c + 1) * elems]
        return carry

    lax.fori_loop(0, columns // 2, step, 0, unroll=UNROLL)

    width = 6 * columns
    total = sums_ref[pl.ds(0, width, stride=8), :]
    for k in range(1, 8):
        total = total + sums_ref[pl.ds(k, width, stride=8), :]
    norm = 1.0 / math.sqrt(70.0)
    factor = jnp.where(iota((width, 1), 0) < 3 * columns, norm, 0.5 * norm)
    terms = total * (factor * volume_ref[...])
    slot = jnp.broadcast_to(slot_ref[...].astype(jnp.float32), (128 - width, elems))
    payload = jnp.concatenate([terms, slot], axis=0).astype(jnp.bfloat16)
    out_ref[...] = dot(sends_ref[...], payload, NT).astype(jnp.bfloat16)


def voxel_kernel(width, got_ref, out_ref):
    got = got_ref[...]
    slot = got[:, width : width + 1].astype(jnp.int32)
    voxels = out_ref.shape[1]
    members = one_hot(slot == iota((got.shape[0], voxels), 1))
    out_ref[...] = dot(got, members, TN)[:width]


def per_device(
    traces, solver, mass, dom_lists, sub_lists, elem_face, volume, elem_owner, elem_slot
):
    n_dom, n_sub = lax.axis_size("dom"), lax.axis_size("sub")
    owners = n_dom * n_sub
    columns, faces = traces.shape[3:]
    rows = dom_lists.shape[1]
    elems = elem_face.shape[1]
    capacity = max(2, 3 * elems // owners)
    width = 6 * columns
    table = traces.reshape(-1, faces)
    values = table.shape[0]
    params = pltpu.CompilerParams(vmem_limit_bytes=VMEM_LIMIT)

    inputs = [
        table,
        dom_lists,
        sub_lists,
        solver[0].transpose(1, 0, 2),
        mass[0],
        elem_face,
        volume.reshape(1, elems),
        elem_owner.reshape(1, elems),
        elem_slot.reshape(1, elems),
    ]
    inputs = [pltpu.with_memory_space_constraint(x, pltpu.HBM) for x in inputs]
    outs = pl.pallas_call(
        lambda *refs: pack_kernel(n_sub, rows, *refs),
        in_specs=[pl.BlockSpec(memory_space=pltpu.HBM)] * N_INPUTS,
        out_shape=[pltpu.VMEM(x.shape, x.dtype) for x in inputs]
        + [pltpu.VMEM((rows, values), jnp.bfloat16)] * (n_sub + 1),
        out_specs=[pl.BlockSpec(memory_space=pltpu.VMEM)] * (N_INPUTS + n_sub + 1),
        scratch_shapes=[
            pltpu.SemaphoreType.DMA((N_INPUTS,)),
            pltpu.SemaphoreType.DMA((CHUNKS,)),
        ],
        compiler_params=params,
        name="pack",
    )(*inputs)
    table, _, sub, matrix, mass, elem_face, volume, owner, slot = outs[:N_INPUTS]
    packed = outs[N_INPUTS:]

    even = [(i, i + 1) for i in range(0, n_dom - 1, 2)]
    odd = [(i, i + 1) for i in range(1, n_dom - 1, 2)]
    halos = [
        lax.ppermute(part, "dom", pairs + [(j, i) for i, j in pairs])
        for part, pairs in zip(packed, (even, odd))
    ]
    for k in range(1, n_sub):
        pairs = [(i, pair_index(i, k, n_sub)[0]) for i in range(n_sub)]
        halos.append(lax.ppermute(packed[1 + k], "sub", [(i, int(j)) for i, j in pairs]))

    slots = owners * capacity
    fixed = pl.pallas_call(
        lambda *refs: prepare_kernel(n_sub, capacity, columns, *refs),
        out_shape=[
            jax.ShapeDtypeStruct((8, BLOCK, 4 * elems), jnp.bfloat16),
            jax.ShapeDtypeStruct(((n_sub + 1) * rows, 4 * elems), jnp.bfloat16),
            jax.ShapeDtypeStruct((2, 6 * GROUP, BLOCK), jnp.bfloat16),
            jax.ShapeDtypeStruct((6 * GROUP, 6 * GROUP), jnp.bfloat16),
            jax.ShapeDtypeStruct((slots, elems), jnp.bfloat16),
        ],
        compiler_params=params,
        cost_estimate=pl.CostEstimate(
            flops=8 * BLOCK * faces * 8 * elems, bytes_accessed=4 << 20, transcendentals=0
        ),
        name="prepare",
    )(sub, table, matrix, mass, elem_face, owner)
    sent = pl.pallas_call(
        lambda *refs: element_kernel(columns, *refs),
        out_shape=jax.ShapeDtypeStruct((slots, 128), jnp.bfloat16),
        scratch_shapes=[
            pltpu.VMEM((8, columns, BLOCK // columns, 4 * elems), jnp.bfloat16),
            pltpu.VMEM((8 * width, elems), jnp.float32),
        ],
        compiler_params=params,
        name="elements",
    )(volume, slot, *fixed, *halos)
    got = lax.all_to_all(sent, ("dom", "sub"), split_axis=0, concat_axis=0, tiled=True)
    summed = pl.pallas_call(
        lambda *refs: voxel_kernel(width, *refs),
        out_shape=jax.ShapeDtypeStruct((width, elems), jnp.float32),
        compiler_params=params,
        name="voxels",
    )(got)
    return summed.reshape(6, columns, elems)


def solution(mesh):
    return jax.shard_map(
        per_device,
        mesh=mesh,
        in_specs=(
            P(None, None, None, "rhs", ("groups", "dom", "sub")),
            P("groups", None, None, None),
            P(),
            P(None, ("dom", "sub")),
            P(None, ("dom", "sub")),
            P(None, ("dom", "sub")),
            P(("dom", "sub")),
            P(("dom", "sub"), None),
            P(("dom", "sub")),
        ),
        out_specs=P(None, "rhs", ("groups", "dom", "sub")),
        check_vma=False,
    )
```

```python
import math

import jax
import jax.numpy as jnp
from jax import lax
from jax.experimental import pallas as pl
from jax.experimental.pallas import tpu as pltpu
from jax.sharding import PartitionSpec as P

BASIS = 35
HALF = 3 * BASIS
GROUP = 40
NODES = 30
BLOCK = 256
N_INPUTS = 9
CHUNKS = 5
UNROLL = 8
VMEM_LIMIT = 24 * 1024 * 1024

NT = (((1,), (1,)), ((), ()))
NN = (((1,), (0,)), ((), ()))
TN = (((0,), (0,)), ((), ()))


def dot(a, b, dims=NN):
    return lax.dot_general(a, b, dims, preferred_element_type=jnp.float32)


def iota(shape, axis):
    return lax.broadcasted_iota(jnp.int32, shape, axis)


def one_hot(condition):
    return jnp.where(condition, 1.0, 0.0).astype(jnp.bfloat16)


def pair_index(index, k, size):
    if size & (size - 1) == 0:
        return index ^ k, index ^ k
    return lax.rem(index + k, size), lax.rem(index + size - k, size)


def pack_kernel(n_sub, rows, *refs):
    hbm_refs, refs = refs[:N_INPUTS], refs[N_INPUTS:]
    vmem_refs, refs = refs[:N_INPUTS], refs[N_INPUTS:]
    out_refs, (sems, chunk_sems) = refs[: n_sub + 1], refs[n_sub + 1 :]
    copies = [
        pltpu.make_async_copy(hbm_refs[i], vmem_refs[i], sems.at[i]) for i in range(1, N_INPUTS)
    ]
    for copy in copies[:2]:
        copy.start()
    table_ref, dom_ref, sub_ref = vmem_refs[:3]
    values, faces = table_ref.shape
    step = values // CHUNKS
    chunks = []
    for k in range(CHUNKS):
        part = pl.ds(k * step, step)
        chunks.append(
            pltpu.make_async_copy(hbm_refs[0].at[part, :], table_ref.at[part, :], chunk_sems.at[k])
        )
        chunks[k].start()
    for copy in copies[2:]:
        copy.start()
    for copy in copies[:2]:
        copy.wait()
    parity = lax.rem(lax.axis_index("dom"), 2)
    within = lax.axis_index("sub")
    lists = [dom_ref[pl.ds(1 - parity, 1), :], dom_ref[pl.ds(parity, 1), :]]
    for k in range(1, n_sub):
        lists.append(sub_ref[pl.ds(pair_index(within, k, n_sub)[0], 1), :])
    face = iota((faces, rows), 0)
    picks = [jnp.where(face == row, 1.0, 0.0).T for row in lists]
    picks = jnp.concatenate(picks, axis=0).astype(jnp.bfloat16)
    for k in range(CHUNKS):
        chunks[k].wait()
        part = slice(k * step, (k + 1) * step)
        packed = dot(picks, table_ref[part, :], NT).astype(jnp.bfloat16)
        for i, out_ref in enumerate(out_refs):
            out_ref[:, part] = packed[i * rows : (i + 1) * rows]
    for copy in copies[2:]:
        copy.wait()


def reorder_matrix(columns):
    per_block = BLOCK // columns
    row = iota((BLOCK, BLOCK), 0)
    col = iota((BLOCK, BLOCK), 1)
    return one_hot(lax.rem(row, per_block) * columns + lax.div(row, per_block) == col)


def block_starts(columns):
    half = 2 * NODES * columns
    return [a * half - (a * half) % 128 + b * BLOCK for a in range(2) for b in range(4)]


def prepare_kernel(
    n_sub,
    capacity,
    columns,
    sub_ref,
    table_ref,
    solver_ref,
    mass_ref,
    elem_ref,
    owner_ref,
    own_ref,
    places_ref,
    matrix_ref,
    masses_ref,
    sends_ref,
):
    faces = table_ref.shape[1]
    elems = elem_ref.shape[1]
    rows = sub_ref.shape[1]
    slots = sends_ref.shape[0]
    parity = lax.rem(lax.axis_index("dom"), 2)
    within = lax.axis_index("sub")
    face_rows = [elem_ref[f : f + 1, :] for f in range(4)]

    def picks(size, start):
        return jnp.concatenate(
            [jnp.where(iota((size, elems), 0) + start == row, 1.0, 0.0) for row in face_rows],
            axis=1,
        )

    own_list = sub_ref[pl.ds(within, 1), :]
    own_list = one_hot(iota((faces, rows), 0) == own_list)
    own_block = picks(rows, faces + (2 + within) * rows).astype(jnp.bfloat16)
    own = (picks(faces, 0) + dot(own_list, own_block)).astype(jnp.bfloat16)
    blocks = [1 - parity, parity]
    for k in range(1, n_sub):
        blocks.append(2 + pair_index(within, k, n_sub)[1])
    place = jnp.full(elem_ref.shape, -1, jnp.int32)
    for i, block in enumerate(blocks):
        offset = elem_ref[...] - (faces + block * rows)
        place = jnp.where((offset >= 0) & (offset < rows), offset + i * rows, place)
    places_ref[...] = place

    reorder = reorder_matrix(columns)
    for b, start in enumerate(block_starts(columns)):
        mine = dot(reorder, table_ref[start : start + BLOCK, :]).astype(jnp.bfloat16)
        own_ref[b] = dot(mine, own).astype(jnp.bfloat16)

    place = iota((3 * GROUP, HALF), 0)
    source = iota((3 * GROUP, HALF), 1)
    spread = one_hot(
        (lax.div(place, GROUP) == lax.div(source, BASIS))
        & (lax.rem(place, GROUP) == lax.rem(source, BASIS))
    )
    solver = solver_ref[:HALF].astype(jnp.float32)
    real = dot(spread, solver[:, 0, :].astype(jnp.bfloat16)).astype(jnp.bfloat16)
    imag = dot(spread, solver[:, 1, :].astype(jnp.bfloat16)).astype(jnp.bfloat16)
    half = 2 * NODES * columns
    for a in range(2):
        shift = ((a * half) % 128) // columns
        source = iota((4 * NODES, BLOCK), 0)
        place = iota((4 * NODES, BLOCK), 1)
        target = lax.div(source, NODES) * 64 + lax.rem(source, NODES) + shift
        for_real = one_hot(target == place)
        for_imag = one_hot(target + NODES == place)
        top = dot(real, for_real) - dot(imag, for_imag)
        bottom = dot(imag, for_real) + dot(real, for_imag)
        matrix_ref[a] = jnp.concatenate([top, bottom], axis=0).astype(jnp.bfloat16)

    size = 6 * GROUP
    spread = one_hot(lax.rem(iota((size, BASIS), 0), GROUP) == iota((size, BASIS), 1))
    tiles = dot(dot(spread, mass_ref[...]).astype(jnp.bfloat16), spread, NT)
    row = iota((size, size), 0)
    col = iota((size, size), 1)
    tiles = jnp.where(lax.div(row, GROUP) == lax.div(col, GROUP), tiles, 0.0)
    masses_ref[...] = jnp.where(row < 3 * GROUP, tiles, -tiles).astype(jnp.bfloat16)

    owner = owner_ref[...]
    owners = iota((max(8, slots // capacity), elems), 0) == owner
    earlier = one_hot(iota((elems, elems), 0) < iota((elems, elems), 1))
    counts = dot(one_hot(owners), earlier)
    rank = jnp.sum(jnp.where(owners, counts, 0.0), axis=0, keepdims=True)
    target = owner * capacity + rank.astype(jnp.int32)
    sends_ref[...] = one_hot(iota((slots, elems), 0) == target)


def element_kernel(
    columns,
    volume_ref,
    slot_ref,
    own_ref,
    places_ref,
    matrix_ref,
    masses_ref,
    sends_ref,
    *refs,
):
    halo_refs = refs[:-3]
    out_ref, gathered_ref, sums_ref = refs[-3:]
    elems = volume_ref.shape[1]
    per_block = BLOCK // columns
    reorder = reorder_matrix(columns)
    halo_rows = [ref[...] for ref in halo_refs]
    count = sum(rows.shape[0] for rows in halo_rows)
    tiles = -(-count // 128)
    halo_rows.append(jnp.zeros((tiles * 128 - count, halo_rows[0].shape[1]), jnp.bfloat16))
    halo_rows = jnp.concatenate(halo_rows, axis=0)
    lanes, inside = [], []
    for f in range(4):
        place = jnp.broadcast_to(places_ref[f : f + 1, :], (BLOCK, elems))
        for t in range(tiles):
            lanes.append(jnp.clip(place - t * 128, 0, 127))
            inside.append((place >= t * 128) & (place < (t + 1) * 128))
    for b, start in enumerate(block_starts(columns)):
        others = dot(reorder, halo_rows[:, start : start + BLOCK], NT)
        for f in range(4):
            part = slice(f * elems, (f + 1) * elems)
            got = own_ref[b, :, part]
            for t in range(tiles):
                found = jnp.take_along_axis(
                    others[:, t * 128 : (t + 1) * 128],
                    lanes[f * tiles + t],
                    axis=1,
                    mode="promise_in_bounds",
                )
                got = got + jnp.where(inside[f * tiles + t], found, 0.0).astype(jnp.bfloat16)
            gathered_ref[b, :, :, part] = got.reshape(columns, per_block, elems)

    masses = masses_ref[...]
    pairs = [(0, 0), (1, 1), (2, 2), (0, 1), (0, 2), (1, 2)]

    def step(index, carry):
        fields = []
        for a in range(2):
            parts = []
            for c in range(2):
                taken = [gathered_ref[a * 4 + b, 2 * index + c] for b in range(4)]
                parts.append(
                    jnp.concatenate(
                        [
                            taken[b][:, f * elems : (f + 1) * elems]
                            for f in range(4)
                            for b in range(4)
                        ],
                        axis=0,
                    )
                )
            values = dot(matrix_ref[a], jnp.concatenate(parts, axis=1))
            fields.append(values.astype(jnp.bfloat16))
        weighted = dot(masses, fields[0])
        shape = (2, 3, GROUP // 8, 8, 2 * elems)
        adjoint = fields[1].astype(jnp.float32).reshape(shape)
        weighted = weighted.reshape(shape)
        for m, (i, j) in enumerate(pairs):
            products = adjoint[:, i] * weighted[:, j]
            if i != j:
                products = products + adjoint[:, j] * weighted[:, i]
            total = jnp.sum(products, axis=(0, 1))
            for c in range(2):
                start = pl.multiple_of((m * columns + 2 * index + c) * 8, 8)
                sums_ref[pl.ds(start, 8), :] = total[:, c * elems : (c + 1) * elems]
        return carry

    lax.fori_loop(0, columns // 2, step, 0, unroll=UNROLL)

    width = 6 * columns
    total = sums_ref[pl.ds(0, width, stride=8), :]
    for k in range(1, 8):
        total = total + sums_ref[pl.ds(k, width, stride=8), :]
    norm = 1.0 / math.sqrt(70.0)
    factor = jnp.where(iota((width, 1), 0) < 3 * columns, norm, 0.5 * norm)
    terms = total * (factor * volume_ref[...])
    slot = jnp.broadcast_to(slot_ref[...].astype(jnp.float32), (128 - width, elems))
    payload = jnp.concatenate([terms, slot], axis=0).astype(jnp.bfloat16)
    out_ref[...] = dot(sends_ref[...], payload, NT).astype(jnp.bfloat16)


def voxel_kernel(width, got_ref, out_ref):
    got = got_ref[...]
    slot = got[:, width : width + 1].astype(jnp.int32)
    voxels = out_ref.shape[1]
    members = one_hot(slot == iota((got.shape[0], voxels), 1))
    out_ref[...] = dot(got, members, TN)[:width]


def per_device(
    traces, solver, mass, dom_lists, sub_lists, elem_face, volume, elem_owner, elem_slot
):
    n_dom, n_sub = lax.axis_size("dom"), lax.axis_size("sub")
    owners = n_dom * n_sub
    columns, faces = traces.shape[3:]
    rows = dom_lists.shape[1]
    elems = elem_face.shape[1]
    capacity = max(2, 3 * elems // owners)
    width = 6 * columns
    table = traces.reshape(-1, faces)
    values = table.shape[0]
    params = pltpu.CompilerParams(vmem_limit_bytes=VMEM_LIMIT)

    inputs = [
        table,
        dom_lists,
        sub_lists,
        solver[0].transpose(1, 0, 2),
        mass[0],
        elem_face,
        volume.reshape(1, elems),
        elem_owner.reshape(1, elems),
        elem_slot.reshape(1, elems),
    ]
    inputs = [pltpu.with_memory_space_constraint(x, pltpu.HBM) for x in inputs]
    outs = pl.pallas_call(
        lambda *refs: pack_kernel(n_sub, rows, *refs),
        in_specs=[pl.BlockSpec(memory_space=pltpu.HBM)] * N_INPUTS,
        out_shape=[pltpu.VMEM(x.shape, x.dtype) for x in inputs]
        + [pltpu.VMEM((rows, values), jnp.bfloat16)] * (n_sub + 1),
        out_specs=[pl.BlockSpec(memory_space=pltpu.VMEM)] * (N_INPUTS + n_sub + 1),
        scratch_shapes=[
            pltpu.SemaphoreType.DMA((N_INPUTS,)),
            pltpu.SemaphoreType.DMA((CHUNKS,)),
        ],
        compiler_params=params,
        name="pack",
    )(*inputs)
    table, _, sub, matrix, mass, elem_face, volume, owner, slot = outs[:N_INPUTS]
    packed = outs[N_INPUTS:]

    even = [(i, i + 1) for i in range(0, n_dom - 1, 2)]
    odd = [(i, i + 1) for i in range(1, n_dom - 1, 2)]
    halos = [
        lax.ppermute(part, "dom", pairs + [(j, i) for i, j in pairs])
        for part, pairs in zip(packed, (even, odd))
    ]
    for k in range(1, n_sub):
        pairs = [(i, pair_index(i, k, n_sub)[0]) for i in range(n_sub)]
        halos.append(lax.ppermute(packed[1 + k], "sub", [(i, int(j)) for i, j in pairs]))

    slots = owners * capacity
    fixed = pl.pallas_call(
        lambda *refs: prepare_kernel(n_sub, capacity, columns, *refs),
        out_shape=[
            jax.ShapeDtypeStruct((8, BLOCK, 4 * elems), jnp.bfloat16),
            jax.ShapeDtypeStruct((4, elems), jnp.int32),
            jax.ShapeDtypeStruct((2, 6 * GROUP, BLOCK), jnp.bfloat16),
            jax.ShapeDtypeStruct((6 * GROUP, 6 * GROUP), jnp.bfloat16),
            jax.ShapeDtypeStruct((slots, elems), jnp.bfloat16),
        ],
        compiler_params=params,
        cost_estimate=pl.CostEstimate(
            flops=8 * BLOCK * faces * 8 * elems, bytes_accessed=4 << 20, transcendentals=0
        ),
        name="prepare",
    )(sub, table, matrix, mass, elem_face, owner)
    sent = pl.pallas_call(
        lambda *refs: element_kernel(columns, *refs),
        out_shape=jax.ShapeDtypeStruct((slots, 128), jnp.bfloat16),
        scratch_shapes=[
            pltpu.VMEM((8, columns, BLOCK // columns, 4 * elems), jnp.bfloat16),
            pltpu.VMEM((8 * width, elems), jnp.float32),
        ],
        compiler_params=params,
        name="elements",
    )(volume, slot, *fixed, *halos)
    got = lax.all_to_all(sent, ("dom", "sub"), split_axis=0, concat_axis=0, tiled=True)
    summed = pl.pallas_call(
        lambda *refs: voxel_kernel(width, *refs),
        out_shape=jax.ShapeDtypeStruct((width, elems), jnp.float32),
        compiler_params=params,
        name="voxels",
    )(got)
    return summed.reshape(6, columns, elems)


def solution(mesh):
    return jax.shard_map(
        per_device,
        mesh=mesh,
        in_specs=(
            P(None, None, None, "rhs", ("groups", "dom", "sub")),
            P("groups", None, None, None),
            P(),
            P(None, ("dom", "sub")),
            P(None, ("dom", "sub")),
            P(None, ("dom", "sub")),
            P(("dom", "sub")),
            P(("dom", "sub"), None),
            P(("dom", "sub")),
        ),
        out_specs=P(None, "rhs", ("groups", "dom", "sub")),
        check_vma=False,
    )
```

```python
import math

import jax
import jax.numpy as jnp
from jax import lax
from jax.experimental import pallas as pl
from jax.experimental.pallas import tpu as pltpu
from jax.sharding import PartitionSpec as P

BASIS = 35
HALF = 3 * BASIS
GROUP = 40
NODES = 30
BLOCK = 256
N_INPUTS = 9
CHUNKS = 1
UNROLL = 8
VMEM_LIMIT = 24 * 1024 * 1024

NT = (((1,), (1,)), ((), ()))
NN = (((1,), (0,)), ((), ()))
TN = (((0,), (0,)), ((), ()))


def dot(a, b, dims=NN):
    return lax.dot_general(a, b, dims, preferred_element_type=jnp.float32)


def iota(shape, axis):
    return lax.broadcasted_iota(jnp.int32, shape, axis)


def one_hot(condition):
    return jnp.where(condition, 1.0, 0.0).astype(jnp.bfloat16)


def pair_index(index, k, size):
    if size & (size - 1) == 0:
        return index ^ k, index ^ k
    return lax.rem(index + k, size), lax.rem(index + size - k, size)


def pack_kernel(n_sub, rows, *refs):
    hbm_refs, refs = refs[:N_INPUTS], refs[N_INPUTS:]
    vmem_refs, refs = refs[:N_INPUTS], refs[N_INPUTS:]
    out_refs, (sems, chunk_sems) = refs[: n_sub + 1], refs[n_sub + 1 :]
    copies = [
        pltpu.make_async_copy(hbm_refs[i], vmem_refs[i], sems.at[i]) for i in range(1, N_INPUTS)
    ]
    for copy in copies[:2]:
        copy.start()
    table_ref, dom_ref, sub_ref = vmem_refs[:3]
    values, faces = table_ref.shape
    step = values // CHUNKS
    chunks = []
    for k in range(CHUNKS):
        part = pl.ds(k * step, step)
        chunks.append(
            pltpu.make_async_copy(hbm_refs[0].at[part, :], table_ref.at[part, :], chunk_sems.at[k])
        )
        chunks[k].start()
    for copy in copies[2:]:
        copy.start()
    for copy in copies[:2]:
        copy.wait()
    parity = lax.rem(lax.axis_index("dom"), 2)
    within = lax.axis_index("sub")
    lists = [dom_ref[pl.ds(1 - parity, 1), :], dom_ref[pl.ds(parity, 1), :]]
    for k in range(1, n_sub):
        lists.append(sub_ref[pl.ds(pair_index(within, k, n_sub)[0], 1), :])
    face = iota((faces, rows), 0)
    picks = [jnp.where(face == row, 1.0, 0.0).T for row in lists]
    picks = jnp.concatenate(picks, axis=0).astype(jnp.bfloat16)
    for k in range(CHUNKS):
        chunks[k].wait()
        part = slice(k * step, (k + 1) * step)
        packed = dot(picks, table_ref[part, :], NT).astype(jnp.bfloat16)
        for i, out_ref in enumerate(out_refs):
            out_ref[:, part] = packed[i * rows : (i + 1) * rows]
    for copy in copies[2:]:
        copy.wait()


def reorder_matrix(columns):
    per_block = BLOCK // columns
    row = iota((BLOCK, BLOCK), 0)
    col = iota((BLOCK, BLOCK), 1)
    return one_hot(lax.rem(row, per_block) * columns + lax.div(row, per_block) == col)


def block_starts(columns):
    half = 2 * NODES * columns
    return [a * half - (a * half) % 128 + b * BLOCK for a in range(2) for b in range(4)]


def prepare_kernel(
    n_sub,
    capacity,
    columns,
    sub_ref,
    table_ref,
    solver_ref,
    mass_ref,
    elem_ref,
    owner_ref,
    own_ref,
    places_ref,
    matrix_ref,
    masses_ref,
    sends_ref,
):
    faces = table_ref.shape[1]
    elems = elem_ref.shape[1]
    rows = sub_ref.shape[1]
    slots = sends_ref.shape[0]
    parity = lax.rem(lax.axis_index("dom"), 2)
    within = lax.axis_index("sub")
    face_rows = [elem_ref[f : f + 1, :] for f in range(4)]

    def picks(size, start):
        return jnp.concatenate(
            [jnp.where(iota((size, elems), 0) + start == row, 1.0, 0.0) for row in face_rows],
            axis=1,
        )

    own_list = sub_ref[pl.ds(within, 1), :]
    own_list = one_hot(iota((faces, rows), 0) == own_list)
    own_block = picks(rows, faces + (2 + within) * rows).astype(jnp.bfloat16)
    own = (picks(faces, 0) + dot(own_list, own_block)).astype(jnp.bfloat16)
    blocks = [1 - parity, parity]
    for k in range(1, n_sub):
        blocks.append(2 + pair_index(within, k, n_sub)[1])
    place = jnp.full(elem_ref.shape, -1, jnp.int32)
    for i, block in enumerate(blocks):
        offset = elem_ref[...] - (faces + block * rows)
        place = jnp.where((offset >= 0) & (offset < rows), offset + i * rows, place)
    places_ref[...] = place

    reorder = reorder_matrix(columns)
    for b, start in enumerate(block_starts(columns)):
        mine = dot(reorder, table_ref[start : start + BLOCK, :]).astype(jnp.bfloat16)
        own_ref[b] = dot(mine, own).astype(jnp.bfloat16)

    place = iota((3 * GROUP, HALF), 0)
    source = iota((3 * GROUP, HALF), 1)
    spread = one_hot(
        (lax.div(place, GROUP) == lax.div(source, BASIS))
        & (lax.rem(place, GROUP) == lax.rem(source, BASIS))
    )
    solver = solver_ref[:HALF].astype(jnp.float32)
    real = dot(spread, solver[:, 0, :].astype(jnp.bfloat16)).astype(jnp.bfloat16)
    imag = dot(spread, solver[:, 1, :].astype(jnp.bfloat16)).astype(jnp.bfloat16)
    half = 2 * NODES * columns
    for a in range(2):
        shift = ((a * half) % 128) // columns
        source = iota((4 * NODES, BLOCK), 0)
        place = iota((4 * NODES, BLOCK), 1)
        target = lax.div(source, NODES) * 64 + lax.rem(source, NODES) + shift
        for_real = one_hot(target == place)
        for_imag = one_hot(target + NODES == place)
        top = dot(real, for_real) - dot(imag, for_imag)
        bottom = dot(imag, for_real) + dot(real, for_imag)
        matrix_ref[a] = jnp.concatenate([top, bottom], axis=0).astype(jnp.bfloat16)

    size = 6 * GROUP
    spread = one_hot(lax.rem(iota((size, BASIS), 0), GROUP) == iota((size, BASIS), 1))
    tiles = dot(dot(spread, mass_ref[...]).astype(jnp.bfloat16), spread, NT)
    row = iota((size, size), 0)
    col = iota((size, size), 1)
    tiles = jnp.where(lax.div(row, GROUP) == lax.div(col, GROUP), tiles, 0.0)
    masses_ref[...] = jnp.where(row < 3 * GROUP, tiles, -tiles).astype(jnp.bfloat16)

    owner = owner_ref[...]
    owners = iota((max(8, slots // capacity), elems), 0) == owner
    earlier = one_hot(iota((elems, elems), 0) < iota((elems, elems), 1))
    counts = dot(one_hot(owners), earlier)
    rank = jnp.sum(jnp.where(owners, counts, 0.0), axis=0, keepdims=True)
    target = owner * capacity + rank.astype(jnp.int32)
    sends_ref[...] = one_hot(iota((slots, elems), 0) == target)


def element_kernel(
    columns,
    volume_ref,
    slot_ref,
    own_ref,
    places_ref,
    matrix_ref,
    masses_ref,
    sends_ref,
    *refs,
):
    halo_refs = refs[:-3]
    out_ref, gathered_ref, sums_ref = refs[-3:]
    elems = volume_ref.shape[1]
    per_block = BLOCK // columns
    reorder = reorder_matrix(columns)
    halo_rows = [ref[...] for ref in halo_refs]
    count = sum(rows.shape[0] for rows in halo_rows)
    tiles = -(-count // 128)
    halo_rows.append(jnp.zeros((tiles * 128 - count, halo_rows[0].shape[1]), jnp.bfloat16))
    halo_rows = jnp.concatenate(halo_rows, axis=0)
    lanes, inside = [], []
    for f in range(4):
        place = jnp.broadcast_to(places_ref[f : f + 1, :], (BLOCK, elems))
        for t in range(tiles):
            lanes.append(jnp.clip(place - t * 128, 0, 127))
            inside.append((place >= t * 128) & (place < (t + 1) * 128))
    for b, start in enumerate(block_starts(columns)):
        others = dot(reorder, halo_rows[:, start : start + BLOCK], NT)
        for f in range(4):
            part = slice(f * elems, (f + 1) * elems)
            got = own_ref[b, :, part]
            for t in range(tiles):
                found = jnp.take_along_axis(
                    others[:, t * 128 : (t + 1) * 128],
                    lanes[f * tiles + t],
                    axis=1,
                    mode="promise_in_bounds",
                )
                got = got + jnp.where(inside[f * tiles + t], found, 0.0).astype(jnp.bfloat16)
            gathered_ref[b, :, :, part] = got.reshape(columns, per_block, elems)

    masses = masses_ref[...]
    pairs = [(0, 0), (1, 1), (2, 2), (0, 1), (0, 2), (1, 2)]

    def step(index, carry):
        fields = []
        for a in range(2):
            parts = []
            for c in range(2):
                taken = [gathered_ref[a * 4 + b, 2 * index + c] for b in range(4)]
                parts.append(
                    jnp.concatenate(
                        [
                            taken[b][:, f * elems : (f + 1) * elems]
                            for f in range(4)
                            for b in range(4)
                        ],
                        axis=0,
                    )
                )
            values = dot(matrix_ref[a], jnp.concatenate(parts, axis=1))
            fields.append(values.astype(jnp.bfloat16))
        weighted = dot(masses, fields[0])
        shape = (2, 3, GROUP // 8, 8, 2 * elems)
        adjoint = fields[1].astype(jnp.float32).reshape(shape)
        weighted = weighted.reshape(shape)
        for m, (i, j) in enumerate(pairs):
            products = adjoint[:, i] * weighted[:, j]
            if i != j:
                products = products + adjoint[:, j] * weighted[:, i]
            total = jnp.sum(products, axis=(0, 1))
            for c in range(2):
                start = pl.multiple_of((m * columns + 2 * index + c) * 8, 8)
                sums_ref[pl.ds(start, 8), :] = total[:, c * elems : (c + 1) * elems]
        return carry

    lax.fori_loop(0, columns // 2, step, 0, unroll=UNROLL)

    width = 6 * columns
    total = sums_ref[pl.ds(0, width, stride=8), :]
    for k in range(1, 8):
        total = total + sums_ref[pl.ds(k, width, stride=8), :]
    norm = 1.0 / math.sqrt(70.0)
    factor = jnp.where(iota((width, 1), 0) < 3 * columns, norm, 0.5 * norm)
    terms = total * (factor * volume_ref[...])
    slot = jnp.broadcast_to(slot_ref[...].astype(jnp.float32), (128 - width, elems))
    payload = jnp.concatenate([terms, slot], axis=0).astype(jnp.bfloat16)
    out_ref[...] = dot(sends_ref[...], payload, NT).astype(jnp.bfloat16)


def voxel_kernel(width, got_ref, out_ref):
    got = got_ref[...]
    slot = got[:, width : width + 1].astype(jnp.int32)
    voxels = out_ref.shape[1]
    members = one_hot(slot == iota((got.shape[0], voxels), 1))
    out_ref[...] = dot(got, members, TN)[:width]


def per_device(
    traces, solver, mass, dom_lists, sub_lists, elem_face, volume, elem_owner, elem_slot
):
    n_dom, n_sub = lax.axis_size("dom"), lax.axis_size("sub")
    owners = n_dom * n_sub
    columns, faces = traces.shape[3:]
    rows = dom_lists.shape[1]
    elems = elem_face.shape[1]
    capacity = max(2, 3 * elems // owners)
    width = 6 * columns
    table = traces.reshape(-1, faces)
    values = table.shape[0]
    params = pltpu.CompilerParams(vmem_limit_bytes=VMEM_LIMIT)

    inputs = [
        table,
        dom_lists,
        sub_lists,
        solver[0].transpose(1, 0, 2),
        mass[0],
        elem_face,
        volume.reshape(1, elems),
        elem_owner.reshape(1, elems),
        elem_slot.reshape(1, elems),
    ]
    inputs = [pltpu.with_memory_space_constraint(x, pltpu.HBM) for x in inputs]
    outs = pl.pallas_call(
        lambda *refs: pack_kernel(n_sub, rows, *refs),
        in_specs=[pl.BlockSpec(memory_space=pltpu.HBM)] * N_INPUTS,
        out_shape=[pltpu.VMEM(x.shape, x.dtype) for x in inputs]
        + [pltpu.VMEM((rows, values), jnp.bfloat16)] * (n_sub + 1),
        out_specs=[pl.BlockSpec(memory_space=pltpu.VMEM)] * (N_INPUTS + n_sub + 1),
        scratch_shapes=[
            pltpu.SemaphoreType.DMA((N_INPUTS,)),
            pltpu.SemaphoreType.DMA((CHUNKS,)),
        ],
        compiler_params=params,
        name="pack",
    )(*inputs)
    table, _, sub, matrix, mass, elem_face, volume, owner, slot = outs[:N_INPUTS]
    packed = outs[N_INPUTS:]

    n_rhs = lax.axis_size("rhs")
    halos = []
    for odd, part in enumerate(packed[:2]):
        pairs = []
        for d in range(n_dom):
            other = d + 1 if (d - odd) % 2 == 0 else d - 1
            inside = 0 <= other < n_dom
            for s in range(n_sub):
                for c in range(n_rhs):
                    target = (other * n_sub + s) * n_rhs + c
                    if not inside:
                        target = (d * n_sub + s) * n_rhs + n_rhs - 1 - c
                    pairs.append(((d * n_sub + s) * n_rhs + c, target))
        halos.append(lax.ppermute(part, ("dom", "sub", "rhs"), pairs))
    for k in range(1, n_sub):
        pairs = [(i, pair_index(i, k, n_sub)[0]) for i in range(n_sub)]
        halos.append(lax.ppermute(packed[1 + k], "sub", [(i, int(j)) for i, j in pairs]))

    slots = owners * capacity
    fixed = pl.pallas_call(
        lambda *refs: prepare_kernel(n_sub, capacity, columns, *refs),
        out_shape=[
            jax.ShapeDtypeStruct((8, BLOCK, 4 * elems), jnp.bfloat16),
            jax.ShapeDtypeStruct((4, elems), jnp.int32),
            jax.ShapeDtypeStruct((2, 6 * GROUP, BLOCK), jnp.bfloat16),
            jax.ShapeDtypeStruct((6 * GROUP, 6 * GROUP), jnp.bfloat16),
            jax.ShapeDtypeStruct((slots, elems), jnp.bfloat16),
        ],
        compiler_params=params,
        cost_estimate=pl.CostEstimate(
            flops=8 * BLOCK * faces * 8 * elems, bytes_accessed=4 << 20, transcendentals=0
        ),
        name="prepare",
    )(sub, table, matrix, mass, elem_face, owner)
    sent = pl.pallas_call(
        lambda *refs: element_kernel(columns, *refs),
        out_shape=jax.ShapeDtypeStruct((slots, 128), jnp.bfloat16),
        scratch_shapes=[
            pltpu.VMEM((8, columns, BLOCK // columns, 4 * elems), jnp.bfloat16),
            pltpu.VMEM((8 * width, elems), jnp.float32),
        ],
        compiler_params=params,
        name="elements",
    )(volume, slot, *fixed, *halos)
    got = lax.all_to_all(sent, ("dom", "sub"), split_axis=0, concat_axis=0, tiled=True)
    summed = pl.pallas_call(
        lambda *refs: voxel_kernel(width, *refs),
        out_shape=jax.ShapeDtypeStruct((width, elems), jnp.float32),
        compiler_params=params,
        name="voxels",
    )(got)
    return summed.reshape(6, columns, elems)


def solution(mesh):
    return jax.shard_map(
        per_device,
        mesh=mesh,
        in_specs=(
            P(None, None, None, "rhs", ("groups", "dom", "sub")),
            P("groups", None, None, None),
            P(),
            P(None, ("dom", "sub")),
            P(None, ("dom", "sub")),
            P(None, ("dom", "sub")),
            P(("dom", "sub")),
            P(("dom", "sub"), None),
            P(("dom", "sub")),
        ),
        out_specs=P(None, "rhs", ("groups", "dom", "sub")),
        check_vma=False,
    )
```

```python
import math

import jax
import jax.numpy as jnp
from jax import lax
from jax.experimental import pallas as pl
from jax.experimental.pallas import tpu as pltpu
from jax.sharding import PartitionSpec as P

BASIS = 35
HALF = 3 * BASIS
NODES = 30
BLOCK = 256
N_SMALL = 6
FULL = 32
ROWS = 216
UNROLL = 8
VMEM_LIMIT = 24 * 1024 * 1024

NT = (((1,), (1,)), ((), ()))
NN = (((1,), (0,)), ((), ()))
TN = (((0,), (0,)), ((), ()))


def dot(a, b, dims=NN):
    return lax.dot_general(a, b, dims, preferred_element_type=jnp.float32)


def iota(shape, axis):
    return lax.broadcasted_iota(jnp.int32, shape, axis)


def one_hot(condition):
    return jnp.where(condition, 1.0, 0.0).astype(jnp.bfloat16)


def pair_index(index, k, size):
    if size & (size - 1) == 0:
        return index ^ k, index ^ k
    return lax.rem(index + k, size), lax.rem(index + size - k, size)


def pack_kernel(n_sub, rows, traces_hbm, dom_hbm, sub_hbm, table_ref, sub_ref, *refs):
    out_refs, (dom_ref, sems) = refs[: n_sub + 1], refs[n_sub + 1 :]
    faces = table_ref.shape[1]
    pairs = [(dom_hbm, dom_ref), (sub_hbm, sub_ref), (traces_hbm, table_ref)]
    copies = [pltpu.make_async_copy(*pair, sems.at[i]) for i, pair in enumerate(pairs)]
    for copy in copies:
        copy.start()
    for copy in copies[:2]:
        copy.wait()
    parity = lax.rem(lax.axis_index("dom"), 2)
    within = lax.axis_index("sub")
    lists = [dom_ref[pl.ds(1 - parity, 1), :], dom_ref[pl.ds(parity, 1), :]]
    for k in range(1, n_sub):
        lists.append(sub_ref[pl.ds(pair_index(within, k, n_sub)[0], 1), :])
    face = iota((faces, rows), 0)
    picks = [jnp.where(face == row, 1.0, 0.0).T for row in lists]
    picks = jnp.concatenate(picks, axis=0).astype(jnp.bfloat16)
    copies[2].wait()
    packed = dot(picks, table_ref[...], NT).astype(jnp.bfloat16)
    for i, out_ref in enumerate(out_refs):
        out_ref[...] = packed[i * rows : (i + 1) * rows]


def reorder_matrix(columns):
    per_block = BLOCK // columns
    row = iota((BLOCK, BLOCK), 0)
    col = iota((BLOCK, BLOCK), 1)
    return one_hot(lax.rem(row, per_block) * columns + lax.div(row, per_block) == col)


def block_starts(columns):
    half = 2 * NODES * columns
    return [a * half - (a * half) % 128 + b * BLOCK for a in range(2) for b in range(4)]


def field_row(part, axis, basis):
    tail = 6 * FULL + axis * 8 + part * (BASIS - FULL) + basis - FULL
    return jnp.where(basis < FULL, (part * 3 + axis) * FULL + basis, tail)


def prepare_kernel(n_sub, capacity, columns, sub_ref, table_ref, *refs):
    hbm_refs, refs = refs[:N_SMALL], refs[N_SMALL:]
    own_ref, places_ref, matrix_ref, sends_ref, volume_ref, slot_ref = refs[:6]
    solver_ref, mass_ref, elem_ref, owner_ref, mine_ref, sems = refs[6:]
    vmem_refs = [elem_ref, owner_ref, solver_ref, mass_ref, volume_ref, slot_ref]
    copies = [
        pltpu.make_async_copy(hbm_refs[i], vmem_refs[i], sems.at[i]) for i in range(N_SMALL)
    ]
    for copy in copies:
        copy.start()
    reorder = reorder_matrix(columns)
    for b, start in enumerate(block_starts(columns)):
        mine = dot(reorder, table_ref[start : start + BLOCK, :])
        mine_ref[b] = mine.astype(jnp.bfloat16)
    for copy in copies:
        copy.wait()
    faces = table_ref.shape[1]
    elems = elem_ref.shape[1]
    rows = sub_ref.shape[1]
    slots = sends_ref.shape[0]
    parity = lax.rem(lax.axis_index("dom"), 2)
    within = lax.axis_index("sub")
    face_rows = [elem_ref[f : f + 1, :] for f in range(4)]

    def picks(size, start):
        return jnp.concatenate(
            [jnp.where(iota((size, elems), 0) + start == row, 1.0, 0.0) for row in face_rows],
            axis=1,
        )

    own_list = sub_ref[pl.ds(within, 1), :]
    own_list = one_hot(iota((faces, rows), 0) == own_list)
    own_block = picks(rows, faces + (2 + within) * rows).astype(jnp.bfloat16)
    own = (picks(faces, 0) + dot(own_list, own_block)).astype(jnp.bfloat16)
    blocks = [1 - parity, parity]
    for k in range(1, n_sub):
        blocks.append(2 + pair_index(within, k, n_sub)[1])
    place = jnp.full(elem_ref.shape, -1, jnp.int32)
    for i, block in enumerate(blocks):
        offset = elem_ref[...] - (faces + block * rows)
        place = jnp.where((offset >= 0) & (offset < rows), offset + i * rows, place)
    places_ref[...] = place

    for b in range(8):
        own_ref[b] = dot(mine_ref[b], own).astype(jnp.bfloat16)

    source = iota((ROWS, HALF), 1)
    axis, basis = lax.div(source, BASIS), lax.rem(source, BASIS)
    place = iota((ROWS, HALF), 0)
    spread = [one_hot(place == field_row(part, axis, basis)) for part in range(2)]
    mass = mass_ref[...]
    source = iota((HALF, BASIS), 0)
    column = iota((HALF, BASIS), 1)
    solver = solver_ref[:HALF].astype(jnp.float32)
    real, imag = solver[:, 0, :], solver[:, 1, :]
    half = 2 * NODES * columns
    for a in range(2):
        if a == 0:
            tall = one_hot(lax.rem(source, BASIS) == column)
            wide = dot(dot(tall, mass).astype(jnp.bfloat16), tall, NT)
            same = lax.div(iota((HALF, HALF), 0), BASIS) == lax.div(iota((HALF, HALF), 1), BASIS)
            wide = jnp.where(same, wide, 0.0).astype(jnp.bfloat16)
            parts = [dot(wide, x.astype(jnp.bfloat16)) for x in (real, imag)]
            signs = (1.0, -1.0)
        else:
            parts = [real, imag]
            signs = (1.0, 1.0)
        parts = [x.astype(jnp.bfloat16) for x in parts]
        shift = ((a * half) % 128) // columns
        source_k = iota((4 * NODES, BLOCK), 0)
        place_k = iota((4 * NODES, BLOCK), 1)
        target = lax.div(source_k, NODES) * 64 + lax.rem(source_k, NODES) + shift
        for_real = one_hot(target == place_k)
        for_imag = one_hot(target + NODES == place_k)
        top = signs[0] * (dot(parts[0], for_real) - dot(parts[1], for_imag))
        bottom = signs[1] * (dot(parts[1], for_real) + dot(parts[0], for_imag))
        matrix = dot(spread[0], top.astype(jnp.bfloat16))
        matrix = matrix + dot(spread[1], bottom.astype(jnp.bfloat16))
        matrix_ref[a] = matrix.astype(jnp.bfloat16)

    owner = owner_ref[...]
    owners = iota((max(8, slots // capacity), elems), 0) == owner
    earlier = one_hot(iota((elems, elems), 0) < iota((elems, elems), 1))
    counts = dot(one_hot(owners), earlier)
    rank = jnp.sum(jnp.where(owners, counts, 0.0), axis=0, keepdims=True)
    target = owner * capacity + rank.astype(jnp.int32)
    sends_ref[...] = one_hot(iota((slots, elems), 0) == target)


def element_kernel(
    columns,
    own_ref,
    places_ref,
    matrix_ref,
    sends_ref,
    volume_ref,
    slot_ref,
    *refs,
):
    halo_refs = refs[:-3]
    out_ref, gathered_ref, sums_ref = refs[-3:]
    elems = volume_ref.shape[1]
    per_block = BLOCK // columns
    reorder = reorder_matrix(columns)
    halo_rows = [ref[...] for ref in halo_refs]
    count = sum(rows.shape[0] for rows in halo_rows)
    tiles = -(-count // 128)
    halo_rows.append(jnp.zeros((tiles * 128 - count, halo_rows[0].shape[1]), jnp.bfloat16))
    halo_rows = jnp.concatenate(halo_rows, axis=0)
    lanes, inside = [], []
    for f in range(4):
        place = jnp.broadcast_to(places_ref[f : f + 1, :], (BLOCK, elems))
        for t in range(tiles):
            lanes.append(jnp.clip(place - t * 128, 0, 127))
            inside.append((place >= t * 128) & (place < (t + 1) * 128))
    for b, start in enumerate(block_starts(columns)):
        others = dot(reorder, halo_rows[:, start : start + BLOCK], NT)
        for f in range(4):
            part = slice(f * elems, (f + 1) * elems)
            got = own_ref[b, :, part]
            for t in range(tiles):
                found = jnp.take_along_axis(
                    others[:, t * 128 : (t + 1) * 128],
                    lanes[f * tiles + t],
                    axis=1,
                    mode="promise_in_bounds",
                )
                got = got + jnp.where(inside[f * tiles + t], found, 0.0).astype(jnp.bfloat16)
            gathered_ref[b, :, :, part] = got.reshape(columns, per_block, elems)

    pairs = [(0, 0), (1, 1), (2, 2), (0, 1), (0, 2), (1, 2)]

    def step(index, carry):
        fields = []
        for a in range(2):
            parts = []
            for c in range(2):
                taken = [gathered_ref[a * 4 + b, 2 * index + c] for b in range(4)]
                parts.append(
                    jnp.concatenate(
                        [
                            taken[b][:, f * elems : (f + 1) * elems]
                            for f in range(4)
                            for b in range(4)
                        ],
                        axis=0,
                    )
                )
            fields.append(dot(matrix_ref[a], jnp.concatenate(parts, axis=1)))
        weighted = fields[0]
        adjoint = fields[1].astype(jnp.bfloat16).astype(jnp.float32)
        split = 6 * FULL
        shape = (2, 3, FULL // 8, 8, 2 * elems)
        tail = (3, 8, 2 * elems)
        weighted, weighted_tail = weighted[:split].reshape(shape), weighted[split:].reshape(tail)
        adjoint, adjoint_tail = adjoint[:split].reshape(shape), adjoint[split:].reshape(tail)
        for m, (i, j) in enumerate(pairs):
            products = adjoint[:, i] * weighted[:, j]
            rest = adjoint_tail[i] * weighted_tail[j]
            if i != j:
                products = products + adjoint[:, j] * weighted[:, i]
                rest = rest + adjoint_tail[j] * weighted_tail[i]
            total = jnp.sum(products, axis=(0, 1)) + rest
            for c in range(2):
                start = pl.multiple_of((m * columns + 2 * index + c) * 8, 8)
                sums_ref[pl.ds(start, 8), :] = total[:, c * elems : (c + 1) * elems]
        return carry

    lax.fori_loop(0, columns // 2, step, 0, unroll=UNROLL)

    width = 6 * columns
    total = sums_ref[pl.ds(0, width, stride=8), :]
    for k in range(1, 8):
        total = total + sums_ref[pl.ds(k, width, stride=8), :]
    norm = 1.0 / math.sqrt(70.0)
    factor = jnp.where(iota((width, 1), 0) < 3 * columns, norm, 0.5 * norm)
    terms = total * (factor * volume_ref[...])
    slot = jnp.broadcast_to(slot_ref[...].astype(jnp.float32), (128 - width, elems))
    payload = jnp.concatenate([terms, slot], axis=0).astype(jnp.bfloat16)
    out_ref[...] = dot(sends_ref[...], payload, NT).astype(jnp.bfloat16)


def voxel_kernel(width, got_ref, out_ref):
    got = got_ref[...]
    slot = got[:, width : width + 1].astype(jnp.int32)
    voxels = out_ref.shape[1]
    members = one_hot(slot == iota((got.shape[0], voxels), 1))
    out_ref[...] = dot(got, members, TN)[:width]


def per_device(
    traces, solver, mass, dom_lists, sub_lists, elem_face, volume, elem_owner, elem_slot
):
    n_dom, n_sub = lax.axis_size("dom"), lax.axis_size("sub")
    owners = n_dom * n_sub
    columns, faces = traces.shape[3:]
    rows = dom_lists.shape[1]
    elems = elem_face.shape[1]
    capacity = max(2, 3 * elems // owners)
    width = 6 * columns
    table = traces.reshape(-1, faces)
    values = table.shape[0]
    params = pltpu.CompilerParams(vmem_limit_bytes=VMEM_LIMIT)

    vmem = pl.BlockSpec(memory_space=pltpu.VMEM)
    hbm = pl.BlockSpec(memory_space=pltpu.HBM)

    def in_hbm(*arrays):
        return [pltpu.with_memory_space_constraint(x, pltpu.HBM) for x in arrays]

    table, sub, *packed = pl.pallas_call(
        lambda *refs: pack_kernel(n_sub, rows, *refs),
        in_specs=[hbm] * 3,
        out_shape=[pltpu.VMEM(x.shape, x.dtype) for x in (table, sub_lists)]
        + [pltpu.VMEM((rows, values), jnp.bfloat16)] * (n_sub + 1),
        out_specs=[vmem] * (n_sub + 3),
        scratch_shapes=[
            pltpu.VMEM(dom_lists.shape, jnp.int32),
            pltpu.SemaphoreType.DMA((3,)),
        ],
        compiler_params=params,
        name="pack",
    )(*in_hbm(table, dom_lists, sub_lists))

    n_rhs = lax.axis_size("rhs")
    halos = []
    for odd, part in enumerate(packed[:2]):
        pairs = []
        for d in range(n_dom):
            other = d + 1 if (d - odd) % 2 == 0 else d - 1
            inside = 0 <= other < n_dom
            for s in range(n_sub):
                for c in range(n_rhs):
                    target = (other * n_sub + s) * n_rhs + c
                    if not inside:
                        target = (d * n_sub + s) * n_rhs + n_rhs - 1 - c
                    pairs.append(((d * n_sub + s) * n_rhs + c, target))
        halos.append(lax.ppermute(part, ("dom", "sub", "rhs"), pairs))
    for k in range(1, n_sub):
        pairs = [(i, pair_index(i, k, n_sub)[0]) for i in range(n_sub)]
        halos.append(lax.ppermute(packed[1 + k], "sub", [(i, int(j)) for i, j in pairs]))

    slots = owners * capacity
    matrix = solver[0].transpose(1, 0, 2)
    fixed = pl.pallas_call(
        lambda *refs: prepare_kernel(n_sub, capacity, columns, *refs),
        in_specs=[vmem] * 2 + [hbm] * N_SMALL,
        out_shape=[
            pltpu.VMEM((8, BLOCK, 4 * elems), jnp.bfloat16),
            pltpu.VMEM((4, elems), jnp.int32),
            pltpu.VMEM((2, ROWS, BLOCK), jnp.bfloat16),
            pltpu.VMEM((slots, elems), jnp.bfloat16),
            pltpu.VMEM((1, elems), jnp.float32),
            pltpu.VMEM((1, elems), jnp.int32),
        ],
        out_specs=[vmem] * 6,
        scratch_shapes=[
            pltpu.VMEM(matrix.shape, jnp.bfloat16),
            pltpu.VMEM(mass.shape[1:], jnp.bfloat16),
            pltpu.VMEM((4, elems), jnp.int32),
            pltpu.VMEM((1, elems), jnp.int32),
            pltpu.VMEM((8, BLOCK, faces), jnp.bfloat16),
            pltpu.SemaphoreType.DMA((N_SMALL,)),
        ],
        compiler_params=params,
        cost_estimate=pl.CostEstimate(
            flops=8 * BLOCK * faces * 8 * elems, bytes_accessed=4 << 20, transcendentals=0
        ),
        name="prepare",
    )(
        sub,
        table,
        *in_hbm(
            elem_face,
            elem_owner.reshape(1, elems),
            matrix,
            mass[0],
            volume.reshape(1, elems),
            elem_slot.reshape(1, elems),
        ),
    )
    sent = pl.pallas_call(
        lambda *refs: element_kernel(columns, *refs),
        out_shape=jax.ShapeDtypeStruct((slots, 128), jnp.bfloat16),
        scratch_shapes=[
            pltpu.VMEM((8, columns, BLOCK // columns, 4 * elems), jnp.bfloat16),
            pltpu.VMEM((8 * width, elems), jnp.float32),
        ],
        compiler_params=params,
        name="elements",
    )(*fixed, *halos)
    got = lax.all_to_all(sent, ("dom", "sub"), split_axis=0, concat_axis=0, tiled=True)
    summed = pl.pallas_call(
        lambda *refs: voxel_kernel(width, *refs),
        out_shape=jax.ShapeDtypeStruct((width, elems), jnp.float32),
        compiler_params=params,
        name="voxels",
    )(got)
    return summed.reshape(6, columns, elems)


def solution(mesh):
    return jax.shard_map(
        per_device,
        mesh=mesh,
        in_specs=(
            P(None, None, None, "rhs", ("groups", "dom", "sub")),
            P("groups", None, None, None),
            P(),
            P(None, ("dom", "sub")),
            P(None, ("dom", "sub")),
            P(None, ("dom", "sub")),
            P(("dom", "sub")),
            P(("dom", "sub"), None),
            P(("dom", "sub")),
        ),
        out_specs=P(None, "rhs", ("groups", "dom", "sub")),
        check_vma=False,
    )
```

```python
import math

import jax
import jax.numpy as jnp
from jax import lax
from jax.experimental import pallas as pl
from jax.experimental.pallas import tpu as pltpu
from jax.sharding import PartitionSpec as P

BASIS = 35
HALF = 3 * BASIS
NODES = 30
BLOCK = 256
N_SMALL = 6
FULL = 32
ROWS = 216
PADDED = 112
VMEM_LIMIT = 24 * 1024 * 1024

NT = (((1,), (1,)), ((), ()))
NN = (((1,), (0,)), ((), ()))
TN = (((0,), (0,)), ((), ()))


def dot(a, b, dims=NN):
    return lax.dot_general(a, b, dims, preferred_element_type=jnp.float32)


def iota(shape, axis):
    return lax.broadcasted_iota(jnp.int32, shape, axis)


def one_hot(condition):
    return jnp.where(condition, 1.0, 0.0).astype(jnp.bfloat16)


def pair_index(index, k, size):
    if size & (size - 1) == 0:
        return index ^ k, index ^ k
    return lax.rem(index + k, size), lax.rem(index + size - k, size)


def halo_order(n_sub):
    return [1, 0] + list(range(2, n_sub + 1))


def pack_kernel(n_sub, rows, traces_hbm, dom_hbm, sub_hbm, table_ref, sub_ref, *refs):
    out_refs, (dom_ref, sems) = refs[: n_sub + 1], refs[n_sub + 1 :]
    faces = table_ref.shape[1]
    pairs = [(dom_hbm, dom_ref), (sub_hbm, sub_ref), (traces_hbm, table_ref)]
    copies = [pltpu.make_async_copy(*pair, sems.at[i]) for i, pair in enumerate(pairs)]
    for copy in copies:
        copy.start()
    for copy in copies[:2]:
        copy.wait()
    parity = lax.rem(lax.axis_index("dom"), 2)
    within = lax.axis_index("sub")
    lists = [dom_ref[pl.ds(1 - parity, 1), :], dom_ref[pl.ds(parity, 1), :]]
    for k in range(1, n_sub):
        lists.append(sub_ref[pl.ds(pair_index(within, k, n_sub)[0], 1), :])
    face = iota((faces, rows), 0)
    picks = [jnp.where(face == row, 1.0, 0.0).T for row in lists]
    picks = jnp.concatenate(picks, axis=0).astype(jnp.bfloat16)
    copies[2].wait()
    packed = dot(picks, table_ref[...], NT).astype(jnp.bfloat16)
    for i, out_ref in enumerate(out_refs):
        out_ref[...] = packed[i * rows : (i + 1) * rows]


def reorder_matrix(columns):
    per_block = BLOCK // columns
    row = iota((BLOCK, BLOCK), 0)
    col = iota((BLOCK, BLOCK), 1)
    return one_hot(lax.rem(row, per_block) * columns + lax.div(row, per_block) == col)


def block_starts(columns):
    half = 2 * NODES * columns
    return [a * half - (a * half) % 128 + b * BLOCK for a in range(2) for b in range(4)]


def row_group(row):
    tail = row - 6 * FULL
    within = lax.rem(tail, 8)
    late = BASIS - FULL
    head = row < 6 * FULL
    group = jnp.where(head, lax.div(row, FULL), lax.div(within, late) * 3 + lax.div(tail, 8))
    basis = jnp.where(head, lax.rem(row, FULL), FULL + lax.rem(within, late))
    used = head | (within < 2 * late)
    return jnp.where(used, group, -1), basis


def prepare_kernel(n_sub, capacity, columns, sub_ref, table_ref, *refs):
    hbm_refs, refs = refs[:N_SMALL], refs[N_SMALL:]
    own_ref, places_ref, matrix_ref, sends_ref, volume_ref, slot_ref = refs[:6]
    solver_ref, mass_ref, elem_ref, owner_ref, mine_ref, sems = refs[6:]
    vmem_refs = [elem_ref, owner_ref, solver_ref, mass_ref, volume_ref, slot_ref]
    copies = [
        pltpu.make_async_copy(hbm_refs[i], vmem_refs[i], sems.at[i]) for i in range(N_SMALL)
    ]
    for copy in copies:
        copy.start()
    faces = table_ref.shape[1]
    elems = elem_ref.shape[1]
    rows = sub_ref.shape[1]
    slots = sends_ref.shape[0]
    parity = lax.rem(lax.axis_index("dom"), 2)
    within = lax.axis_index("sub")

    reorder = reorder_matrix(columns)
    for b, start in enumerate(block_starts(columns)):
        mine = dot(reorder, table_ref[start : start + BLOCK, :])
        mine_ref[b] = mine.astype(jnp.bfloat16)
    own_list = sub_ref[pl.ds(within, 1), :]
    square = iota((rows, rows), 0) == iota((rows, rows), 1)
    own_list = jnp.sum(jnp.where(square, own_list, 0), axis=1, keepdims=True)
    half = 2 * NODES * columns
    source = iota((4 * NODES, BLOCK), 0)
    place = iota((4 * NODES, BLOCK), 1)
    target = lax.div(source, NODES) * 64 + lax.rem(source, NODES)
    spots = []
    for a in range(2):
        first = target + ((a * half) % 128) // columns
        spots += [one_hot(first == place), one_hot(first + NODES == place)]
    spots = jnp.concatenate(spots, axis=1)
    group, basis = row_group(iota((ROWS, 1), 0))
    column = iota((1, 2 * PADDED), 1)
    field = lax.rem(column, PADDED)
    column_group = lax.div(column, PADDED) * 3 + lax.div(field, BASIS)
    column_basis = lax.rem(field, BASIS)
    same = (group == column_group) & (field < HALF)
    spread = one_hot(same & (basis == column_basis))
    sign = jnp.where(same, jnp.where(column < PADDED, 1.0, -1.0), 0.0)
    tall = one_hot(basis == iota((ROWS, BASIS), 1))
    wide = one_hot(iota((BASIS, 2 * PADDED), 0) == column_basis)
    earlier = one_hot(iota((elems, elems), 0) < iota((elems, elems), 1))
    for copy in copies:
        copy.wait()

    elem_face = elem_ref[...]
    offset = elem_face - (faces + (2 + within) * rows)
    own = []
    for f in range(4):
        found = jnp.where(iota((rows, elems), 0) == offset[f : f + 1, :], own_list, 0)
        found = jnp.sum(found, axis=0, keepdims=True)
        inside = (offset[f : f + 1, :] >= 0) & (offset[f : f + 1, :] < rows)
        index = jnp.where(inside, found, elem_face[f : f + 1, :])
        own.append(one_hot(iota((faces, elems), 0) == index))
    own = jnp.concatenate(own, axis=1)
    for b in range(8):
        own_ref[b] = dot(mine_ref[b], own).astype(jnp.bfloat16)
    blocks = [1 - parity, parity]
    for k in range(1, n_sub):
        blocks.append(2 + pair_index(within, k, n_sub)[1])
    blocks = [blocks[i] for i in halo_order(n_sub)]
    per_tile = 128 // rows - 1
    for t in range(places_ref.shape[0] // 4):
        lane = jnp.full(elem_face.shape, 127, jnp.int32)
        for i, block in enumerate(blocks[t * per_tile : (t + 1) * per_tile]):
            offset = elem_face - (faces + block * rows)
            lane = jnp.where((offset >= 0) & (offset < rows), offset + i * rows, lane)
        places_ref[4 * t : 4 * t + 4, :] = lane

    solver = solver_ref[:PADDED].astype(jnp.float32)
    solver = jnp.concatenate([solver[:, 0, :], solver[:, 1, :]], axis=0).astype(jnp.bfloat16)
    placed = dot(solver, spots)
    masses = dot(dot(tall, mass_ref[...]).astype(jnp.bfloat16), wide) * sign
    spreads = [masses.astype(jnp.bfloat16), spread]
    for a in range(2):
        first, second = (placed[:, (2 * a + i) * BLOCK : (2 * a + i + 1) * BLOCK] for i in range(2))
        top = first[:PADDED] - second[PADDED:]
        bottom = first[PADDED:] + second[:PADDED]
        both = jnp.concatenate([top, bottom], axis=0).astype(jnp.bfloat16)
        matrix_ref[a] = dot(spreads[a], both).astype(jnp.bfloat16)

    owner = owner_ref[...]
    owners = iota((max(8, slots // capacity), elems), 0) == owner
    counts = dot(one_hot(owners), earlier)
    rank = jnp.sum(jnp.where(owners, counts, 0.0), axis=0, keepdims=True)
    target = owner * capacity + rank.astype(jnp.int32)
    sends_ref[...] = one_hot(iota((slots, elems), 0) == target)


def element_kernel(
    columns,
    own_ref,
    places_ref,
    matrix_ref,
    sends_ref,
    volume_ref,
    slot_ref,
    *refs,
):
    halo_refs, (out_ref, gathered_ref, sums_ref) = refs[:-3], refs[-3:]
    elems = volume_ref.shape[1]
    per_block = BLOCK // columns
    tiles = places_ref.shape[0] // 4
    reorder = reorder_matrix(columns)
    rows, values = halo_refs[0].shape
    per_tile = 128 // rows - 1
    tables = []
    for t in range(tiles):
        parts = [ref[...] for ref in halo_refs[t * per_tile : (t + 1) * per_tile]]
        parts.append(jnp.zeros((128 - rows * len(parts), values), jnp.bfloat16))
        tables.append(jnp.concatenate(parts, axis=0))
    lanes = [jnp.broadcast_to(places_ref[i : i + 1, :], (BLOCK, elems)) for i in range(4 * tiles)]
    starts = block_starts(columns)

    def gather(b):
        part = slice(starts[b], starts[b] + BLOCK)
        others = [dot(reorder, table[:, part], NT) for table in tables]
        for f in range(4):
            part = slice(f * elems, (f + 1) * elems)
            got = own_ref[b, :, part]
            for t in range(tiles):
                found = jnp.take_along_axis(
                    others[t], lanes[4 * t + f], axis=1, mode="promise_in_bounds"
                )
                got = got + found.astype(jnp.bfloat16)
            gathered_ref[b, :, :, part] = got.reshape(columns, per_block, elems)

    def fields(a, index):
        parts = []
        for c in range(2):
            taken = [gathered_ref[a * 4 + b, 2 * index + c] for b in range(4)]
            parts.append(
                jnp.concatenate(
                    [taken[b][:, f * elems : (f + 1) * elems] for f in range(4) for b in range(4)],
                    axis=0,
                )
            )
        return dot(matrix_ref[a], jnp.concatenate(parts, axis=1))

    for b in range(8):
        gather(b)

    pairs = [(0, 0), (1, 1), (2, 2), (0, 1), (0, 2), (1, 2)]
    split = 6 * FULL
    shape = (2, 3, FULL // 8, 8, 2 * elems)
    tail = (3, 8, 2 * elems)
    for index in range(columns // 2):
        weighted = fields(0, index)
        adjoint = fields(1, index).astype(jnp.bfloat16).astype(jnp.float32)
        weighted, weighted_tail = weighted[:split].reshape(shape), weighted[split:].reshape(tail)
        adjoint, adjoint_tail = adjoint[:split].reshape(shape), adjoint[split:].reshape(tail)
        for m, (i, j) in enumerate(pairs):
            products = adjoint[:, i] * weighted[:, j]
            rest = adjoint_tail[i] * weighted_tail[j]
            if i != j:
                products = products + adjoint[:, j] * weighted[:, i]
                rest = rest + adjoint_tail[j] * weighted_tail[i]
            total = jnp.sum(products, axis=(0, 1)) + rest
            for c in range(2):
                start = (m * columns + 2 * index + c) * 8
                sums_ref[start : start + 8, :] = total[:, c * elems : (c + 1) * elems]

    width = 6 * columns
    total = sums_ref[pl.ds(0, width, stride=8), :]
    for k in range(1, 8):
        total = total + sums_ref[pl.ds(k, width, stride=8), :]
    norm = 1.0 / math.sqrt(70.0)
    factor = jnp.where(iota((width, 1), 0) < 3 * columns, norm, 0.5 * norm)
    terms = total * (factor * volume_ref[...])
    slot = jnp.broadcast_to(slot_ref[...].astype(jnp.float32), (128 - width, elems))
    payload = jnp.concatenate([terms, slot], axis=0).astype(jnp.bfloat16)
    out_ref[...] = dot(sends_ref[...], payload, NT).astype(jnp.bfloat16)


def voxel_kernel(width, got_ref, out_ref):
    got = got_ref[...]
    slot = got[:, width : width + 1].astype(jnp.int32)
    voxels = out_ref.shape[1]
    members = one_hot(slot == iota((got.shape[0], voxels), 1))
    out_ref[...] = dot(got, members, TN)[:width]


def per_device(
    traces, solver, mass, dom_lists, sub_lists, elem_face, volume, elem_owner, elem_slot
):
    n_dom, n_sub = lax.axis_size("dom"), lax.axis_size("sub")
    owners = n_dom * n_sub
    columns, faces = traces.shape[3:]
    rows = dom_lists.shape[1]
    elems = elem_face.shape[1]
    capacity = max(2, 3 * elems // owners)
    width = 6 * columns
    table = traces.reshape(-1, faces)
    values = table.shape[0]
    params = pltpu.CompilerParams(vmem_limit_bytes=VMEM_LIMIT)

    vmem = pl.BlockSpec(memory_space=pltpu.VMEM)
    hbm = pl.BlockSpec(memory_space=pltpu.HBM)

    def in_hbm(*arrays):
        return [pltpu.with_memory_space_constraint(x, pltpu.HBM) for x in arrays]

    table, sub, *packed = pl.pallas_call(
        lambda *refs: pack_kernel(n_sub, rows, *refs),
        in_specs=[hbm] * 3,
        out_shape=[pltpu.VMEM(x.shape, x.dtype) for x in (table, sub_lists)]
        + [pltpu.VMEM((rows, values), jnp.bfloat16)] * (n_sub + 1),
        out_specs=[vmem] * (n_sub + 3),
        scratch_shapes=[
            pltpu.VMEM(dom_lists.shape, jnp.int32),
            pltpu.SemaphoreType.DMA((3,)),
        ],
        compiler_params=params,
        name="pack",
    )(*in_hbm(table, dom_lists, sub_lists))

    n_rhs = lax.axis_size("rhs")
    halos = []
    for odd, part in enumerate(packed[:2]):
        pairs = []
        for d in range(n_dom):
            other = d + 1 if (d - odd) % 2 == 0 else d - 1
            inside = 0 <= other < n_dom
            for s in range(n_sub):
                for c in range(n_rhs):
                    target = (other * n_sub + s) * n_rhs + c
                    if not inside:
                        target = (d * n_sub + s) * n_rhs + n_rhs - 1 - c
                    pairs.append(((d * n_sub + s) * n_rhs + c, target))
        halos.append(lax.ppermute(part, ("dom", "sub", "rhs"), pairs))
    for k in range(1, n_sub):
        pairs = [(i, pair_index(i, k, n_sub)[0]) for i in range(n_sub)]
        halos.append(lax.ppermute(packed[1 + k], "sub", [(i, int(j)) for i, j in pairs]))

    slots = owners * capacity
    tiles = -(-(n_sub + 1) // (128 // rows - 1))
    matrix = solver[0].transpose(1, 0, 2)
    fixed = pl.pallas_call(
        lambda *refs: prepare_kernel(n_sub, capacity, columns, *refs),
        in_specs=[vmem] * 2 + [hbm] * N_SMALL,
        out_shape=[
            pltpu.VMEM((8, BLOCK, 4 * elems), jnp.bfloat16),
            pltpu.VMEM((4 * tiles, elems), jnp.int32),
            pltpu.VMEM((2, ROWS, BLOCK), jnp.bfloat16),
            pltpu.VMEM((slots, elems), jnp.bfloat16),
            pltpu.VMEM((1, elems), jnp.float32),
            pltpu.VMEM((1, elems), jnp.int32),
        ],
        out_specs=[vmem] * 6,
        scratch_shapes=[
            pltpu.VMEM(matrix.shape, jnp.bfloat16),
            pltpu.VMEM(mass.shape[1:], jnp.bfloat16),
            pltpu.VMEM((4, elems), jnp.int32),
            pltpu.VMEM((1, elems), jnp.int32),
            pltpu.VMEM((8, BLOCK, faces), jnp.bfloat16),
            pltpu.SemaphoreType.DMA((N_SMALL,)),
        ],
        compiler_params=params,
        cost_estimate=pl.CostEstimate(
            flops=8 * BLOCK * faces * 8 * elems, bytes_accessed=4 << 20, transcendentals=0
        ),
        name="prepare",
    )(
        sub,
        table,
        *in_hbm(
            elem_face,
            elem_owner.reshape(1, elems),
            matrix,
            mass[0],
            volume.reshape(1, elems),
            elem_slot.reshape(1, elems),
        ),
    )
    sent = pl.pallas_call(
        lambda *refs: element_kernel(columns, *refs),
        out_shape=jax.ShapeDtypeStruct((slots, 128), jnp.bfloat16),
        scratch_shapes=[
            pltpu.VMEM((8, columns, BLOCK // columns, 4 * elems), jnp.bfloat16),
            pltpu.VMEM((8 * width, elems), jnp.float32),
        ],
        compiler_params=params,
        name="elements",
    )(*fixed, *[halos[i] for i in halo_order(n_sub)])
    got = lax.all_to_all(sent, ("dom", "sub"), split_axis=0, concat_axis=0, tiled=True)
    summed = pl.pallas_call(
        lambda *refs: voxel_kernel(width, *refs),
        out_shape=jax.ShapeDtypeStruct((width, elems), jnp.float32),
        compiler_params=params,
        name="voxels",
    )(got)
    return summed.reshape(6, columns, elems)


def solution(mesh):
    return jax.shard_map(
        per_device,
        mesh=mesh,
        in_specs=(
            P(None, None, None, "rhs", ("groups", "dom", "sub")),
            P("groups", None, None, None),
            P(),
            P(None, ("dom", "sub")),
            P(None, ("dom", "sub")),
            P(None, ("dom", "sub")),
            P(("dom", "sub")),
            P(("dom", "sub"), None),
            P(("dom", "sub")),
        ),
        out_specs=P(None, "rhs", ("groups", "dom", "sub")),
        check_vma=False,
    )
```

```python
import itertools
import math

import jax
import jax.numpy as jnp
from jax import lax
from jax.experimental import pallas as pl
from jax.experimental.pallas import tpu as pltpu
from jax.sharding import PartitionSpec as P

BASIS = 35
HALF = 3 * BASIS
NODES = 30
BLOCK = 256
N_SMALL = 6
FULL = 32
ROWS = 216
PADDED = 112
VMEM_LIMIT = 24 * 1024 * 1024

NT = (((1,), (1,)), ((), ()))
NN = (((1,), (0,)), ((), ()))
TN = (((0,), (0,)), ((), ()))


def dot(a, b, dims=NN):
    return lax.dot_general(a, b, dims, preferred_element_type=jnp.float32)


def iota(shape, axis):
    return lax.broadcasted_iota(jnp.int32, shape, axis)


def one_hot(condition):
    return jnp.where(condition, 1.0, 0.0).astype(jnp.bfloat16)


def pair_index(index, k, size):
    if size & (size - 1) == 0:
        return index ^ k, index ^ k
    return lax.rem(index + k, size), lax.rem(index + size - k, size)


def swapped(messages):
    first = lax.axis_index("rhs") == 0
    one, two = messages[1], messages[2]
    return [messages[0], jnp.where(first, one, two), jnp.where(first, two, one)] + messages[3:]


def pack_kernel(n_sub, rows, traces_hbm, dom_hbm, sub_hbm, table_ref, sub_ref, *refs):
    out_refs, (dom_ref, sems) = refs[: n_sub + 1], refs[n_sub + 1 :]
    faces = table_ref.shape[1]
    pairs = [(dom_hbm, dom_ref), (sub_hbm, sub_ref), (traces_hbm, table_ref)]
    copies = [pltpu.make_async_copy(*pair, sems.at[i]) for i, pair in enumerate(pairs)]
    for copy in copies:
        copy.start()
    for copy in copies[:2]:
        copy.wait()
    parity = lax.rem(lax.axis_index("dom"), 2)
    within = lax.axis_index("sub")
    lists = [dom_ref[pl.ds(parity, 1), :], dom_ref[pl.ds(1 - parity, 1), :]]
    for k in range(1, n_sub):
        lists.append(sub_ref[pl.ds(pair_index(within, k, n_sub)[0], 1), :])
    lists = swapped(lists)
    face = iota((faces, rows), 0)
    picks = [jnp.where(face == row, 1.0, 0.0).T for row in lists]
    picks = jnp.concatenate(picks, axis=0).astype(jnp.bfloat16)
    copies[2].wait()
    packed = dot(picks, table_ref[...], NT).astype(jnp.bfloat16)
    for i, out_ref in enumerate(out_refs):
        out_ref[...] = packed[i * rows : (i + 1) * rows]


def reorder_matrix(columns):
    per_block = BLOCK // columns
    row = iota((BLOCK, BLOCK), 0)
    col = iota((BLOCK, BLOCK), 1)
    return one_hot(lax.rem(row, per_block) * columns + lax.div(row, per_block) == col)


def block_starts(columns):
    half = 2 * NODES * columns
    return [a * half - (a * half) % 128 + b * BLOCK for a in range(2) for b in range(4)]


def row_group(row):
    tail = row - 6 * FULL
    within = lax.rem(tail, 8)
    late = BASIS - FULL
    head = row < 6 * FULL
    group = jnp.where(head, lax.div(row, FULL), lax.div(within, late) * 3 + lax.div(tail, 8))
    basis = jnp.where(head, lax.rem(row, FULL), FULL + lax.rem(within, late))
    used = head | (within < 2 * late)
    return jnp.where(used, group, -1), basis


def prepare_kernel(n_sub, capacity, columns, sub_ref, table_ref, *refs):
    hbm_refs, refs = refs[:N_SMALL], refs[N_SMALL:]
    own_ref, places_ref, matrix_ref, sends_ref, volume_ref, slot_ref = refs[:6]
    solver_ref, mass_ref, elem_ref, owner_ref, mine_ref, sems = refs[6:]
    vmem_refs = [elem_ref, owner_ref, solver_ref, mass_ref, volume_ref, slot_ref]
    copies = [
        pltpu.make_async_copy(hbm_refs[i], vmem_refs[i], sems.at[i]) for i in range(N_SMALL)
    ]
    for copy in copies:
        copy.start()
    faces = table_ref.shape[1]
    elems = elem_ref.shape[1]
    rows = sub_ref.shape[1]
    slots = sends_ref.shape[0]
    parity = lax.rem(lax.axis_index("dom"), 2)
    within = lax.axis_index("sub")

    reorder = reorder_matrix(columns)
    for b, start in enumerate(block_starts(columns)):
        mine = dot(reorder, table_ref[start : start + BLOCK, :])
        mine_ref[b] = mine.astype(jnp.bfloat16)
    own_list = sub_ref[pl.ds(within, 1), :]
    square = iota((rows, rows), 0) == iota((rows, rows), 1)
    own_list = jnp.sum(jnp.where(square, own_list, 0), axis=1, keepdims=True)
    half = 2 * NODES * columns
    source = iota((4 * NODES, BLOCK), 0)
    place = iota((4 * NODES, BLOCK), 1)
    target = lax.div(source, NODES) * 64 + lax.rem(source, NODES)
    spots = []
    for a in range(2):
        first = target + ((a * half) % 128) // columns
        spots += [one_hot(first == place), one_hot(first + NODES == place)]
    spots = jnp.concatenate(spots, axis=1)
    group, basis = row_group(iota((ROWS, 1), 0))
    column = iota((1, 2 * PADDED), 1)
    field = lax.rem(column, PADDED)
    column_group = lax.div(column, PADDED) * 3 + lax.div(field, BASIS)
    column_basis = lax.rem(field, BASIS)
    same = (group == column_group) & (field < HALF)
    spread = one_hot(same & (basis == column_basis))
    sign = jnp.where(same, jnp.where(column < PADDED, 1.0, -1.0), 0.0)
    tall = one_hot(basis == iota((ROWS, BASIS), 1))
    wide = one_hot(iota((BASIS, 2 * PADDED), 0) == column_basis)
    earlier = one_hot(iota((elems, elems), 0) < iota((elems, elems), 1))
    for copy in copies:
        copy.wait()

    elem_face = elem_ref[...]
    offset = elem_face - (faces + (2 + within) * rows)
    own = []
    for f in range(4):
        found = jnp.where(iota((rows, elems), 0) == offset[f : f + 1, :], own_list, 0)
        found = jnp.sum(found, axis=0, keepdims=True)
        inside = (offset[f : f + 1, :] >= 0) & (offset[f : f + 1, :] < rows)
        index = jnp.where(inside, found, elem_face[f : f + 1, :])
        own.append(one_hot(iota((faces, elems), 0) == index))
    own = jnp.concatenate(own, axis=1)
    for b in range(8):
        own_ref[b] = dot(mine_ref[b], own).astype(jnp.bfloat16)
    blocks = [parity, 1 - parity]
    for k in range(1, n_sub):
        blocks.append(2 + pair_index(within, k, n_sub)[1])
    blocks = swapped(blocks)
    per_tile = 128 // rows - 1
    for t in range(places_ref.shape[0] // 4):
        lane = jnp.full(elem_face.shape, 127, jnp.int32)
        for i, block in enumerate(blocks[t * per_tile : (t + 1) * per_tile]):
            offset = elem_face - (faces + block * rows)
            lane = jnp.where((offset >= 0) & (offset < rows), offset + i * rows, lane)
        places_ref[4 * t : 4 * t + 4, :] = lane

    solver = solver_ref[:PADDED].astype(jnp.float32)
    solver = jnp.concatenate([solver[:, 0, :], solver[:, 1, :]], axis=0).astype(jnp.bfloat16)
    placed = dot(solver, spots)
    masses = dot(dot(tall, mass_ref[...]).astype(jnp.bfloat16), wide) * sign
    spreads = [masses.astype(jnp.bfloat16), spread]
    for a in range(2):
        first, second = (placed[:, (2 * a + i) * BLOCK : (2 * a + i + 1) * BLOCK] for i in range(2))
        top = first[:PADDED] - second[PADDED:]
        bottom = first[PADDED:] + second[:PADDED]
        both = jnp.concatenate([top, bottom], axis=0).astype(jnp.bfloat16)
        matrix_ref[a] = dot(spreads[a], both).astype(jnp.bfloat16)

    owner = owner_ref[...]
    owners = iota((max(8, slots // capacity), elems), 0) == owner
    counts = dot(one_hot(owners), earlier)
    rank = jnp.sum(jnp.where(owners, counts, 0.0), axis=0, keepdims=True)
    target = owner * capacity + rank.astype(jnp.int32)
    sends_ref[...] = one_hot(iota((slots, elems), 0) == target)


def element_kernel(
    columns,
    own_ref,
    places_ref,
    matrix_ref,
    sends_ref,
    volume_ref,
    slot_ref,
    *refs,
):
    halo_refs, (out_ref, gathered_ref, sums_ref) = refs[:-3], refs[-3:]
    elems = volume_ref.shape[1]
    per_block = BLOCK // columns
    tiles = places_ref.shape[0] // 4
    reorder = reorder_matrix(columns)
    rows, values = halo_refs[0].shape
    per_tile = 128 // rows - 1
    tables = []
    for t in range(tiles):
        parts = [ref[...] for ref in halo_refs[t * per_tile : (t + 1) * per_tile]]
        parts.append(jnp.zeros((128 - rows * len(parts), values), jnp.bfloat16))
        tables.append(jnp.concatenate(parts, axis=0))
    lanes = [jnp.broadcast_to(places_ref[i : i + 1, :], (BLOCK, elems)) for i in range(4 * tiles)]
    starts = block_starts(columns)

    def gather(b):
        part = slice(starts[b], starts[b] + BLOCK)
        others = [dot(reorder, table[:, part], NT) for table in tables]
        for f in range(4):
            part = slice(f * elems, (f + 1) * elems)
            got = own_ref[b, :, part]
            for t in range(tiles):
                found = jnp.take_along_axis(
                    others[t], lanes[4 * t + f], axis=1, mode="promise_in_bounds"
                )
                got = got + found.astype(jnp.bfloat16)
            gathered_ref[b, :, :, part] = got.reshape(columns, per_block, elems)

    def fields(a, index):
        parts = []
        for c in range(2):
            taken = [gathered_ref[a * 4 + b, 2 * index + c] for b in range(4)]
            parts.append(
                jnp.concatenate(
                    [taken[b][:, f * elems : (f + 1) * elems] for f in range(4) for b in range(4)],
                    axis=0,
                )
            )
        return dot(matrix_ref[a], jnp.concatenate(parts, axis=1))

    for b in range(8):
        gather(b)

    pairs = [(0, 0), (1, 1), (2, 2), (0, 1), (0, 2), (1, 2)]
    split = 6 * FULL
    shape = (2, 3, FULL // 8, 8, 2 * elems)
    tail = (3, 8, 2 * elems)
    for index in range(columns // 2):
        weighted = fields(0, index)
        adjoint = fields(1, index).astype(jnp.bfloat16).astype(jnp.float32)
        weighted, weighted_tail = weighted[:split].reshape(shape), weighted[split:].reshape(tail)
        adjoint, adjoint_tail = adjoint[:split].reshape(shape), adjoint[split:].reshape(tail)
        for m, (i, j) in enumerate(pairs):
            products = adjoint[:, i] * weighted[:, j]
            rest = adjoint_tail[i] * weighted_tail[j]
            if i != j:
                products = products + adjoint[:, j] * weighted[:, i]
                rest = rest + adjoint_tail[j] * weighted_tail[i]
            total = jnp.sum(products, axis=(0, 1)) + rest
            for c in range(2):
                start = (m * columns + 2 * index + c) * 8
                sums_ref[start : start + 8, :] = total[:, c * elems : (c + 1) * elems]

    width = 6 * columns
    total = sums_ref[pl.ds(0, width, stride=8), :]
    for k in range(1, 8):
        total = total + sums_ref[pl.ds(k, width, stride=8), :]
    norm = 1.0 / math.sqrt(70.0)
    factor = jnp.where(iota((width, 1), 0) < 3 * columns, norm, 0.5 * norm)
    terms = total * (factor * volume_ref[...])
    slot = jnp.broadcast_to(slot_ref[...].astype(jnp.float32), (128 - width, elems))
    payload = jnp.concatenate([terms, slot], axis=0).astype(jnp.bfloat16)
    out_ref[...] = dot(sends_ref[...], payload, NT).astype(jnp.bfloat16)


def voxel_kernel(width, got_ref, out_ref):
    got = got_ref[...]
    slot = got[:, width : width + 1].astype(jnp.int32)
    voxels = out_ref.shape[1]
    members = one_hot(slot == iota((got.shape[0], voxels), 1))
    out_ref[...] = dot(got, members, TN)[:width]


def per_device(
    traces, solver, mass, dom_lists, sub_lists, elem_face, volume, elem_owner, elem_slot
):
    n_dom, n_sub = lax.axis_size("dom"), lax.axis_size("sub")
    owners = n_dom * n_sub
    columns, faces = traces.shape[3:]
    rows = dom_lists.shape[1]
    elems = elem_face.shape[1]
    capacity = max(2, 3 * elems // owners)
    width = 6 * columns
    table = traces.reshape(-1, faces)
    values = table.shape[0]
    params = pltpu.CompilerParams(vmem_limit_bytes=VMEM_LIMIT)

    vmem = pl.BlockSpec(memory_space=pltpu.VMEM)
    hbm = pl.BlockSpec(memory_space=pltpu.HBM)

    def in_hbm(*arrays):
        return [pltpu.with_memory_space_constraint(x, pltpu.HBM) for x in arrays]

    table, sub, *packed = pl.pallas_call(
        lambda *refs: pack_kernel(n_sub, rows, *refs),
        in_specs=[hbm] * 3,
        out_shape=[pltpu.VMEM(x.shape, x.dtype) for x in (table, sub_lists)]
        + [pltpu.VMEM((rows, values), jnp.bfloat16)] * (n_sub + 1),
        out_specs=[vmem] * (n_sub + 3),
        scratch_shapes=[
            pltpu.VMEM(dom_lists.shape, jnp.int32),
            pltpu.SemaphoreType.DMA((3,)),
        ],
        compiler_params=params,
        name="pack",
    )(*in_hbm(table, dom_lists, sub_lists))

    n_rhs = lax.axis_size("rhs")

    def partner(message, d, s, c):
        if message < 2:
            other = d + 1 if (d + message) % 2 else d - 1
            if 0 <= other < n_dom:
                return other, s, c
            return d, s, n_rhs - 1 - c
        return d, int(pair_index(s, message - 1, n_sub)[0]), c

    halos = []
    for k, part in enumerate(packed):
        pairs = []
        for d, s, c in itertools.product(range(n_dom), range(n_sub), range(n_rhs)):
            message = 3 - k if c and k in (1, 2) else k
            to_d, to_s, to_c = partner(message, d, s, c)
            pairs.append(((d * n_sub + s) * n_rhs + c, (to_d * n_sub + to_s) * n_rhs + to_c))
        halos.append(lax.ppermute(part, ("dom", "sub", "rhs"), pairs))
    slots = owners * capacity
    tiles = -(-(n_sub + 1) // (128 // rows - 1))
    matrix = solver[0].transpose(1, 0, 2)
    fixed = pl.pallas_call(
        lambda *refs: prepare_kernel(n_sub, capacity, columns, *refs),
        in_specs=[vmem] * 2 + [hbm] * N_SMALL,
        out_shape=[
            pltpu.VMEM((8, BLOCK, 4 * elems), jnp.bfloat16),
            pltpu.VMEM((4 * tiles, elems), jnp.int32),
            pltpu.VMEM((2, ROWS, BLOCK), jnp.bfloat16),
            pltpu.VMEM((slots, elems), jnp.bfloat16),
            pltpu.VMEM((1, elems), jnp.float32),
            pltpu.VMEM((1, elems), jnp.int32),
        ],
        out_specs=[vmem] * 6,
        scratch_shapes=[
            pltpu.VMEM(matrix.shape, jnp.bfloat16),
            pltpu.VMEM(mass.shape[1:], jnp.bfloat16),
            pltpu.VMEM((4, elems), jnp.int32),
            pltpu.VMEM((1, elems), jnp.int32),
            pltpu.VMEM((8, BLOCK, faces), jnp.bfloat16),
            pltpu.SemaphoreType.DMA((N_SMALL,)),
        ],
        compiler_params=params,
        cost_estimate=pl.CostEstimate(
            flops=8 * BLOCK * faces * 8 * elems, bytes_accessed=4 << 20, transcendentals=0
        ),
        name="prepare",
    )(
        sub,
        table,
        *in_hbm(
            elem_face,
            elem_owner.reshape(1, elems),
            matrix,
            mass[0],
            volume.reshape(1, elems),
            elem_slot.reshape(1, elems),
        ),
    )
    sent = pl.pallas_call(
        lambda *refs: element_kernel(columns, *refs),
        out_shape=jax.ShapeDtypeStruct((slots, 128), jnp.bfloat16),
        scratch_shapes=[
            pltpu.VMEM((8, columns, BLOCK // columns, 4 * elems), jnp.bfloat16),
            pltpu.VMEM((8 * width + 8, elems), jnp.float32),
        ],
        compiler_params=params,
        name="elements",
    )(*fixed, *halos)
    got = lax.all_to_all(sent, ("dom", "sub"), split_axis=0, concat_axis=0, tiled=True)
    summed = pl.pallas_call(
        lambda *refs: voxel_kernel(width, *refs),
        out_shape=jax.ShapeDtypeStruct((width, elems), jnp.float32),
        compiler_params=params,
        name="voxels",
    )(got)
    return summed.reshape(6, columns, elems)


def solution(mesh):
    return jax.shard_map(
        per_device,
        mesh=mesh,
        in_specs=(
            P(None, None, None, "rhs", ("groups", "dom", "sub")),
            P("groups", None, None, None),
            P(),
            P(None, ("dom", "sub")),
            P(None, ("dom", "sub")),
            P(None, ("dom", "sub")),
            P(("dom", "sub")),
            P(("dom", "sub"), None),
            P(("dom", "sub")),
        ),
        out_specs=P(None, "rhs", ("groups", "dom", "sub")),
        check_vma=False,
    )
```

```python
import itertools
import math

import jax
import jax.numpy as jnp
from jax import lax
from jax.experimental import pallas as pl
from jax.experimental.pallas import tpu as pltpu
from jax.sharding import PartitionSpec as P

BASIS = 35
HALF = 3 * BASIS
NODES = 30
BLOCK = 256
N_SMALL = 6
FULL = 32
ROWS = 216
PADDED = 112
VMEM_LIMIT = 24 * 1024 * 1024

NT = (((1,), (1,)), ((), ()))
NN = (((1,), (0,)), ((), ()))
TN = (((0,), (0,)), ((), ()))


def dot(a, b, dims=NN):
    return lax.dot_general(a, b, dims, preferred_element_type=jnp.float32)


def iota(shape, axis):
    return lax.broadcasted_iota(jnp.int32, shape, axis)


def one_hot(condition):
    return jnp.where(condition, 1.0, 0.0).astype(jnp.bfloat16)


def pair_index(index, k, size):
    if size & (size - 1) == 0:
        return index ^ k, index ^ k
    return lax.rem(index + k, size), lax.rem(index + size - k, size)


def swapped(messages):
    first = lax.axis_index("rhs") == 0
    one, two = messages[1], messages[2]
    return [messages[0], jnp.where(first, one, two), jnp.where(first, two, one)] + messages[3:]


def pack_kernel(n_sub, rows, traces_hbm, dom_hbm, sub_hbm, table_ref, sub_ref, *refs):
    out_refs, (dom_ref, sems) = refs[: n_sub + 1], refs[n_sub + 1 :]
    faces = table_ref.shape[1]
    pairs = [(dom_hbm, dom_ref), (sub_hbm, sub_ref), (traces_hbm, table_ref)]
    copies = [pltpu.make_async_copy(*pair, sems.at[i]) for i, pair in enumerate(pairs)]
    for i in (2, 0, 1):
        copies[i].start()
    for copy in copies[:2]:
        copy.wait()
    parity = lax.rem(lax.axis_index("dom"), 2)
    within = lax.axis_index("sub")
    lists = [dom_ref[pl.ds(parity, 1), :], dom_ref[pl.ds(1 - parity, 1), :]]
    for k in range(1, n_sub):
        lists.append(sub_ref[pl.ds(pair_index(within, k, n_sub)[0], 1), :])
    lists = swapped(lists)
    face = iota((faces, rows), 0)
    picks = [jnp.where(face == row, 1.0, 0.0).T for row in lists]
    picks = jnp.concatenate(picks, axis=0).astype(jnp.bfloat16)
    copies[2].wait()
    packed = dot(picks, table_ref[...], NT).astype(jnp.bfloat16)
    for i, out_ref in enumerate(out_refs):
        out_ref[...] = packed[i * rows : (i + 1) * rows]


def reorder_matrix(columns):
    per_block = BLOCK // columns
    row = iota((BLOCK, BLOCK), 0)
    col = iota((BLOCK, BLOCK), 1)
    return one_hot(lax.rem(row, per_block) * columns + lax.div(row, per_block) == col)


def block_starts(columns):
    half = 2 * NODES * columns
    return [a * half - (a * half) % 128 + b * BLOCK for a in range(2) for b in range(4)]


def row_group(row):
    tail = row - 6 * FULL
    within = lax.rem(tail, 8)
    late = BASIS - FULL
    head = row < 6 * FULL
    group = jnp.where(head, lax.div(row, FULL), lax.div(within, late) * 3 + lax.div(tail, 8))
    basis = jnp.where(head, lax.rem(row, FULL), FULL + lax.rem(within, late))
    used = head | (within < 2 * late)
    return jnp.where(used, group, -1), basis


def prepare_kernel(n_sub, capacity, columns, sub_ref, table_ref, *refs):
    hbm_refs, refs = refs[:N_SMALL], refs[N_SMALL:]
    own_ref, places_ref, matrix_ref, sends_ref, volume_ref, slot_ref = refs[:6]
    solver_ref, mass_ref, elem_ref, owner_ref, mine_ref, sems = refs[6:]
    vmem_refs = [elem_ref, owner_ref, solver_ref, mass_ref, volume_ref, slot_ref]
    copies = [
        pltpu.make_async_copy(hbm_refs[i], vmem_refs[i], sems.at[i]) for i in range(N_SMALL)
    ]
    for copy in copies:
        copy.start()
    faces = table_ref.shape[1]
    elems = elem_ref.shape[1]
    rows = sub_ref.shape[1]
    slots = sends_ref.shape[0]
    parity = lax.rem(lax.axis_index("dom"), 2)
    within = lax.axis_index("sub")

    reorder = reorder_matrix(columns)
    for b, start in enumerate(block_starts(columns)):
        mine = dot(reorder, table_ref[start : start + BLOCK, :])
        mine_ref[b] = mine.astype(jnp.bfloat16)
    own_list = sub_ref[pl.ds(within, 1), :]
    square = iota((rows, rows), 0) == iota((rows, rows), 1)
    own_list = jnp.sum(jnp.where(square, own_list, 0), axis=1, keepdims=True)
    half = 2 * NODES * columns
    source = iota((4 * NODES, BLOCK), 0)
    place = iota((4 * NODES, BLOCK), 1)
    target = lax.div(source, NODES) * 64 + lax.rem(source, NODES)
    spots = []
    for a in range(2):
        first = target + ((a * half) % 128) // columns
        spots += [one_hot(first == place), one_hot(first + NODES == place)]
    spots = jnp.concatenate(spots, axis=1)
    group, basis = row_group(iota((ROWS, 1), 0))
    column = iota((1, 2 * PADDED), 1)
    field = lax.rem(column, PADDED)
    column_group = lax.div(column, PADDED) * 3 + lax.div(field, BASIS)
    column_basis = lax.rem(field, BASIS)
    same = (group == column_group) & (field < HALF)
    spread = one_hot(same & (basis == column_basis))
    sign = jnp.where(same, jnp.where(column < PADDED, 1.0, -1.0), 0.0)
    tall = one_hot(basis == iota((ROWS, BASIS), 1))
    wide = one_hot(iota((BASIS, 2 * PADDED), 0) == column_basis)
    earlier = one_hot(iota((elems, elems), 0) < iota((elems, elems), 1))
    for copy in copies:
        copy.wait()

    elem_face = elem_ref[...]
    offset = elem_face - (faces + (2 + within) * rows)
    own = []
    for f in range(4):
        found = jnp.where(iota((rows, elems), 0) == offset[f : f + 1, :], own_list, 0)
        found = jnp.sum(found, axis=0, keepdims=True)
        inside = (offset[f : f + 1, :] >= 0) & (offset[f : f + 1, :] < rows)
        index = jnp.where(inside, found, elem_face[f : f + 1, :])
        own.append(one_hot(iota((faces, elems), 0) == index))
    own = jnp.concatenate(own, axis=1)
    mine = mine_ref[...].reshape(8 * BLOCK, faces)
    own_ref[...] = dot(mine, own).astype(jnp.bfloat16).reshape(own_ref.shape)
    blocks = [parity, 1 - parity]
    for k in range(1, n_sub):
        blocks.append(2 + pair_index(within, k, n_sub)[1])
    blocks = swapped(blocks)
    per_tile = 128 // rows - 1
    for t in range(places_ref.shape[0] // 4):
        lane = jnp.full(elem_face.shape, 127, jnp.int32)
        for i, block in enumerate(blocks[t * per_tile : (t + 1) * per_tile]):
            offset = elem_face - (faces + block * rows)
            lane = jnp.where((offset >= 0) & (offset < rows), offset + i * rows, lane)
        places_ref[4 * t : 4 * t + 4, :] = lane

    solver = solver_ref[:PADDED].astype(jnp.float32)
    solver = jnp.concatenate([solver[:, 0, :], solver[:, 1, :]], axis=0).astype(jnp.bfloat16)
    placed = dot(solver, spots)
    masses = dot(dot(tall, mass_ref[...]).astype(jnp.bfloat16), wide) * sign
    spreads = [masses.astype(jnp.bfloat16), spread]
    for a in range(2):
        first, second = (placed[:, (2 * a + i) * BLOCK : (2 * a + i + 1) * BLOCK] for i in range(2))
        top = first[:PADDED] - second[PADDED:]
        bottom = first[PADDED:] + second[:PADDED]
        both = jnp.concatenate([top, bottom], axis=0).astype(jnp.bfloat16)
        matrix_ref[a] = dot(spreads[a], both).astype(jnp.bfloat16)

    owner = owner_ref[...]
    owners = iota((max(8, slots // capacity), elems), 0) == owner
    counts = dot(one_hot(owners), earlier)
    rank = jnp.sum(jnp.where(owners, counts, 0.0), axis=0, keepdims=True)
    target = owner * capacity + rank.astype(jnp.int32)
    sends_ref[...] = one_hot(iota((slots, elems), 0) == target)


def element_kernel(
    columns,
    own_ref,
    places_ref,
    matrix_ref,
    sends_ref,
    volume_ref,
    slot_ref,
    *refs,
):
    halo_refs, (out_ref, gathered_ref, sums_ref) = refs[:-3], refs[-3:]
    elems = volume_ref.shape[1]
    per_block = BLOCK // columns
    tiles = places_ref.shape[0] // 4
    reorder = reorder_matrix(columns)
    rows, values = halo_refs[0].shape
    per_tile = 128 // rows - 1
    tables = []
    for t in range(tiles):
        parts = [ref[...] for ref in halo_refs[t * per_tile : (t + 1) * per_tile]]
        parts.append(jnp.zeros((128 - rows * len(parts), values), jnp.bfloat16))
        tables.append(jnp.concatenate(parts, axis=0))
    starts = block_starts(columns)
    found = 0.0
    others = []
    for t in range(tiles):
        blocks = []
        for b in range(0, 8, 2):
            pair = [tables[t][:, start : start + BLOCK] for start in starts[b : b + 2]]
            pair = dot(reorder, jnp.concatenate(pair, axis=0), NT)
            blocks += [pair[:, :128], pair[:, 128:]]
        others.append(blocks)
        hot = [
            one_hot(iota((128, elems), 0) == places_ref[i : i + 1, :])
            for i in range(4 * t, 4 * t + 3)
        ]
        stacked = jnp.concatenate([x.astype(jnp.bfloat16) for x in blocks], axis=0)
        found = found + dot(stacked, jnp.concatenate(hot, axis=1))
    found = found.astype(jnp.bfloat16)
    lanes = [
        jnp.broadcast_to(places_ref[4 * t + 3 : 4 * t + 4, :], (BLOCK, elems))
        for t in range(tiles)
    ]
    for b in range(8):
        part = slice(0, 3 * elems)
        got = own_ref[b, :, part] + found[b * BLOCK : (b + 1) * BLOCK]
        gathered_ref[b, :, :, part] = got.reshape(columns, per_block, 3 * elems)
        part = slice(3 * elems, 4 * elems)
        got = own_ref[b, :, part]
        for t in range(tiles):
            last = jnp.take_along_axis(
                others[t][b], lanes[t], axis=1, mode="promise_in_bounds"
            )
            got = got + last.astype(jnp.bfloat16)
        gathered_ref[b, :, :, part] = got.reshape(columns, per_block, elems)

    def fields(a, index):
        parts = []
        for c in range(2):
            taken = [gathered_ref[a * 4 + b, 2 * index + c] for b in range(4)]
            parts.append(
                jnp.concatenate(
                    [taken[b][:, f * elems : (f + 1) * elems] for f in range(4) for b in range(4)],
                    axis=0,
                )
            )
        return dot(matrix_ref[a], jnp.concatenate(parts, axis=1))

    pairs = [(0, 0), (1, 1), (2, 2), (0, 1), (0, 2), (1, 2)]
    split = 6 * FULL
    shape = (2, 3, FULL // 8, 8, 2 * elems)
    tail = (3, 8, 2 * elems)
    for index in range(columns // 2):
        weighted = fields(0, index)
        adjoint = fields(1, index).astype(jnp.bfloat16).astype(jnp.float32)
        weighted, weighted_tail = weighted[:split].reshape(shape), weighted[split:].reshape(tail)
        adjoint, adjoint_tail = adjoint[:split].reshape(shape), adjoint[split:].reshape(tail)
        for m, (i, j) in enumerate(pairs):
            products = adjoint[:, i] * weighted[:, j]
            rest = adjoint_tail[i] * weighted_tail[j]
            if i != j:
                products = products + adjoint[:, j] * weighted[:, i]
                rest = rest + adjoint_tail[j] * weighted_tail[i]
            total = jnp.sum(products, axis=(0, 1)) + rest
            for c in range(2):
                start = (m * columns + 2 * index + c) * 8
                sums_ref[start : start + 8, :] = total[:, c * elems : (c + 1) * elems]

    width = 6 * columns
    total = sums_ref[pl.ds(0, width, stride=8), :]
    for k in range(1, 8):
        total = total + sums_ref[pl.ds(k, width, stride=8), :]
    norm = 1.0 / math.sqrt(70.0)
    factor = jnp.where(iota((width, 1), 0) < 3 * columns, norm, 0.5 * norm)
    terms = total * (factor * volume_ref[...])
    slot = jnp.broadcast_to(slot_ref[...].astype(jnp.float32), (128 - width, elems))
    payload = jnp.concatenate([terms, slot], axis=0).astype(jnp.bfloat16)
    out_ref[...] = dot(sends_ref[...], payload, NT).astype(jnp.bfloat16)


def voxel_kernel(width, got_ref, out_ref):
    got = got_ref[...]
    slot = got[:, width : width + 1].astype(jnp.float32)
    voxels = out_ref.shape[1]
    members = one_hot(slot == iota((got.shape[0], voxels), 1).astype(jnp.float32))
    out_ref[...] = dot(got, members, TN)[:width]


def per_device(
    traces, solver, mass, dom_lists, sub_lists, elem_face, volume, elem_owner, elem_slot
):
    n_dom, n_sub = lax.axis_size("dom"), lax.axis_size("sub")
    owners = n_dom * n_sub
    columns, faces = traces.shape[3:]
    rows = dom_lists.shape[1]
    elems = elem_face.shape[1]
    capacity = max(2, 3 * elems // owners)
    width = 6 * columns
    table = traces.reshape(-1, faces)
    values = table.shape[0]
    params = pltpu.CompilerParams(vmem_limit_bytes=VMEM_LIMIT)

    vmem = pl.BlockSpec(memory_space=pltpu.VMEM)
    hbm = pl.BlockSpec(memory_space=pltpu.HBM)

    def in_hbm(*arrays):
        return [pltpu.with_memory_space_constraint(x, pltpu.HBM) for x in arrays]

    table, sub, *packed = pl.pallas_call(
        lambda *refs: pack_kernel(n_sub, rows, *refs),
        in_specs=[hbm] * 3,
        out_shape=[pltpu.VMEM(x.shape, x.dtype) for x in (table, sub_lists)]
        + [pltpu.VMEM((rows, values), jnp.bfloat16)] * (n_sub + 1),
        out_specs=[vmem] * (n_sub + 3),
        scratch_shapes=[
            pltpu.VMEM(dom_lists.shape, jnp.int32),
            pltpu.SemaphoreType.DMA((3,)),
        ],
        compiler_params=params,
        name="pack",
    )(*in_hbm(table, dom_lists, sub_lists))

    n_rhs = lax.axis_size("rhs")

    def partner(message, d, s, c):
        if message < 2:
            other = d + 1 if (d + message) % 2 else d - 1
            if 0 <= other < n_dom:
                return other, s, c
            return d, s, n_rhs - 1 - c
        return d, int(pair_index(s, message - 1, n_sub)[0]), c

    halos = []
    for k, part in enumerate(packed):
        pairs = []
        for d, s, c in itertools.product(range(n_dom), range(n_sub), range(n_rhs)):
            message = 3 - k if c and k in (1, 2) else k
            to_d, to_s, to_c = partner(message, d, s, c)
            pairs.append(((d * n_sub + s) * n_rhs + c, (to_d * n_sub + to_s) * n_rhs + to_c))
        halos.append(lax.ppermute(part, ("dom", "sub", "rhs"), pairs))
    slots = owners * capacity
    tiles = -(-(n_sub + 1) // (128 // rows - 1))
    matrix = solver[0].transpose(1, 0, 2)
    fixed = pl.pallas_call(
        lambda *refs: prepare_kernel(n_sub, capacity, columns, *refs),
        in_specs=[vmem] * 2 + [hbm] * N_SMALL,
        out_shape=[
            pltpu.VMEM((8, BLOCK, 4 * elems), jnp.bfloat16),
            pltpu.VMEM((4 * tiles, elems), jnp.int32),
            pltpu.VMEM((2, ROWS, BLOCK), jnp.bfloat16),
            pltpu.VMEM((slots, elems), jnp.bfloat16),
            pltpu.VMEM((1, elems), jnp.float32),
            pltpu.VMEM((1, elems), jnp.int32),
        ],
        out_specs=[vmem] * 6,
        scratch_shapes=[
            pltpu.VMEM(matrix.shape, jnp.bfloat16),
            pltpu.VMEM(mass.shape[1:], jnp.bfloat16),
            pltpu.VMEM((4, elems), jnp.int32),
            pltpu.VMEM((1, elems), jnp.int32),
            pltpu.VMEM((8, BLOCK, faces), jnp.bfloat16),
            pltpu.SemaphoreType.DMA((N_SMALL,)),
        ],
        compiler_params=params,
        cost_estimate=pl.CostEstimate(
            flops=8 * BLOCK * faces * 8 * elems, bytes_accessed=4 << 20, transcendentals=0
        ),
        name="prepare",
    )(
        sub,
        table,
        *in_hbm(
            elem_face,
            elem_owner.reshape(1, elems),
            matrix,
            mass[0],
            volume.reshape(1, elems),
            elem_slot.reshape(1, elems),
        ),
    )
    sent = pl.pallas_call(
        lambda *refs: element_kernel(columns, *refs),
        out_shape=jax.ShapeDtypeStruct((slots, 128), jnp.bfloat16),
        scratch_shapes=[
            pltpu.VMEM((8, columns, BLOCK // columns, 4 * elems), jnp.bfloat16),
            pltpu.VMEM((8 * width + 8, elems), jnp.float32),
        ],
        compiler_params=params,
        name="elements",
    )(*fixed, *halos)
    got = lax.all_to_all(sent, ("dom", "sub"), split_axis=0, concat_axis=0, tiled=True)
    summed = pl.pallas_call(
        lambda *refs: voxel_kernel(width, *refs),
        out_shape=jax.ShapeDtypeStruct((width, elems), jnp.float32),
        compiler_params=params,
        name="voxels",
    )(got)
    return summed.reshape(6, columns, elems)


def solution(mesh):
    return jax.shard_map(
        per_device,
        mesh=mesh,
        in_specs=(
            P(None, None, None, "rhs", ("groups", "dom", "sub")),
            P("groups", None, None, None),
            P(),
            P(None, ("dom", "sub")),
            P(None, ("dom", "sub")),
            P(None, ("dom", "sub")),
            P(("dom", "sub")),
            P(("dom", "sub"), None),
            P(("dom", "sub")),
        ),
        out_specs=P(None, "rhs", ("groups", "dom", "sub")),
        check_vma=False,
    )
```

```python
import itertools
import math

import jax
import jax.numpy as jnp
from jax import lax
from jax.experimental import pallas as pl
from jax.experimental.pallas import tpu as pltpu
from jax.sharding import PartitionSpec as P

BASIS = 35
HALF = 3 * BASIS
NODES = 30
BLOCK = 256
N_SMALL = 6
FULL = 32
ROWS = 216
PADDED = 112
VMEM_LIMIT = 24 * 1024 * 1024

NT = (((1,), (1,)), ((), ()))
NN = (((1,), (0,)), ((), ()))
TN = (((0,), (0,)), ((), ()))


def dot(a, b, dims=NN):
    return lax.dot_general(a, b, dims, preferred_element_type=jnp.float32)


def iota(shape, axis):
    return lax.broadcasted_iota(jnp.int32, shape, axis)


def one_hot(condition):
    return jnp.where(condition, 1.0, 0.0).astype(jnp.bfloat16)


def pair_index(index, k, size):
    if size & (size - 1) == 0:
        return index ^ k, index ^ k
    return lax.rem(index + k, size), lax.rem(index + size - k, size)


def swapped(messages):
    first = lax.axis_index("rhs") == 0
    even, slab = messages[1], messages[2]
    return [messages[0], jnp.where(first, slab, even), jnp.where(first, even, slab)] + messages[3:]


def pack_kernel(n_sub, rows, traces_hbm, dom_hbm, sub_hbm, table_ref, sub_ref, *refs):
    out_refs, (dom_ref, sems) = refs[: n_sub + 1], refs[n_sub + 1 :]
    faces = table_ref.shape[1]
    pairs = [(dom_hbm, dom_ref), (sub_hbm, sub_ref), (traces_hbm, table_ref)]
    copies = [pltpu.make_async_copy(*pair, sems.at[i]) for i, pair in enumerate(pairs)]
    for i in (2, 0, 1):
        copies[i].start()
    for copy in copies[:2]:
        copy.wait()
    parity = lax.rem(lax.axis_index("dom"), 2)
    within = lax.axis_index("sub")
    lists = [dom_ref[pl.ds(parity, 1), :], dom_ref[pl.ds(1 - parity, 1), :]]
    for k in range(1, n_sub):
        lists.append(sub_ref[pl.ds(pair_index(within, k, n_sub)[0], 1), :])
    lists = swapped(lists)
    face = iota((faces, rows), 0)
    picks = [jnp.where(face == row, 1.0, 0.0).T for row in lists]
    picks = jnp.concatenate(picks, axis=0).astype(jnp.bfloat16)
    copies[2].wait()
    packed = dot(picks, table_ref[...], NT).astype(jnp.bfloat16)
    for i, out_ref in enumerate(out_refs):
        out_ref[...] = packed[i * rows : (i + 1) * rows]


def reorder_matrix(columns):
    per_block = BLOCK // columns
    row = iota((BLOCK, BLOCK), 0)
    col = iota((BLOCK, BLOCK), 1)
    return one_hot(lax.rem(row, per_block) * columns + lax.div(row, per_block) == col)


def block_starts(columns):
    half = 2 * NODES * columns
    return [a * half - (a * half) % 128 + b * BLOCK for a in range(2) for b in range(4)]


def row_group(row):
    tail = row - 6 * FULL
    within = lax.rem(tail, 8)
    late = BASIS - FULL
    head = row < 6 * FULL
    group = jnp.where(head, lax.div(row, FULL), lax.div(within, late) * 3 + lax.div(tail, 8))
    basis = jnp.where(head, lax.rem(row, FULL), FULL + lax.rem(within, late))
    used = head | (within < 2 * late)
    return jnp.where(used, group, -1), basis


def prepare_kernel(n_sub, capacity, columns, sub_ref, table_ref, *refs):
    hbm_refs, refs = refs[:N_SMALL], refs[N_SMALL:]
    own_ref, places_ref, matrix_ref, sends_ref, volume_ref, slot_ref = refs[:6]
    solver_ref, mass_ref, elem_ref, owner_ref, mine_ref, sems = refs[6:]
    vmem_refs = [elem_ref, owner_ref, solver_ref, mass_ref, volume_ref, slot_ref]
    copies = [
        pltpu.make_async_copy(hbm_refs[i], vmem_refs[i], sems.at[i]) for i in range(N_SMALL)
    ]
    for copy in copies:
        copy.start()
    faces = table_ref.shape[1]
    elems = elem_ref.shape[1]
    rows = sub_ref.shape[1]
    slots = sends_ref.shape[0]
    parity = lax.rem(lax.axis_index("dom"), 2)
    within = lax.axis_index("sub")

    reorder = reorder_matrix(columns)
    for b, start in enumerate(block_starts(columns)):
        mine = dot(reorder, table_ref[start : start + BLOCK, :])
        mine_ref[b] = mine.astype(jnp.bfloat16)
    own_list = sub_ref[pl.ds(within, 1), :]
    square = iota((rows, rows), 0) == iota((rows, rows), 1)
    own_list = jnp.sum(jnp.where(square, own_list, 0), axis=1, keepdims=True)
    half = 2 * NODES * columns
    source = iota((4 * NODES, BLOCK), 0)
    place = iota((4 * NODES, BLOCK), 1)
    target = lax.div(source, NODES) * 64 + lax.rem(source, NODES)
    spots = []
    for a in range(2):
        first = target + ((a * half) % 128) // columns
        spots += [one_hot(first == place), one_hot(first + NODES == place)]
    spots = jnp.concatenate(spots, axis=1)
    group, basis = row_group(iota((ROWS, 1), 0))
    column = iota((1, 2 * PADDED), 1)
    field = lax.rem(column, PADDED)
    column_group = lax.div(column, PADDED) * 3 + lax.div(field, BASIS)
    column_basis = lax.rem(field, BASIS)
    same = (group == column_group) & (field < HALF)
    spread = one_hot(same & (basis == column_basis))
    sign = jnp.where(same, jnp.where(column < PADDED, 1.0, -1.0), 0.0)
    tall = one_hot(basis == iota((ROWS, BASIS), 1))
    wide = one_hot(iota((BASIS, 2 * PADDED), 0) == column_basis)
    earlier = one_hot(iota((elems, elems), 0) < iota((elems, elems), 1))
    for copy in copies:
        copy.wait()

    elem_face = elem_ref[...]
    offset = elem_face - (faces + (2 + within) * rows)
    own = []
    for f in range(4):
        found = jnp.where(iota((rows, elems), 0) == offset[f : f + 1, :], own_list, 0)
        found = jnp.sum(found, axis=0, keepdims=True)
        inside = (offset[f : f + 1, :] >= 0) & (offset[f : f + 1, :] < rows)
        index = jnp.where(inside, found, elem_face[f : f + 1, :])
        own.append(one_hot(iota((faces, elems), 0) == index))
    own = jnp.concatenate(own, axis=1)
    mine = mine_ref[...].reshape(8 * BLOCK, faces)
    own_ref[...] = dot(mine, own).astype(jnp.bfloat16).reshape(own_ref.shape)
    blocks = [parity, 1 - parity]
    for k in range(1, n_sub):
        blocks.append(2 + pair_index(within, k, n_sub)[1])
    blocks = swapped(blocks)
    per_tile = 128 // rows - 1
    for t in range(places_ref.shape[0] // 4):
        lane = jnp.full(elem_face.shape, 127, jnp.int32)
        for i, block in enumerate(blocks[t * per_tile : (t + 1) * per_tile]):
            offset = elem_face - (faces + block * rows)
            lane = jnp.where((offset >= 0) & (offset < rows), offset + i * rows, lane)
        places_ref[4 * t : 4 * t + 4, :] = lane

    solver = solver_ref[:PADDED].astype(jnp.float32)
    solver = jnp.concatenate([solver[:, 0, :], solver[:, 1, :]], axis=0).astype(jnp.bfloat16)
    placed = dot(solver, spots)
    masses = dot(dot(tall, mass_ref[...]).astype(jnp.bfloat16), wide) * sign
    spreads = [masses.astype(jnp.bfloat16), spread]
    for a in range(2):
        first, second = (placed[:, (2 * a + i) * BLOCK : (2 * a + i + 1) * BLOCK] for i in range(2))
        top = first[:PADDED] - second[PADDED:]
        bottom = first[PADDED:] + second[:PADDED]
        both = jnp.concatenate([top, bottom], axis=0).astype(jnp.bfloat16)
        matrix_ref[a] = dot(spreads[a], both).astype(jnp.bfloat16)

    owner = owner_ref[...]
    owners = iota((max(8, slots // capacity), elems), 0) == owner
    counts = dot(one_hot(owners), earlier)
    rank = jnp.sum(jnp.where(owners, counts, 0.0), axis=0, keepdims=True)
    target = owner * capacity + rank.astype(jnp.int32)
    sends_ref[...] = one_hot(iota((slots, elems), 0) == target)


def element_kernel(
    columns,
    own_ref,
    places_ref,
    matrix_ref,
    sends_ref,
    volume_ref,
    slot_ref,
    *refs,
):
    halo_refs, (out_ref, gathered_ref, sums_ref) = refs[:-3], refs[-3:]
    elems = volume_ref.shape[1]
    per_block = BLOCK // columns
    tiles = places_ref.shape[0] // 4
    reorder = reorder_matrix(columns)
    rows, values = halo_refs[0].shape
    per_tile = 128 // rows - 1
    tables = []
    for t in range(tiles):
        parts = [ref[...] for ref in halo_refs[t * per_tile : (t + 1) * per_tile]]
        parts.append(jnp.zeros((128 - rows * len(parts), values), jnp.bfloat16))
        tables.append(jnp.concatenate(parts, axis=0))
    starts = block_starts(columns)
    found = 0.0
    others = []
    for t in range(tiles):
        blocks = []
        for b in range(0, 8, 2):
            pair = [tables[t][:, start : start + BLOCK] for start in starts[b : b + 2]]
            pair = dot(reorder, jnp.concatenate(pair, axis=0), NT)
            blocks += [pair[:, :128], pair[:, 128:]]
        others.append(blocks)
        hot = [
            one_hot(iota((128, elems), 0) == places_ref[i : i + 1, :])
            for i in range(4 * t, 4 * t + 3)
        ]
        stacked = jnp.concatenate([x.astype(jnp.bfloat16) for x in blocks], axis=0)
        found = found + dot(stacked, jnp.concatenate(hot, axis=1))
    found = found.astype(jnp.bfloat16)
    lanes = [
        jnp.broadcast_to(places_ref[4 * t + 3 : 4 * t + 4, :], (BLOCK, elems))
        for t in range(tiles)
    ]
    for b in range(8):
        part = slice(0, 3 * elems)
        got = own_ref[b, :, part] + found[b * BLOCK : (b + 1) * BLOCK]
        gathered_ref[b, :, :, part] = got.reshape(columns, per_block, 3 * elems)
        part = slice(3 * elems, 4 * elems)
        got = own_ref[b, :, part]
        for t in range(tiles):
            last = jnp.take_along_axis(
                others[t][b], lanes[t], axis=1, mode="promise_in_bounds"
            )
            got = got + last.astype(jnp.bfloat16)
        gathered_ref[b, :, :, part] = got.reshape(columns, per_block, elems)

    def fields(a, index):
        parts = []
        for c in range(2):
            taken = [gathered_ref[a * 4 + b, 2 * index + c] for b in range(4)]
            parts.append(
                jnp.concatenate(
                    [taken[b][:, f * elems : (f + 1) * elems] for f in range(4) for b in range(4)],
                    axis=0,
                )
            )
        return dot(matrix_ref[a], jnp.concatenate(parts, axis=1))

    pairs = [(0, 0), (1, 1), (2, 2), (0, 1), (0, 2), (1, 2)]
    split = 6 * FULL
    shape = (2, 3, FULL // 8, 8, 2 * elems)
    tail = (3, 8, 2 * elems)
    for index in range(columns // 2):
        weighted = fields(0, index)
        adjoint = fields(1, index).astype(jnp.bfloat16).astype(jnp.float32)
        weighted, weighted_tail = weighted[:split].reshape(shape), weighted[split:].reshape(tail)
        adjoint, adjoint_tail = adjoint[:split].reshape(shape), adjoint[split:].reshape(tail)
        for m, (i, j) in enumerate(pairs):
            products = adjoint[:, i] * weighted[:, j]
            rest = adjoint_tail[i] * weighted_tail[j]
            if i != j:
                products = products + adjoint[:, j] * weighted[:, i]
                rest = rest + adjoint_tail[j] * weighted_tail[i]
            total = jnp.sum(products, axis=(0, 1)) + rest
            for c in range(2):
                start = (m * columns + 2 * index + c) * 8
                sums_ref[start : start + 8, :] = total[:, c * elems : (c + 1) * elems]

    width = 6 * columns
    total = sums_ref[pl.ds(0, width, stride=8), :]
    for k in range(1, 8):
        total = total + sums_ref[pl.ds(k, width, stride=8), :]
    norm = 1.0 / math.sqrt(70.0)
    factor = jnp.where(iota((width, 1), 0) < 3 * columns, norm, 0.5 * norm)
    terms = total * (factor * volume_ref[...])
    slot = jnp.broadcast_to(slot_ref[...].astype(jnp.float32), (128 - width, elems))
    payload = jnp.concatenate([terms, slot], axis=0).astype(jnp.bfloat16)
    out_ref[...] = dot(sends_ref[...], payload, NT).astype(jnp.bfloat16)


def voxel_kernel(width, got_ref, out_ref):
    got = got_ref[...]
    slot = got[:, width : width + 1].astype(jnp.float32)
    voxels = out_ref.shape[1]
    members = one_hot(slot == iota((got.shape[0], voxels), 1).astype(jnp.float32))
    out_ref[...] = dot(got, members, TN)[:width]


def per_device(
    traces, solver, mass, dom_lists, sub_lists, elem_face, volume, elem_owner, elem_slot
):
    n_dom, n_sub = lax.axis_size("dom"), lax.axis_size("sub")
    owners = n_dom * n_sub
    columns, faces = traces.shape[3:]
    rows = dom_lists.shape[1]
    elems = elem_face.shape[1]
    capacity = max(2, 3 * elems // owners)
    width = 6 * columns
    table = traces.reshape(-1, faces)
    values = table.shape[0]
    params = pltpu.CompilerParams(vmem_limit_bytes=VMEM_LIMIT)

    vmem = pl.BlockSpec(memory_space=pltpu.VMEM)
    hbm = pl.BlockSpec(memory_space=pltpu.HBM)

    def in_hbm(*arrays):
        return [pltpu.with_memory_space_constraint(x, pltpu.HBM) for x in arrays]

    table, sub, *packed = pl.pallas_call(
        lambda *refs: pack_kernel(n_sub, rows, *refs),
        in_specs=[hbm] * 3,
        out_shape=[pltpu.VMEM(x.shape, x.dtype) for x in (table, sub_lists)]
        + [pltpu.VMEM((rows, values), jnp.bfloat16)] * (n_sub + 1),
        out_specs=[vmem] * (n_sub + 3),
        scratch_shapes=[
            pltpu.VMEM(dom_lists.shape, jnp.int32),
            pltpu.SemaphoreType.DMA((3,)),
        ],
        compiler_params=params,
        name="pack",
    )(*in_hbm(table, dom_lists, sub_lists))

    n_rhs = lax.axis_size("rhs")

    def partner(message, d, s, c):
        if message < 2:
            other = d + 1 if (d + message) % 2 else d - 1
            if 0 <= other < n_dom:
                return other, s, c
            return d, s, n_rhs - 1 - c
        return d, int(pair_index(s, message - 1, n_sub)[0]), c

    halos = []
    for k, part in enumerate(packed):
        pairs = []
        for d, s, c in itertools.product(range(n_dom), range(n_sub), range(n_rhs)):
            message = 3 - k if c == 0 and k in (1, 2) else k
            to_d, to_s, to_c = partner(message, d, s, c)
            pairs.append(((d * n_sub + s) * n_rhs + c, (to_d * n_sub + to_s) * n_rhs + to_c))
        halos.append(lax.ppermute(part, ("dom", "sub", "rhs"), pairs))
    slots = owners * capacity
    tiles = -(-(n_sub + 1) // (128 // rows - 1))
    matrix = solver[0].transpose(1, 0, 2)
    fixed = pl.pallas_call(
        lambda *refs: prepare_kernel(n_sub, capacity, columns, *refs),
        in_specs=[vmem] * 2 + [hbm] * N_SMALL,
        out_shape=[
            pltpu.VMEM((8, BLOCK, 4 * elems), jnp.bfloat16),
            pltpu.VMEM((4 * tiles, elems), jnp.int32),
            pltpu.VMEM((2, ROWS, BLOCK), jnp.bfloat16),
            pltpu.VMEM((slots, elems), jnp.bfloat16),
            pltpu.VMEM((1, elems), jnp.float32),
            pltpu.VMEM((1, elems), jnp.int32),
        ],
        out_specs=[vmem] * 6,
        scratch_shapes=[
            pltpu.VMEM(matrix.shape, jnp.bfloat16),
            pltpu.VMEM(mass.shape[1:], jnp.bfloat16),
            pltpu.VMEM((4, elems), jnp.int32),
            pltpu.VMEM((1, elems), jnp.int32),
            pltpu.VMEM((8, BLOCK, faces), jnp.bfloat16),
            pltpu.SemaphoreType.DMA((N_SMALL,)),
        ],
        compiler_params=params,
        cost_estimate=pl.CostEstimate(
            flops=8 * BLOCK * faces * 8 * elems, bytes_accessed=4 << 20, transcendentals=0
        ),
        name="prepare",
    )(
        sub,
        table,
        *in_hbm(
            elem_face,
            elem_owner.reshape(1, elems),
            matrix,
            mass[0],
            volume.reshape(1, elems),
            elem_slot.reshape(1, elems),
        ),
    )
    sent = pl.pallas_call(
        lambda *refs: element_kernel(columns, *refs),
        out_shape=jax.ShapeDtypeStruct((slots, 128), jnp.bfloat16),
        scratch_shapes=[
            pltpu.VMEM((8, columns, BLOCK // columns, 4 * elems), jnp.bfloat16),
            pltpu.VMEM((8 * width + 8, elems), jnp.float32),
        ],
        compiler_params=params,
        name="elements",
    )(*fixed, *halos)
    got = lax.all_to_all(sent, ("dom", "sub"), split_axis=0, concat_axis=0, tiled=True)
    summed = pl.pallas_call(
        lambda *refs: voxel_kernel(width, *refs),
        out_shape=jax.ShapeDtypeStruct((width, elems), jnp.float32),
        compiler_params=params,
        name="voxels",
    )(got)
    return summed.reshape(6, columns, elems)


def solution(mesh):
    return jax.shard_map(
        per_device,
        mesh=mesh,
        in_specs=(
            P(None, None, None, "rhs", ("groups", "dom", "sub")),
            P("groups", None, None, None),
            P(),
            P(None, ("dom", "sub")),
            P(None, ("dom", "sub")),
            P(None, ("dom", "sub")),
            P(("dom", "sub")),
            P(("dom", "sub"), None),
            P(("dom", "sub")),
        ),
        out_specs=P(None, "rhs", ("groups", "dom", "sub")),
        check_vma=False,
    )
```

```python
import itertools
import math

import jax
import jax.numpy as jnp
from jax import lax
from jax.experimental import pallas as pl
from jax.experimental.pallas import tpu as pltpu
from jax.sharding import PartitionSpec as P

BASIS = 35
HALF = 3 * BASIS
NODES = 30
BLOCK = 256
N_SMALL = 6
FULL = 32
ROWS = 216
PADDED = 112
VMEM_LIMIT = 24 * 1024 * 1024

NT = (((1,), (1,)), ((), ()))
NN = (((1,), (0,)), ((), ()))
TN = (((0,), (0,)), ((), ()))


def dot(a, b, dims=NN):
    return lax.dot_general(a, b, dims, preferred_element_type=jnp.float32)


def iota(shape, axis):
    return lax.broadcasted_iota(jnp.int32, shape, axis)


def one_hot(condition):
    return jnp.where(condition, 1.0, 0.0).astype(jnp.bfloat16)


def pair_index(index, k, size):
    if size & (size - 1) == 0:
        return index ^ k, index ^ k
    return lax.rem(index + k, size), lax.rem(index + size - k, size)


def swapped(messages):
    first = lax.axis_index("rhs") == 0
    even, slab = messages[1], messages[2]
    return [messages[0], jnp.where(first, slab, even), jnp.where(first, even, slab)] + messages[3:]


def pack_kernel(n_sub, rows, traces_hbm, dom_hbm, sub_hbm, table_ref, sub_ref, *refs):
    out_refs, (dom_ref, sems) = refs[: n_sub + 1], refs[n_sub + 1 :]
    faces = table_ref.shape[1]
    pairs = [(dom_hbm, dom_ref), (sub_hbm, sub_ref), (traces_hbm, table_ref)]
    copies = [pltpu.make_async_copy(*pair, sems.at[i]) for i, pair in enumerate(pairs)]
    for i in (2, 0, 1):
        copies[i].start()
    for copy in copies[:2]:
        copy.wait()
    parity = lax.rem(lax.axis_index("dom"), 2)
    within = lax.axis_index("sub")
    lists = [dom_ref[pl.ds(parity, 1), :], dom_ref[pl.ds(1 - parity, 1), :]]
    for k in range(1, n_sub):
        lists.append(sub_ref[pl.ds(pair_index(within, k, n_sub)[0], 1), :])
    lists = swapped(lists)
    face = iota((faces, rows), 0)
    picks = [jnp.where(face == row, 1.0, 0.0).T for row in lists]
    picks = jnp.concatenate(picks, axis=0).astype(jnp.bfloat16)
    copies[2].wait()
    packed = dot(picks, table_ref[...], NT).astype(jnp.bfloat16)
    for i, out_ref in enumerate(out_refs):
        out_ref[...] = packed[i * rows : (i + 1) * rows]


def reorder_matrix(columns):
    per_block = BLOCK // columns
    row = iota((BLOCK, BLOCK), 0)
    col = iota((BLOCK, BLOCK), 1)
    return one_hot(lax.rem(row, per_block) * columns + lax.div(row, per_block) == col)


def block_starts(columns):
    half = 2 * NODES * columns
    return [a * half - (a * half) % 128 + b * BLOCK for a in range(2) for b in range(4)]


def row_group(row):
    tail = row - 6 * FULL
    within = lax.rem(tail, 8)
    late = BASIS - FULL
    head = row < 6 * FULL
    group = jnp.where(head, lax.div(row, FULL), lax.div(within, late) * 3 + lax.div(tail, 8))
    basis = jnp.where(head, lax.rem(row, FULL), FULL + lax.rem(within, late))
    used = head | (within < 2 * late)
    return jnp.where(used, group, -1), basis


def prepare_kernel(n_sub, capacity, columns, sub_ref, table_ref, *refs):
    hbm_refs, refs = refs[:N_SMALL], refs[N_SMALL:]
    own_ref, places_ref, matrix_ref, sends_ref, reorder_ref, hot_ref, scale_ref, slot_ref = refs[:8]
    solver_ref, mass_ref, elem_ref, owner_ref, volume_ref, mine_ref, sems = refs[8:]
    vmem_refs = [elem_ref, owner_ref, solver_ref, mass_ref, volume_ref, slot_ref]
    copies = [
        pltpu.make_async_copy(hbm_refs[i], vmem_refs[i], sems.at[i]) for i in range(N_SMALL)
    ]
    for copy in copies:
        copy.start()
    faces = table_ref.shape[1]
    elems = elem_ref.shape[1]
    rows = sub_ref.shape[1]
    slots = sends_ref.shape[0]
    parity = lax.rem(lax.axis_index("dom"), 2)
    within = lax.axis_index("sub")

    reorder = reorder_matrix(columns)
    reorder_ref[...] = reorder
    for b, start in enumerate(block_starts(columns)):
        mine = dot(reorder, table_ref[start : start + BLOCK, :])
        mine_ref[b] = mine.astype(jnp.bfloat16)
    own_list = sub_ref[pl.ds(within, 1), :]
    square = iota((rows, rows), 0) == iota((rows, rows), 1)
    own_list = jnp.sum(jnp.where(square, own_list, 0), axis=1, keepdims=True)
    half = 2 * NODES * columns
    source = iota((4 * NODES, BLOCK), 0)
    place = iota((4 * NODES, BLOCK), 1)
    target = lax.div(source, NODES) * 64 + lax.rem(source, NODES)
    spots = []
    for a in range(2):
        first = target + ((a * half) % 128) // columns
        spots += [one_hot(first == place), one_hot(first + NODES == place)]
    spots = jnp.concatenate(spots, axis=1)
    group, basis = row_group(iota((ROWS, 1), 0))
    column = iota((1, 2 * PADDED), 1)
    field = lax.rem(column, PADDED)
    column_group = lax.div(column, PADDED) * 3 + lax.div(field, BASIS)
    column_basis = lax.rem(field, BASIS)
    same = (group == column_group) & (field < HALF)
    spread = one_hot(same & (basis == column_basis))
    sign = jnp.where(same, jnp.where(column < PADDED, 1.0, -1.0), 0.0)
    tall = one_hot(basis == iota((ROWS, BASIS), 1))
    wide = one_hot(iota((BASIS, 2 * PADDED), 0) == column_basis)
    earlier = one_hot(iota((elems, elems), 0) < iota((elems, elems), 1))
    for copy in copies:
        copy.wait()

    elem_face = elem_ref[...]
    offset = elem_face - (faces + (2 + within) * rows)
    own = []
    for f in range(4):
        found = jnp.where(iota((rows, elems), 0) == offset[f : f + 1, :], own_list, 0)
        found = jnp.sum(found, axis=0, keepdims=True)
        inside = (offset[f : f + 1, :] >= 0) & (offset[f : f + 1, :] < rows)
        index = jnp.where(inside, found, elem_face[f : f + 1, :])
        own.append(one_hot(iota((faces, elems), 0) == index))
    own = jnp.concatenate(own, axis=1)
    mine = mine_ref[...].reshape(8 * BLOCK, faces)
    own_ref[...] = dot(mine, own).astype(jnp.bfloat16).reshape(own_ref.shape)
    blocks = [parity, 1 - parity]
    for k in range(1, n_sub):
        blocks.append(2 + pair_index(within, k, n_sub)[1])
    blocks = swapped(blocks)
    per_tile = 128 // rows - 1
    for t in range(places_ref.shape[0] // 4):
        lane = jnp.full(elem_face.shape, 127, jnp.int32)
        for i, block in enumerate(blocks[t * per_tile : (t + 1) * per_tile]):
            offset = elem_face - (faces + block * rows)
            lane = jnp.where((offset >= 0) & (offset < rows), offset + i * rows, lane)
        places_ref[4 * t : 4 * t + 4, :] = lane
        hot = [one_hot(iota((128, elems), 0) == lane[f : f + 1, :]) for f in range(3)]
        hot_ref[t] = jnp.concatenate(hot, axis=1)

    solver = solver_ref[:PADDED].astype(jnp.float32)
    solver = jnp.concatenate([solver[:, 0, :], solver[:, 1, :]], axis=0).astype(jnp.bfloat16)
    placed = dot(solver, spots)
    masses = dot(dot(tall, mass_ref[...]).astype(jnp.bfloat16), wide) * sign
    spreads = [masses.astype(jnp.bfloat16), spread]
    for a in range(2):
        first, second = (placed[:, (2 * a + i) * BLOCK : (2 * a + i + 1) * BLOCK] for i in range(2))
        top = first[:PADDED] - second[PADDED:]
        bottom = first[PADDED:] + second[:PADDED]
        both = jnp.concatenate([top, bottom], axis=0).astype(jnp.bfloat16)
        matrix_ref[a] = dot(spreads[a], both).astype(jnp.bfloat16)

    owner = owner_ref[...]
    owners = iota((max(8, slots // capacity), elems), 0) == owner
    counts = dot(one_hot(owners), earlier)
    rank = jnp.sum(jnp.where(owners, counts, 0.0), axis=0, keepdims=True)
    target = owner * capacity + rank.astype(jnp.int32)
    sends_ref[...] = one_hot(iota((slots, elems), 0) == target)

    width = 6 * columns
    norm = 1.0 / math.sqrt(70.0)
    factor = jnp.where(iota((width, 1), 0) < 3 * columns, norm, 0.5 * norm)
    scale_ref[...] = factor * volume_ref[...]


def element_kernel(
    columns,
    own_ref,
    places_ref,
    matrix_ref,
    sends_ref,
    reorder_ref,
    hot_ref,
    scale_ref,
    slot_ref,
    *refs,
):
    halo_refs, (out_ref, gathered_ref, sums_ref) = refs[:-3], refs[-3:]
    elems = scale_ref.shape[1]
    per_block = BLOCK // columns
    tiles = places_ref.shape[0] // 4
    reorder = reorder_ref[...]
    rows, values = halo_refs[0].shape
    per_tile = 128 // rows - 1
    tables = []
    for t in range(tiles):
        parts = [ref[...] for ref in halo_refs[t * per_tile : (t + 1) * per_tile]]
        parts.append(jnp.zeros((128 - rows * len(parts), values), jnp.bfloat16))
        tables.append(jnp.concatenate(parts, axis=0))
    starts = block_starts(columns)
    found = 0.0
    others = []
    for t in range(tiles):
        blocks = []
        for b in range(0, 8, 2):
            pair = [tables[t][:, start : start + BLOCK] for start in starts[b : b + 2]]
            pair = dot(reorder, jnp.concatenate(pair, axis=0), NT)
            blocks += [pair[:, :128], pair[:, 128:]]
        others.append(blocks)
        stacked = jnp.concatenate([x.astype(jnp.bfloat16) for x in blocks], axis=0)
        found = found + dot(stacked, hot_ref[t])
    found = found.astype(jnp.bfloat16)
    lanes = [
        jnp.broadcast_to(places_ref[4 * t + 3 : 4 * t + 4, :], (BLOCK, elems))
        for t in range(tiles)
    ]
    for b in range(8):
        part = slice(0, 3 * elems)
        got = own_ref[b, :, part] + found[b * BLOCK : (b + 1) * BLOCK]
        gathered_ref[b, :, :, part] = got.reshape(columns, per_block, 3 * elems)
        part = slice(3 * elems, 4 * elems)
        got = own_ref[b, :, part]
        for t in range(tiles):
            last = jnp.take_along_axis(
                others[t][b], lanes[t], axis=1, mode="promise_in_bounds"
            )
            got = got + last.astype(jnp.bfloat16)
        gathered_ref[b, :, :, part] = got.reshape(columns, per_block, elems)

    def fields(a, index):
        parts = []
        for c in range(2):
            taken = [gathered_ref[a * 4 + b, 2 * index + c] for b in range(4)]
            parts.append(
                jnp.concatenate(
                    [taken[b][:, f * elems : (f + 1) * elems] for f in range(4) for b in range(4)],
                    axis=0,
                )
            )
        return dot(matrix_ref[a], jnp.concatenate(parts, axis=1))

    pairs = [(0, 0), (1, 1), (2, 2), (0, 1), (0, 2), (1, 2)]
    split = 6 * FULL
    shape = (2, 3, FULL // 8, 8, 2 * elems)
    tail = (3, 8, 2 * elems)
    for index in range(columns // 2):
        weighted = fields(0, index)
        adjoint = fields(1, index).astype(jnp.bfloat16).astype(jnp.float32)
        weighted, weighted_tail = weighted[:split].reshape(shape), weighted[split:].reshape(tail)
        adjoint, adjoint_tail = adjoint[:split].reshape(shape), adjoint[split:].reshape(tail)
        for m, (i, j) in enumerate(pairs):
            products = adjoint[:, i] * weighted[:, j]
            rest = adjoint_tail[i] * weighted_tail[j]
            if i != j:
                products = products + adjoint[:, j] * weighted[:, i]
                rest = rest + adjoint_tail[j] * weighted_tail[i]
            total = jnp.sum(products, axis=(0, 1)) + rest
            for c in range(2):
                start = (m * columns + 2 * index + c) * 8
                sums_ref[start : start + 8, :] = total[:, c * elems : (c + 1) * elems]

    width = 6 * columns
    total = sums_ref[pl.ds(0, width, stride=8), :]
    for k in range(1, 8):
        total = total + sums_ref[pl.ds(k, width, stride=8), :]
    terms = total * scale_ref[...]
    slot = jnp.broadcast_to(slot_ref[...].astype(jnp.float32), (128 - width, elems))
    payload = jnp.concatenate([terms, slot], axis=0).astype(jnp.bfloat16)
    out_ref[...] = dot(sends_ref[...], payload, NT).astype(jnp.bfloat16)


def voxel_kernel(width, got_ref, out_ref):
    got = got_ref[...]
    slot = got[:, width : width + 1].astype(jnp.float32)
    voxels = out_ref.shape[1]
    members = one_hot(slot == iota((got.shape[0], voxels), 1).astype(jnp.float32))
    out_ref[...] = dot(got, members, TN)[:width]


def per_device(
    traces, solver, mass, dom_lists, sub_lists, elem_face, volume, elem_owner, elem_slot
):
    n_dom, n_sub = lax.axis_size("dom"), lax.axis_size("sub")
    owners = n_dom * n_sub
    columns, faces = traces.shape[3:]
    rows = dom_lists.shape[1]
    elems = elem_face.shape[1]
    capacity = max(2, 3 * elems // owners)
    width = 6 * columns
    table = traces.reshape(-1, faces)
    values = table.shape[0]
    params = pltpu.CompilerParams(vmem_limit_bytes=VMEM_LIMIT)

    vmem = pl.BlockSpec(memory_space=pltpu.VMEM)
    hbm = pl.BlockSpec(memory_space=pltpu.HBM)

    def in_hbm(*arrays):
        return [pltpu.with_memory_space_constraint(x, pltpu.HBM) for x in arrays]

    table, sub, *packed = pl.pallas_call(
        lambda *refs: pack_kernel(n_sub, rows, *refs),
        in_specs=[hbm] * 3,
        out_shape=[pltpu.VMEM(x.shape, x.dtype) for x in (table, sub_lists)]
        + [pltpu.VMEM((rows, values), jnp.bfloat16)] * (n_sub + 1),
        out_specs=[vmem] * (n_sub + 3),
        scratch_shapes=[
            pltpu.VMEM(dom_lists.shape, jnp.int32),
            pltpu.SemaphoreType.DMA((3,)),
        ],
        compiler_params=params,
        name="pack",
    )(*in_hbm(table, dom_lists, sub_lists))

    n_rhs = lax.axis_size("rhs")

    def partner(message, d, s, c):
        if message < 2:
            other = d + 1 if (d + message) % 2 else d - 1
            if 0 <= other < n_dom:
                return other, s, c
            return d, s, n_rhs - 1 - c
        return d, int(pair_index(s, message - 1, n_sub)[0]), c

    halos = []
    for k, part in enumerate(packed):
        pairs = []
        for d, s, c in itertools.product(range(n_dom), range(n_sub), range(n_rhs)):
            message = 3 - k if c == 0 and k in (1, 2) else k
            to_d, to_s, to_c = partner(message, d, s, c)
            pairs.append(((d * n_sub + s) * n_rhs + c, (to_d * n_sub + to_s) * n_rhs + to_c))
        halos.append(lax.ppermute(part, ("dom", "sub", "rhs"), pairs))
    slots = owners * capacity
    tiles = -(-(n_sub + 1) // (128 // rows - 1))
    matrix = solver[0].transpose(1, 0, 2)
    fixed = pl.pallas_call(
        lambda *refs: prepare_kernel(n_sub, capacity, columns, *refs),
        in_specs=[vmem] * 2 + [hbm] * N_SMALL,
        out_shape=[
            pltpu.VMEM((8, BLOCK, 4 * elems), jnp.bfloat16),
            pltpu.VMEM((4 * tiles, elems), jnp.int32),
            pltpu.VMEM((2, ROWS, BLOCK), jnp.bfloat16),
            pltpu.VMEM((slots, elems), jnp.bfloat16),
            pltpu.VMEM((BLOCK, BLOCK), jnp.bfloat16),
            pltpu.VMEM((tiles, 128, 3 * elems), jnp.bfloat16),
            pltpu.VMEM((width, elems), jnp.float32),
            pltpu.VMEM((1, elems), jnp.int32),
        ],
        out_specs=[vmem] * 8,
        scratch_shapes=[
            pltpu.VMEM(matrix.shape, jnp.bfloat16),
            pltpu.VMEM(mass.shape[1:], jnp.bfloat16),
            pltpu.VMEM((4, elems), jnp.int32),
            pltpu.VMEM((1, elems), jnp.int32),
            pltpu.VMEM((1, elems), jnp.float32),
            pltpu.VMEM((8, BLOCK, faces), jnp.bfloat16),
            pltpu.SemaphoreType.DMA((N_SMALL,)),
        ],
        compiler_params=params,
        cost_estimate=pl.CostEstimate(
            flops=8 * BLOCK * faces * 8 * elems, bytes_accessed=4 << 20, transcendentals=0
        ),
        name="prepare",
    )(
        sub,
        table,
        *in_hbm(
            elem_face,
            elem_owner.reshape(1, elems),
            matrix,
            mass[0],
            volume.reshape(1, elems),
            elem_slot.reshape(1, elems),
        ),
    )
    sent = pl.pallas_call(
        lambda *refs: element_kernel(columns, *refs),
        out_shape=jax.ShapeDtypeStruct((slots, 128), jnp.bfloat16),
        scratch_shapes=[
            pltpu.VMEM((8, columns, BLOCK // columns, 4 * elems), jnp.bfloat16),
            pltpu.VMEM((8 * width + 8, elems), jnp.float32),
        ],
        compiler_params=params,
        name="elements",
    )(*fixed, *halos)
    got = lax.all_to_all(sent, ("dom", "sub"), split_axis=0, concat_axis=0, tiled=True)
    summed = pl.pallas_call(
        lambda *refs: voxel_kernel(width, *refs),
        out_shape=jax.ShapeDtypeStruct((width, elems), jnp.float32),
        compiler_params=params,
        name="voxels",
    )(got)
    return summed.reshape(6, columns, elems)


def solution(mesh):
    return jax.shard_map(
        per_device,
        mesh=mesh,
        in_specs=(
            P(None, None, None, "rhs", ("groups", "dom", "sub")),
            P("groups", None, None, None),
            P(),
            P(None, ("dom", "sub")),
            P(None, ("dom", "sub")),
            P(None, ("dom", "sub")),
            P(("dom", "sub")),
            P(("dom", "sub"), None),
            P(("dom", "sub")),
        ),
        out_specs=P(None, "rhs", ("groups", "dom", "sub")),
        check_vma=False,
    )
```

```python
import itertools
import math

import jax
import jax.numpy as jnp
from jax import lax
from jax.experimental import pallas as pl
from jax.experimental.pallas import tpu as pltpu
from jax.sharding import PartitionSpec as P

BASIS = 35
HALF = 3 * BASIS
NODES = 30
BLOCK = 256
N_SMALL = 6
FULL = 32
ROWS = 216
PADDED = 112
VMEM_LIMIT = 24 * 1024 * 1024

NT = (((1,), (1,)), ((), ()))
NN = (((1,), (0,)), ((), ()))
TN = (((0,), (0,)), ((), ()))


def dot(a, b, dims=NN):
    return lax.dot_general(a, b, dims, preferred_element_type=jnp.float32)


def iota(shape, axis):
    return lax.broadcasted_iota(jnp.int32, shape, axis)


def one_hot(condition):
    return jnp.where(condition, 1.0, 0.0).astype(jnp.bfloat16)


def pair_index(index, k, size):
    if size & (size - 1) == 0:
        return index ^ k, index ^ k
    return lax.rem(index + k, size), lax.rem(index + size - k, size)


def swapped(messages):
    first = lax.axis_index("rhs") == 0
    even, slab = messages[1], messages[2]
    return [messages[0], jnp.where(first, slab, even), jnp.where(first, even, slab)] + messages[3:]


def pack_kernel(n_sub, rows, traces_hbm, dom_hbm, sub_hbm, table_ref, sub_ref, *refs):
    out_refs, (dom_ref, sems) = refs[: n_sub + 1], refs[n_sub + 1 :]
    faces = table_ref.shape[1]
    pairs = [(dom_hbm, dom_ref), (sub_hbm, sub_ref), (traces_hbm, table_ref)]
    copies = [pltpu.make_async_copy(*pair, sems.at[i]) for i, pair in enumerate(pairs)]
    for i in (2, 0, 1):
        copies[i].start()
    for copy in copies[:2]:
        copy.wait()
    parity = lax.rem(lax.axis_index("dom"), 2)
    within = lax.axis_index("sub")
    lists = [dom_ref[pl.ds(parity, 1), :], dom_ref[pl.ds(1 - parity, 1), :]]
    for k in range(1, n_sub):
        lists.append(sub_ref[pl.ds(pair_index(within, k, n_sub)[0], 1), :])
    lists = swapped(lists)
    face = iota((faces, rows), 0)
    picks = [jnp.where(face == row, 1.0, 0.0).T for row in lists]
    picks = jnp.concatenate(picks, axis=0).astype(jnp.bfloat16)
    copies[2].wait()
    packed = dot(picks, table_ref[...], NT).astype(jnp.bfloat16)
    for i, out_ref in enumerate(out_refs):
        out_ref[...] = packed[i * rows : (i + 1) * rows]


def reorder_matrix(columns):
    per_block = BLOCK // columns
    row = iota((BLOCK, BLOCK), 0)
    col = iota((BLOCK, BLOCK), 1)
    return one_hot(lax.rem(row, per_block) * columns + lax.div(row, per_block) == col)


def block_starts(columns):
    half = 2 * NODES * columns
    return [a * half - (a * half) % 128 + b * BLOCK for a in range(2) for b in range(4)]


def row_group(row):
    tail = row - 6 * FULL
    within = lax.rem(tail, 8)
    late = BASIS - FULL
    head = row < 6 * FULL
    group = jnp.where(head, lax.div(row, FULL), lax.div(within, late) * 3 + lax.div(tail, 8))
    basis = jnp.where(head, lax.rem(row, FULL), FULL + lax.rem(within, late))
    used = head | (within < 2 * late)
    return jnp.where(used, group, -1), basis


def prepare_kernel(n_sub, capacity, columns, sub_ref, table_ref, *refs):
    hbm_refs, refs = refs[:N_SMALL], refs[N_SMALL:]
    own_ref, places_ref, matrix_ref, sends_ref, reorder_ref, hot_ref, scale_ref, slot_ref = refs[:8]
    solver_ref, mass_ref, elem_ref, owner_ref, volume_ref, mine_ref, sems = refs[8:]
    vmem_refs = [elem_ref, owner_ref, solver_ref, mass_ref, volume_ref, slot_ref]
    copies = [
        pltpu.make_async_copy(hbm_refs[i], vmem_refs[i], sems.at[i]) for i in range(N_SMALL)
    ]
    for copy in copies:
        copy.start()
    faces = table_ref.shape[1]
    elems = elem_ref.shape[1]
    rows = sub_ref.shape[1]
    slots = sends_ref.shape[0]
    parity = lax.rem(lax.axis_index("dom"), 2)
    within = lax.axis_index("sub")

    reorder = reorder_matrix(columns)
    reorder_ref[...] = reorder
    for b, start in enumerate(block_starts(columns)):
        mine = dot(reorder, table_ref[start : start + BLOCK, :])
        mine_ref[b] = mine.astype(jnp.bfloat16)
    own_list = sub_ref[pl.ds(within, 1), :]
    square = iota((rows, rows), 0) == iota((rows, rows), 1)
    own_list = jnp.sum(jnp.where(square, own_list, 0), axis=1, keepdims=True)
    half = 2 * NODES * columns
    source = iota((4 * NODES, BLOCK), 0)
    place = iota((4 * NODES, BLOCK), 1)
    target = lax.div(source, NODES) * 64 + lax.rem(source, NODES)
    spots = []
    for a in range(2):
        first = target + ((a * half) % 128) // columns
        spots += [one_hot(first == place), one_hot(first + NODES == place)]
    spots = jnp.concatenate(spots, axis=1)
    group, basis = row_group(iota((ROWS, 1), 0))
    column = iota((1, 2 * PADDED), 1)
    field = lax.rem(column, PADDED)
    column_group = lax.div(column, PADDED) * 3 + lax.div(field, BASIS)
    column_basis = lax.rem(field, BASIS)
    same = (group == column_group) & (field < HALF)
    spread = one_hot(same & (basis == column_basis))
    sign = jnp.where(same, jnp.where(column < PADDED, 1.0, -1.0), 0.0)
    tall = one_hot(basis == iota((ROWS, BASIS), 1))
    wide = one_hot(iota((BASIS, 2 * PADDED), 0) == column_basis)
    earlier = one_hot(iota((elems, elems), 0) < iota((elems, elems), 1))
    for copy in copies:
        copy.wait()

    elem_face = elem_ref[...]
    offset = elem_face - (faces + (2 + within) * rows)
    own = []
    for f in range(4):
        found = jnp.where(iota((rows, elems), 0) == offset[f : f + 1, :], own_list, 0)
        found = jnp.sum(found, axis=0, keepdims=True)
        inside = (offset[f : f + 1, :] >= 0) & (offset[f : f + 1, :] < rows)
        index = jnp.where(inside, found, elem_face[f : f + 1, :])
        own.append(one_hot(iota((faces, elems), 0) == index))
    own = jnp.concatenate(own, axis=1)
    mine = mine_ref[...].reshape(8 * BLOCK, faces)
    own_ref[...] = dot(mine, own).astype(jnp.bfloat16).reshape(own_ref.shape)
    blocks = [parity, 1 - parity]
    for k in range(1, n_sub):
        blocks.append(2 + pair_index(within, k, n_sub)[1])
    blocks = swapped(blocks)
    per_tile = 128 // rows - 1
    for t in range(places_ref.shape[0] // 4):
        lane = jnp.full(elem_face.shape, 127, jnp.int32)
        for i, block in enumerate(blocks[t * per_tile : (t + 1) * per_tile]):
            offset = elem_face - (faces + block * rows)
            lane = jnp.where((offset >= 0) & (offset < rows), offset + i * rows, lane)
        places_ref[4 * t : 4 * t + 4, :] = lane
        hot = [one_hot(iota((128, elems), 0) == lane[f : f + 1, :]) for f in range(3)]
        hot_ref[t] = jnp.concatenate(hot, axis=1)

    solver = solver_ref[:PADDED].astype(jnp.float32)
    solver = jnp.concatenate([solver[:, 0, :], solver[:, 1, :]], axis=0).astype(jnp.bfloat16)
    placed = dot(solver, spots)
    masses = dot(dot(tall, mass_ref[...]).astype(jnp.bfloat16), wide) * sign
    spreads = [masses.astype(jnp.bfloat16), spread]
    for a in range(2):
        first, second = (placed[:, (2 * a + i) * BLOCK : (2 * a + i + 1) * BLOCK] for i in range(2))
        top = first[:PADDED] - second[PADDED:]
        bottom = first[PADDED:] + second[:PADDED]
        both = jnp.concatenate([top, bottom], axis=0).astype(jnp.bfloat16)
        matrix_ref[a] = dot(spreads[a], both).astype(jnp.bfloat16)

    owner = owner_ref[...]
    owners = iota((max(8, slots // capacity), elems), 0) == owner
    counts = dot(one_hot(owners), earlier)
    rank = jnp.sum(jnp.where(owners, counts, 0.0), axis=0, keepdims=True)
    target = owner * capacity + rank.astype(jnp.int32)
    sends_ref[...] = one_hot(iota((slots, elems), 0) == target)

    width = 6 * columns
    norm = 1.0 / math.sqrt(70.0)
    factor = jnp.where(iota((width, 1), 0) < 3 * columns, norm, 0.5 * norm)
    scale_ref[...] = factor * volume_ref[...]


def element_kernel(
    columns,
    own_ref,
    places_ref,
    matrix_ref,
    sends_ref,
    reorder_ref,
    hot_ref,
    scale_ref,
    slot_ref,
    *refs,
):
    halo_refs, (out_ref, gathered_ref, sums_ref) = refs[:-3], refs[-3:]
    elems = scale_ref.shape[1]
    per_block = BLOCK // columns
    tiles = places_ref.shape[0] // 4
    reorder = reorder_ref[...]
    rows, values = halo_refs[0].shape
    per_tile = 128 // rows - 1
    tables = []
    for t in range(tiles):
        parts = [ref[...] for ref in halo_refs[t * per_tile : (t + 1) * per_tile]]
        parts.append(jnp.zeros((128 - rows * len(parts), values), jnp.bfloat16))
        tables.append(jnp.concatenate(parts, axis=0))
    starts = block_starts(columns)
    found = None
    others = []
    for t in range(tiles):
        blocks = []
        for b in range(0, 8, 2):
            pair = [tables[t][:, start : start + BLOCK] for start in starts[b : b + 2]]
            pair = dot(reorder, jnp.concatenate(pair, axis=0), NT)
            blocks += [pair[:, :128], pair[:, 128:]]
        others.append(blocks)
        stacked = jnp.concatenate([x.astype(jnp.bfloat16) for x in blocks], axis=0)
        part = dot(stacked, hot_ref[t])
        found = part if found is None else found + part
    found = found.astype(jnp.bfloat16)
    lanes = [
        jnp.broadcast_to(places_ref[4 * t + 3 : 4 * t + 4, :], (BLOCK, elems))
        for t in range(tiles)
    ]
    for b in range(8):
        part = slice(0, 3 * elems)
        got = own_ref[b, :, part] + found[b * BLOCK : (b + 1) * BLOCK]
        gathered_ref[b, :, :, part] = got.reshape(columns, per_block, 3 * elems)
        part = slice(3 * elems, 4 * elems)
        got = own_ref[b, :, part]
        for t in range(tiles):
            last = jnp.take_along_axis(
                others[t][b], lanes[t], axis=1, mode="promise_in_bounds"
            )
            got = got + last.astype(jnp.bfloat16)
        gathered_ref[b, :, :, part] = got.reshape(columns, per_block, elems)

    def fields(a, index):
        parts = []
        for c in range(2):
            taken = [gathered_ref[a * 4 + b, 2 * index + c] for b in range(4)]
            parts.append(
                jnp.concatenate(
                    [taken[b][:, f * elems : (f + 1) * elems] for f in range(4) for b in range(4)],
                    axis=0,
                )
            )
        return dot(matrix_ref[a], jnp.concatenate(parts, axis=1))

    pairs = [(0, 0), (1, 1), (2, 2), (0, 1), (0, 2), (1, 2)]
    split = 6 * FULL
    shape = (2, 3, FULL // 8, 8, 2 * elems)
    tail = (3, 8, 2 * elems)
    for index in range(columns // 2):
        weighted = fields(0, index)
        adjoint = fields(1, index).astype(jnp.bfloat16).astype(jnp.float32)
        weighted, weighted_tail = weighted[:split].reshape(shape), weighted[split:].reshape(tail)
        adjoint, adjoint_tail = adjoint[:split].reshape(shape), adjoint[split:].reshape(tail)
        for m, (i, j) in enumerate(pairs):
            products = adjoint[:, i] * weighted[:, j]
            rest = adjoint_tail[i] * weighted_tail[j]
            if i != j:
                products = products + adjoint[:, j] * weighted[:, i]
                rest = rest + adjoint_tail[j] * weighted_tail[i]
            total = jnp.sum(products, axis=(0, 1)) + rest
            for c in range(2):
                start = (m * columns + 2 * index + c) * 8
                sums_ref[start : start + 8, :] = total[:, c * elems : (c + 1) * elems]

    width = 6 * columns
    total = sums_ref[pl.ds(0, width, stride=8), :]
    for k in range(1, 8):
        total = total + sums_ref[pl.ds(k, width, stride=8), :]
    terms = total * scale_ref[...]
    slot = jnp.broadcast_to(slot_ref[...].astype(jnp.float32), (128 - width, elems))
    payload = jnp.concatenate([terms, slot], axis=0).astype(jnp.bfloat16)
    out_ref[...] = dot(sends_ref[...], payload, NT).astype(jnp.bfloat16)


def voxel_kernel(width, got_ref, out_ref):
    got = got_ref[...]
    slot = got[:, width : width + 1].astype(jnp.float32)
    voxels = out_ref.shape[1]
    members = one_hot(slot == iota((got.shape[0], voxels), 1).astype(jnp.float32))
    out_ref[...] = dot(got, members, TN)[:width]


def per_device(
    traces, solver, mass, dom_lists, sub_lists, elem_face, volume, elem_owner, elem_slot
):
    n_dom, n_sub = lax.axis_size("dom"), lax.axis_size("sub")
    owners = n_dom * n_sub
    columns, faces = traces.shape[3:]
    rows = dom_lists.shape[1]
    elems = elem_face.shape[1]
    capacity = max(2, 3 * elems // owners)
    width = 6 * columns
    table = traces.reshape(-1, faces)
    values = table.shape[0]
    params = pltpu.CompilerParams(vmem_limit_bytes=VMEM_LIMIT)

    vmem = pl.BlockSpec(memory_space=pltpu.VMEM)
    hbm = pl.BlockSpec(memory_space=pltpu.HBM)

    def in_hbm(*arrays):
        return [pltpu.with_memory_space_constraint(x, pltpu.HBM) for x in arrays]

    table, sub, *packed = pl.pallas_call(
        lambda *refs: pack_kernel(n_sub, rows, *refs),
        in_specs=[hbm] * 3,
        out_shape=[pltpu.VMEM(x.shape, x.dtype) for x in (table, sub_lists)]
        + [pltpu.VMEM((rows, values), jnp.bfloat16)] * (n_sub + 1),
        out_specs=[vmem] * (n_sub + 3),
        scratch_shapes=[
            pltpu.VMEM(dom_lists.shape, jnp.int32),
            pltpu.SemaphoreType.DMA((3,)),
        ],
        compiler_params=params,
        name="pack",
    )(*in_hbm(table, dom_lists, sub_lists))

    n_rhs = lax.axis_size("rhs")

    def partner(message, d, s, c):
        if message < 2:
            other = d + 1 if (d + message) % 2 else d - 1
            if 0 <= other < n_dom:
                return other, s, c
            return d, s, n_rhs - 1 - c
        return d, int(pair_index(s, message - 1, n_sub)[0]), c

    halos = []
    for k, part in enumerate(packed):
        pairs = []
        for d, s, c in itertools.product(range(n_dom), range(n_sub), range(n_rhs)):
            message = 3 - k if c == 0 and k in (1, 2) else k
            to_d, to_s, to_c = partner(message, d, s, c)
            pairs.append(((d * n_sub + s) * n_rhs + c, (to_d * n_sub + to_s) * n_rhs + to_c))
        halos.append(lax.ppermute(part, ("dom", "sub", "rhs"), pairs))
    slots = owners * capacity
    tiles = -(-(n_sub + 1) // (128 // rows - 1))
    matrix = solver[0].transpose(1, 0, 2)
    fixed = pl.pallas_call(
        lambda *refs: prepare_kernel(n_sub, capacity, columns, *refs),
        in_specs=[vmem] * 2 + [hbm] * N_SMALL,
        out_shape=[
            pltpu.VMEM((8, BLOCK, 4 * elems), jnp.bfloat16),
            pltpu.VMEM((4 * tiles, elems), jnp.int32),
            pltpu.VMEM((2, ROWS, BLOCK), jnp.bfloat16),
            pltpu.VMEM((slots, elems), jnp.bfloat16),
            pltpu.VMEM((BLOCK, BLOCK), jnp.bfloat16),
            pltpu.VMEM((tiles, 128, 3 * elems), jnp.bfloat16),
            pltpu.VMEM((width, elems), jnp.float32),
            pltpu.VMEM((1, elems), jnp.int32),
        ],
        out_specs=[vmem] * 8,
        scratch_shapes=[
            pltpu.VMEM(matrix.shape, jnp.bfloat16),
            pltpu.VMEM(mass.shape[1:], jnp.bfloat16),
            pltpu.VMEM((4, elems), jnp.int32),
            pltpu.VMEM((1, elems), jnp.int32),
            pltpu.VMEM((1, elems), jnp.float32),
            pltpu.VMEM((8, BLOCK, faces), jnp.bfloat16),
            pltpu.SemaphoreType.DMA((N_SMALL,)),
        ],
        compiler_params=params,
        cost_estimate=pl.CostEstimate(
            flops=8 * BLOCK * faces * 8 * elems, bytes_accessed=4 << 20, transcendentals=0
        ),
        name="prepare",
    )(
        sub,
        table,
        *in_hbm(
            elem_face,
            elem_owner.reshape(1, elems),
            matrix,
            mass[0],
            volume.reshape(1, elems),
            elem_slot.reshape(1, elems),
        ),
    )
    sent = pl.pallas_call(
        lambda *refs: element_kernel(columns, *refs),
        out_shape=jax.ShapeDtypeStruct((slots, 128), jnp.bfloat16),
        scratch_shapes=[
            pltpu.VMEM((8, columns, BLOCK // columns, 4 * elems), jnp.bfloat16),
            pltpu.VMEM((8 * width + 8, elems), jnp.float32),
        ],
        compiler_params=params,
        name="elements",
    )(*fixed, *halos)
    got = lax.all_to_all(sent, ("dom", "sub"), split_axis=0, concat_axis=0, tiled=True)
    summed = pl.pallas_call(
        lambda *refs: voxel_kernel(width, *refs),
        out_shape=jax.ShapeDtypeStruct((width, elems), jnp.float32),
        compiler_params=params,
        name="voxels",
    )(got)
    return summed.reshape(6, columns, elems)


def solution(mesh):
    return jax.shard_map(
        per_device,
        mesh=mesh,
        in_specs=(
            P(None, None, None, "rhs", ("groups", "dom", "sub")),
            P("groups", None, None, None),
            P(),
            P(None, ("dom", "sub")),
            P(None, ("dom", "sub")),
            P(None, ("dom", "sub")),
            P(("dom", "sub")),
            P(("dom", "sub"), None),
            P(("dom", "sub")),
        ),
        out_specs=P(None, "rhs", ("groups", "dom", "sub")),
        check_vma=False,
    )
```
